32 devices in a mesh: section: 2 (over core), block: 16 (over z, y, x).
Axes of the slice: x: 2, y: 2, z: 4, core: 2. Of those that a mesh axis runs over, the one named last changes fastest.
Arguments:
- env: float32 [2, 256, 512, 512], P('section', 'block'), may hold values from -6 to 6
- site: float32 [2, 8192, 2, 512], P('section', 'block'), may hold values from -0.25 to 0.25
- sector_tiles: int32 [16], replicated, may hold values from 1 to 16, 128 in all
- mpo_mask: int32 [2, 16, 16], P('section'), may hold values 0 or 1
- mpo_coef: float32 [2, 2, 16, 16], P('section'), may hold values from -1.5 to 1.5
- psi: float32 [2, 8192, 512], P('section', 'block'), may hold values from -0.03125 to 0.03125
- center_coef: float32 [2, 16], P('section'), may hold values from -1.5 to 1.5
Outputs:
- new_env: float32 [2, 256, 512, 512], P('section', 'block')
- hpsi: float32 [2, 8192, 512], P('section', 'block')
The draws below stay inside these ranges and needn't reach their ends.
Inputs may be any that keep to these rules, and one draw needn't show every extreme that they name: Sector q holds 32 * sector_tiles[q] states; the entries sum to M // 32 and the largest equals 16.
All inputs are finite; a program needn't handle non-finite values. No bound on the sum of `mpo_mask` on one device may be relied on, other than what follows from the above.
Results may differ from the reference program's by a relative error of at most 0.0003.
Values sent between devices are 32-bit elements; how exact they have to be, the bound alone decides.
No kernel may reach another device: no remote copies, remote signals or barrier semaphores. Data moves between devices by JAX's collectives and lax.ppermute only.
A program may use at most 192 MiB of HBM per device.

```python
import math
import jax
import jax.numpy as jnp
import numpy as np
from jax import lax

M = 4096
NSEC = 16
TROW = 32
MOST = 16
W = 16
SMAX = 512


def touch_ends(values, stream_key, smallest, largest):
    longest = values.shape.index(max(values.shape))
    spots = []
    for shift in (0, 1):
        where = [jax.random.randint(jax.random.fold_in(stream_key, axis), (), 0, length) for axis, length in enumerate(values.shape)]
        where[longest] = (where[longest] + shift) % values.shape[longest]
        spots.append(tuple(where))
    return values.at[spots[0]].set(smallest).at[spots[1]].set(largest)


def level_of(key, extent, shards, least, high):
    gain, own = 1.0, jax.random.fold_in(key, 6)
    for position, blocks in shards:
        heights = jnp.exp(jax.random.uniform(jax.random.fold_in(own, position), (blocks,), jnp.float32, least / len(shards), high / len(shards)))
        gain = gain * jnp.repeat(heights, extent[position] // blocks).reshape([-1 if axis == position else 1 for axis in range(len(extent))])
    return gain


def profile(number_of, total, bound, lean):
    loads = [(1 << 20) // math.isqrt(standing ** lean) + 1 for standing in range(2, number_of + 1)]
    surplus, holding = total - bound - (number_of - 1), [1] * (number_of - 1)
    while surplus > 0:
        free = [i for i in range(number_of - 1) if holding[i] < bound]
        pool, budget = sum([loads[i] for i in free]), surplus
        for i in free:
            addition = min(bound - holding[i], max(1, budget * loads[i] // pool), surplus)
            holding[i] = holding[i] + addition
            surplus = surplus - addition
    return np.array([bound] + holding)


def uneven_parts(own_key, amount, total, limit, skew):
    if amount == 2:
        one = jax.random.randint(own_key, (), max(1, total - limit), min(limit, total - 1) + 1)
        return jnp.stack([one, total - one])
    lengths = jnp.asarray(profile(amount, total, limit, skew), jnp.int32)
    twos = (amount - 1) // 2
    giver, receiver = lengths[1:1 + 2 * twos:2], lengths[2:2 + 2 * twos:2]
    room = jnp.minimum(giver - 1, limit - receiver)
    shifted = jax.random.randint(jax.random.fold_in(own_key, 1), (twos,), 0, 1 << 20) % (room + 1)
    lengths = lengths.at[1:1 + 2 * twos:2].set(giver - shifted).at[2:2 + 2 * twos:2].set(receiver + shifted)
    return lengths[jax.random.permutation(jax.random.fold_in(own_key, 2), amount)]


def normal_values(key, dims, deviation, limit, cuts=(), kind=jnp.bfloat16):
    loudness = level_of(key, dims, cuts, -0.22, 0.18) if cuts else 1.0
    array = jax.random.normal(key, dims, jnp.float32) * deviation * loudness
    return jnp.minimum(jnp.maximum(array, -limit), limit).astype(kind)


def setup_inputs(seed: int = 0) -> dict:
    keys = jax.random.split(jax.random.key(seed), 8)
    env = normal_values(keys[0], (2, NSEC * W, SMAX, SMAX), 1.0, 6.0, ((0, 2), (1, 16)), jnp.float32)
    site = normal_values(keys[1], (2, NSEC * SMAX, 2, SMAX), SMAX ** -0.5, 0.25, ((0, 2), (1, 16)), jnp.float32)
    sector_tiles = uneven_parts(keys[2], NSEC, M // TROW, MOST, 2).astype(jnp.int32)
    mpo_mask = touch_ends((jax.random.randint(keys[3], (2, W, W), 0, 2) < 1).astype(jnp.int32), jax.random.fold_in(keys[3], 1), 0, 1)
    mpo_coef = normal_values(keys[4], (2, 2, W, W), W ** -0.5, 1.5, ((0, 2),), jnp.float32)
    psi = normal_values(keys[5], (2, NSEC * SMAX, SMAX), (SMAX * SMAX // 8) ** -0.5, 0.03125, ((0, 2), (1, 16)), jnp.float32)
    center_coef = normal_values(keys[6], (2, W), W ** -0.5, 1.5, ((0, 2),), jnp.float32)
    return {"env": env, "site": site, "sector_tiles": sector_tiles, "mpo_mask": mpo_mask, "mpo_coef": mpo_coef, "psi": psi, "center_coef": center_coef}


HIGH = lax.Precision.HIGHEST


def reference(env, site, sector_tiles, mpo_mask, mpo_coef, psi, center_coef):
    sizes = jnp.concatenate([sector_tiles * TROW, jnp.zeros((1,), jnp.int32)])
    span = jnp.arange(SMAX, dtype=jnp.int32)
    fresh_envs = []
    for section in range(2):
        env_here = env[section].reshape(NSEC, W, SMAX, SMAX)
        site_here = site[section].reshape(NSEC, SMAX, 2, SMAX)
        mixing = mpo_coef[section] * mpo_mask[section].astype(jnp.float32)

        def absorb(sector):
            blocks = env_here[sector]
            tensor = site_here[sector]
            row_keep = (span < sizes[sector]).astype(jnp.float32)
            results = []
            for spin in range(2):
                col_keep = (span < sizes[sector + spin]).astype(jnp.float32)
                masked = tensor[:, spin, :] * row_keep[:, None] * col_keep[None, :]
                inner = jnp.einsum("wij,jk->wik", blocks, masked, precision=HIGH)
                outer = jnp.einsum("ji,wjk->wik", masked, inner, precision=HIGH)
                results.append(jnp.einsum("wv,wij->vij", mixing[spin], outer, precision=HIGH))
            return results[0], results[1]

        stay_terms, rise_terms = lax.map(absorb, jnp.arange(NSEC, dtype=jnp.int32))
        carried = jnp.concatenate([jnp.zeros((1, W, SMAX, SMAX), jnp.float32), rise_terms[:-1]], axis=0)
        fresh_envs.append(stay_terms + carried)
    left_env, right_env = fresh_envs
    outputs = []
    for pair in range(2):
        wave = psi[pair].reshape(NSEC, SMAX, SMAX)

        def apply_block(sector):
            first = jnp.einsum("wij,jk->wik", left_env[sector], wave[sector], precision=HIGH)
            second = jnp.einsum("wij,wjk->wik", first, right_env[sector], precision=HIGH)
            return jnp.einsum("w,wik->ik", center_coef[pair], second, precision=HIGH)

        outputs.append(lax.map(apply_block, jnp.arange(NSEC, dtype=jnp.int32)).reshape(NSEC * SMAX, SMAX))
    new_env = jnp.stack([left_env.reshape(NSEC * W, SMAX, SMAX), right_env.reshape(NSEC * W, SMAX, SMAX)])
    return new_env, jnp.stack(outputs)
```

```python
import functools

import jax
import jax.numpy as jnp
from jax import lax
from jax.experimental import pallas as pl
from jax.experimental.pallas import tpu as pltpu
from jax.sharding import PartitionSpec as P

TROW = 32
LANE = 128
CHUNK = 1024
STEPS = 128
DETOUR_END = 24
QUARTERS = 4
BYTES = 52 * 1024 * 1024

F32 = jnp.float32
BF16 = jnp.bfloat16
HIGH = lax.Precision.HIGHEST
SMEM_SPEC = pl.BlockSpec(memory_space=pltpu.SMEM)
ANY_SPEC = pl.BlockSpec(memory_space=pl.ANY)


def params():
    return pltpu.CompilerParams(vmem_limit_bytes=BYTES)


def halves(value):
    top = value.astype(BF16)
    rest = (value - top.astype(F32)).astype(BF16)
    return top, rest


def left3(value):
    top, rest = halves(value)
    return jnp.concatenate([top, top, rest], axis=1)


def right3(value):
    top, rest = halves(value)
    return jnp.concatenate([top, rest, top], axis=0)


def dot3(a, b):
    return jnp.dot(a, b, preferred_element_type=F32)


def hop(place, direction, depth):
    x, y, z = place & 1, place >> 1 & 1, place >> 2
    if direction == 0:
        x ^= 1
    elif direction == 1:
        y ^= 1
    else:
        z += 1 if direction == 2 else -1
    return x + 2 * y + 4 * z if 0 <= z < depth else None


ROUTES = {
    0: ((0,), (1, 0, 1), (2, 0, 3), (3, 0, 2)),
    1: ((0, 1), (1, 0), (2, 0, 1, 3), (3, 1, 0, 2), (2, 1, 0, 3), (3, 0, 1, 2)),
    2: ((0,), (1, 0, 1), (2, 0, 3), (3, 0, 2)),
    3: ((0, 1, 2), (1, 2, 0), (2, 0, 1), (2, 1, 0), (0, 2, 1), (1, 0, 2)),
}


def routes_of(pair, depth):
    found = []
    for turns in ROUTES[pair % 4]:
        place, hops = pair, []
        for turn in turns:
            hops.append((place, turn))
            place = hop(place, turn, depth)
            if place is None:
                break
        if place == pair + 1:
            found.append(hops)
    return found


def neighbours(direction, count):
    depth = count // 4
    pairs = []
    for place in range(count):
        target = hop(place, direction, depth)
        if target is not None:
            pairs.append((place, target))
    return pairs


def schedule_kernel(count, width, slots, tiles, me_ref, send, recv, info, busy, state):
    depth = count // 4
    me = me_ref[0]
    dump = STEPS * 4

    def clear(i, _):
        send[i] = -1
        recv[i] = -1
        return 0

    lax.fori_loop(0, dump + 8, clear, 0)
    for i in range(count * 4):
        busy[i] = 0
    for i in range(3):
        state[i] = 0
    need = []
    for pair in range(count - 1):
        small = jnp.minimum(tiles[pair], tiles[pair + 1])
        strips = (small + 3) >> 2
        need.append((width * strips * small * TROW + (CHUNK - 1)) // CHUNK)
    top = need[0]
    for value in need[1:]:
        top = jnp.maximum(top, value)

    def level(i, _):
        k = top - i

        @pl.when(state[1] >= 1 << (DETOUR_END + 1))
        def _():
            used = state[1]
            length = jnp.int32(0)
            for shift in (16, 8, 4, 2, 1):
                large = used >= 1 << shift
                length += jnp.where(large, shift, 0)
                used = jnp.where(large, used >> shift, used)
            state[0] = state[0] + length + 1
            state[1] = 0
            state[2] = state[2] + 1
            for j in range(count * 4):
                busy[j] = 0

        for pair in range(count - 1):

            @pl.when(need[pair] >= k)
            def _(pair=pair):
                ways = routes_of(pair, depth)
                best = jnp.int32(0x7FFFFFFF)
                choice = jnp.int32(0)
                start = jnp.int32(0)
                detour_ok = state[2] < 2
                for number, hops in enumerate(ways):
                    taken = jnp.int32(0)
                    for late, (place, turn) in enumerate(hops):
                        taken = taken | (busy[place * 4 + turn] >> late)
                    last = 31 if number == 0 else DETOUR_END + 1
                    free = ~taken & ((1 << (last - len(hops) + 1)) - 1)
                    low = free & -free
                    key = low << (len(hops) - 1)
                    better = (low > 0) & (key < best)
                    if number > 0:
                        better = better & detour_ok
                    best = jnp.where(better, key, best)
                    choice = jnp.where(better, number, choice)
                    start = jnp.where(better, low, start)
                state[1] = state[1] | best
                when = jnp.int32(0)
                bit = start
                for shift in (16, 8, 4, 2, 1):
                    large = bit >= 1 << shift
                    when += jnp.where(large, shift, 0)
                    bit = jnp.where(large, bit >> shift, bit)
                step = state[0] + when
                number_of = need[pair] - k
                for number, hops in enumerate(ways):

                    @pl.when(choice == number)
                    def _(hops=hops):
                        for late, (place, turn) in enumerate(hops):
                            link = place * 4 + turn
                            busy[link] = busy[link] | (start << late)
                            at = (step + late) * 4 + turn
                            if late == 0:
                                from_slot = number_of
                            else:
                                before = hops[late - 1][1]
                                from_slot = 2 * slots + before
                            if late == len(hops) - 1:
                                to_slot = slots + number_of
                            else:
                                to_slot = 2 * slots + turn
                            send[jnp.where(me == place, at, dump)] = from_slot
                            there = hop(place, turn, depth)
                            recv[jnp.where(me == there, at, dump)] = to_slot

        return 0

    lax.fori_loop(0, top, level, 0)
    used = state[1]
    length = jnp.int32(0)
    for shift in (16, 8, 4, 2, 1):
        large = used >= 1 << shift
        length += jnp.where(large, shift, 0)
        used = jnp.where(large, used >> shift, used)
    info[0] = state[0] + length + jnp.where(state[1] > 0, 1, 0)


def schedule(sector_tiles, me, count, width, slots):
    size = STEPS * 4 + 8
    return pl.pallas_call(
        functools.partial(schedule_kernel, count, width, slots),
        out_shape=(
            jax.ShapeDtypeStruct((size,), jnp.int32),
            jax.ShapeDtypeStruct((size,), jnp.int32),
            jax.ShapeDtypeStruct((8,), jnp.int32),
        ),
        in_specs=[SMEM_SPEC, SMEM_SPEC],
        out_specs=(SMEM_SPEC, SMEM_SPEC, SMEM_SPEC),
        scratch_shapes=[pltpu.SMEM((count * 4,), jnp.int32), pltpu.SMEM((8,), jnp.int32)],
        name="route_schedule",
    )(sector_tiles, me)


def shuffle_kernel(slots, step_ref, send, recv, *refs):
    arrived, store, leaving = refs[:4], refs[-8], refs[-7:-3]
    held, sems_in, sems_out = refs[-3:]
    step = step_ref[0]

    def part(slot):
        return store.at[pl.ds(jnp.clip(slot, 0, 2 * slots - 1) * CHUNK, CHUNK)]

    loads, saves = [], []
    for turn in range(4):
        slot = recv[jnp.maximum(step - 1, 0) * 4 + turn]
        present = (step > 0) & (slot >= 0)
        loads.append((present, pltpu.make_async_copy(arrived[turn], held.at[turn], sems_in.at[turn])))
        final = present & (slot < 2 * slots)
        saves.append((final, pltpu.make_async_copy(held.at[turn], part(slot), sems_out.at[turn])))
    for turn in range(4):
        slot = send[step * 4 + turn]
        own = (slot >= 0) & (slot < 2 * slots)
        loads.append((own, pltpu.make_async_copy(part(slot), held.at[4 + turn], sems_in.at[4 + turn])))
        source = jnp.where(slot >= 2 * slots, slot & 3, 4 + turn)
        saves.append((slot >= 0, pltpu.make_async_copy(held.at[source], leaving[turn], sems_out.at[4 + turn])))
    begin(loads)
    finish(loads)
    begin(saves)
    finish(saves)


def shuffle(step, send, recv, arrived, store, after=()):
    chunk = jax.ShapeDtypeStruct((CHUNK, LANE), F32)
    slots = store.shape[0] // (2 * CHUNK)
    out = pl.pallas_call(
        functools.partial(shuffle_kernel, slots),
        out_shape=(jax.ShapeDtypeStruct(store.shape, F32),) + (chunk,) * 4,
        in_specs=[SMEM_SPEC] * 3 + [ANY_SPEC] * (5 + len(after)),
        out_specs=(ANY_SPEC,) * 5,
        scratch_shapes=[
            pltpu.VMEM((8, CHUNK, LANE), F32),
            pltpu.SemaphoreType.DMA((8,)),
            pltpu.SemaphoreType.DMA((8,)),
        ],
        input_output_aliases={7: 0},
        cost_estimate=pl.CostEstimate(flops=0, bytes_accessed=8 * 1024 * 1024, transcendentals=0),
        name="shuffle_chunks",
    )(jnp.reshape(step, (1,)).astype(jnp.int32), send, recv, *arrived, store, *after)
    return out[0], out[1:]


def prepare_kernel(x_ref, a3_ref, at3_ref):
    value = x_ref[0]
    a3_ref[0] = right3(value)
    at3_ref[0] = left3(value.T)


def prepare(tensors):
    number, rows, cols = tensors.shape
    return pl.pallas_call(
        prepare_kernel,
        grid=(number,),
        out_shape=(
            jax.ShapeDtypeStruct((number, 3 * rows, cols), BF16),
            jax.ShapeDtypeStruct((number, cols, 3 * rows), BF16),
        ),
        in_specs=[pl.BlockSpec((1, rows, cols), lambda s: (s, 0, 0))],
        out_specs=(
            pl.BlockSpec((1, 3 * rows, cols), lambda s: (s, 0, 0)),
            pl.BlockSpec((1, cols, 3 * rows), lambda s: (s, 0, 0)),
        ),
        compiler_params=params(),
        name="split_site",
    )(tensors)


def mix_kernel(k_ref, e_ref, f_ref, k3):
    @pl.when(pl.program_id(0) == 0)
    def _():
        k3[...] = left3(k_ref[...])

    width, rows, cols = e_ref.shape
    few = k_ref.shape[0] // width
    for start in range(0, rows, few):
        e3 = right3(e_ref[:, start : start + few, :].reshape(width * few, cols))
        f_ref[:, start : start + few, :] = dot3(k3[...], e3).reshape(width, few, cols)


def mix_all(spread, env):
    width, extent, _ = env.shape
    rows = 4 * spread.shape[0] // width
    block = pl.BlockSpec((width, rows, extent), lambda c: (0, c, 0))
    return pl.pallas_call(
        mix_kernel,
        grid=(extent // rows,),
        out_shape=jax.ShapeDtypeStruct(env.shape, F32),
        in_specs=[pl.BlockSpec(spread.shape, lambda c: (0, 0)), block],
        out_specs=block,
        scratch_shapes=[pltpu.VMEM((spread.shape[0], 3 * spread.shape[1]), BF16)],
        compiler_params=params(),
        cost_estimate=pl.CostEstimate(flops=13 * 10**9, bytes_accessed=48 * 2**20, transcendentals=0),
        name="mix_environment",
    )(spread, env)


def strip_copies(plane, size, store, base, number, jcount, sem, inward):
    found = []
    size = pl.multiple_of(size, TROW)
    for j in range(plane.shape[1] // LANE):
        start = base + (number * jcount + j) * size
        flat = store.at[pl.ds(pl.multiple_of(start, TROW), size)]
        corner = plane.at[pl.ds(0, size), pl.ds(j * LANE, LANE)]
        pair = (flat, corner) if inward else (corner, flat)
        found.append((j < jcount, pltpu.make_async_copy(*pair, sem)))
    return found


def begin(copies):
    for wanted, copy in copies:

        @pl.when(wanted)
        def _(copy=copy):
            copy.start()


def finish(copies):
    for wanted, copy in copies:

        @pl.when(wanted)
        def _(copy=copy):
            copy.wait()


def outgoing_kernel(info, f_ref, a3_ref, at3_ref, store, plane, sem):
    number = pl.program_id(0)
    mode, size, jcount = info[0], info[1], info[2]

    @pl.when(mode == 1)
    def _():
        inner = dot3(left3(f_ref[0]), a3_ref[0])
        plane[...] = dot3(at3_ref[0], right3(inner))

    @pl.when(mode == 2)
    def _():
        plane[...] = f_ref[0]

    @pl.when(mode > 0)
    def _():
        copies = strip_copies(plane, size, store, 0, number, jcount, sem, False)
        begin(copies)
        finish(copies)


def outgoing(info, mixed, a3, at3, slots):
    width, extent, _ = mixed.shape
    return pl.pallas_call(
        outgoing_kernel,
        grid=(width,),
        out_shape=jax.ShapeDtypeStruct((2 * slots * CHUNK, LANE), F32),
        in_specs=[
            SMEM_SPEC,
            pl.BlockSpec((1, extent, extent), lambda w: (w, 0, 0)),
            pl.BlockSpec((1,) + a3.shape[1:], lambda w: (1, 0, 0)),
            pl.BlockSpec((1,) + at3.shape[1:], lambda w: (1, 0, 0)),
        ],
        out_specs=ANY_SPEC,
        scratch_shapes=[pltpu.VMEM((extent, extent), F32), pltpu.SemaphoreType.DMA],
        compiler_params=params(),
        name="outgoing_terms",
    )(info, mixed, a3, at3)


def staying_kernel(f_ref, a3_ref, at3_ref, out_ref):
    inner = dot3(left3(f_ref[0]), a3_ref[0])
    out_ref[0] = dot3(at3_ref[0], right3(inner))


def staying(mixed, a3, at3, part):
    width, extent, _ = mixed.shape
    planes = width // QUARTERS
    return pl.pallas_call(
        staying_kernel,
        grid=(planes,),
        out_shape=jax.ShapeDtypeStruct((planes, extent, extent), F32),
        in_specs=[
            pl.BlockSpec((1, extent, extent), lambda w: (part * planes + w, 0, 0)),
            pl.BlockSpec((1,) + a3.shape[1:], lambda w: (0, 0, 0)),
            pl.BlockSpec((1,) + at3.shape[1:], lambda w: (0, 0, 0)),
        ],
        out_specs=pl.BlockSpec((1, extent, extent), lambda w: (w, 0, 0)),
        compiler_params=params(),
        cost_estimate=pl.CostEstimate(
            flops=planes * 12 * extent**3, bytes_accessed=planes * 8 * extent**2, transcendentals=0
        ),
        name="staying_terms",
    )(mixed, a3, at3)


def arriving_kernel(part, first, info, stay_ref, a3_ref, at3_ref, store, *refs):
    out_ref, whole_ref, planes, sems = refs[-4:]
    w = pl.program_id(0)
    count = pl.num_programs(0)
    mode, size, jcount, base = info[0], info[1], info[2], info[3]
    slot = lax.rem(w, 2)

    def copies(index, place):
        number = part * count + index
        return strip_copies(planes.at[place], size, store, base, number, jcount, sems.at[place], True)

    @pl.when(w == 0)
    def _():
        planes[...] = jnp.zeros_like(planes)

        @pl.when(mode > 0)
        def _():
            begin(copies(w, slot))

    @pl.when((mode > 0) & (w + 1 < count))
    def _():
        begin(copies(w + 1, 1 - slot))

    @pl.when(mode > 0)
    def _():
        finish(copies(w, slot))

    @pl.when(mode == 0)
    def _():
        out_ref[0] = stay_ref[0]

    @pl.when(mode == 1)
    def _():
        out_ref[0] = stay_ref[0] + planes[slot]

    @pl.when(mode == 2)
    def _():
        inner = dot3(left3(planes[slot]), a3_ref[0])
        out_ref[0] = stay_ref[0] + dot3(at3_ref[0], right3(inner))

    whole_ref[0] = out_ref[0]


def arriving(info, stay, a3, at3, store, whole, part, width):
    planes, extent, _ = stay.shape
    first = whole is None
    return pl.pallas_call(
        functools.partial(arriving_kernel, part, first),
        grid=(planes,),
        out_shape=(
            jax.ShapeDtypeStruct(stay.shape, F32),
            jax.ShapeDtypeStruct((width, extent, extent), F32),
        ),
        in_specs=[
            SMEM_SPEC,
            pl.BlockSpec((1, extent, extent), lambda w: (w, 0, 0)),
            pl.BlockSpec((1,) + a3.shape[1:], lambda w: (0, 0, 0)),
            pl.BlockSpec((1,) + at3.shape[1:], lambda w: (0, 0, 0)),
            ANY_SPEC,
        ]
        + ([] if first else [ANY_SPEC]),
        out_specs=(
            pl.BlockSpec((1, extent, extent), lambda w: (w, 0, 0)),
            pl.BlockSpec((1, extent, extent), lambda w: (part * planes + w, 0, 0)),
        ),
        scratch_shapes=[pltpu.VMEM((2, extent, extent), F32), pltpu.SemaphoreType.DMA((2,))],
        input_output_aliases={} if first else {5: 1},
        compiler_params=params(),
        cost_estimate=pl.CostEstimate(
            flops=planes * 6 * extent**3, bytes_accessed=planes * 16 * extent**2, transcendentals=0
        ),
        name="arriving_terms",
    )(info, stay, a3, at3, store, *([] if first else [whole]))


def center_kernel(part, first, info, coef, psi_ref, own_ref, other_ref, *refs):
    out_ref, p3 = refs[-2:]
    w = pl.program_id(0)

    @pl.when(w == 0)
    def _():
        p3[...] = right3(psi_ref[...])
        if first:
            out_ref[...] = jnp.zeros_like(out_ref)
        else:
            out_ref[...] = refs[0][...]

    is_left = info[4] == 0
    own, other = own_ref[0], other_ref[0]
    left = jnp.where(is_left, own, other)
    right = jnp.where(is_left, other, own)
    weight = coef[part * pl.num_programs(0) + w]
    inner = dot3(left3(left), p3[...]) * weight
    out_ref[...] += dot3(left3(inner), right3(right))


def center(info, coef, psi, own, other, before, part):
    planes, extent, _ = own.shape
    first = before is None
    whole = pl.BlockSpec((extent, extent), lambda w: (0, 0))
    return pl.pallas_call(
        functools.partial(center_kernel, part, first),
        grid=(planes,),
        out_shape=jax.ShapeDtypeStruct((extent, extent), F32),
        in_specs=[
            SMEM_SPEC,
            SMEM_SPEC,
            whole,
            pl.BlockSpec((1, extent, extent), lambda w: (w, 0, 0)),
            pl.BlockSpec((1, extent, extent), lambda w: (w, 0, 0)),
        ]
        + ([] if first else [whole]),
        out_specs=whole,
        scratch_shapes=[pltpu.VMEM((3 * extent, extent), BF16)],
        compiler_params=params(),
        cost_estimate=pl.CostEstimate(
            flops=planes * 12 * extent**3, bytes_accessed=planes * 8 * extent**2, transcendentals=0
        ),
        name="center_terms",
    )(info, coef, psi, own, other, *([] if first else [before]))


def routed(env, site, sector_tiles, mpo_mask, mpo_coef, psi, center_coef):
    count = sector_tiles.shape[0]
    sector = lax.axis_index("block")
    section = lax.axis_index("section")
    blocks = env[0]
    width, extent, _ = blocks.shape
    slots = width * extent * extent // (CHUNK * LANE)
    labels = jnp.arange(count, dtype=jnp.int32)

    def size_of(which):
        return jnp.sum(jnp.where(labels == which, sector_tiles, 0)) * TROW

    size_here, size_next, size_last = size_of(sector), size_of(sector + 1), size_of(sector - 1)
    me = jnp.reshape(sector, (1,)).astype(jnp.int32)
    send, recv, steps = schedule(sector_tiles, me, count, width, slots)

    def pair_info(here, there, present, base):
        small = jnp.minimum(here, there)
        mode = jnp.where(present, jnp.where(here < there, 2, 1), 0)
        strips = (small + LANE - 1) // LANE
        return jnp.stack([mode, small, strips, base, section]).astype(jnp.int32)

    info_out = pair_info(size_here, size_next, sector + 1 < count, 0)
    info_in = pair_info(size_last, size_here, sector > 0, slots * CHUNK)

    span = jnp.arange(extent, dtype=jnp.int32)
    row_keep = span < size_here
    tensors = jnp.stack(
        [
            jnp.where(row_keep[:, None] & (span < size)[None, :], site[0][:, spin, :], 0.0)
            for spin, size in enumerate((size_here, size_next))
        ]
    )
    earlier = lax.ppermute(tensors[1], "block", [(q, q + 1) for q in range(count - 1)])
    a3, at3 = prepare(tensors)
    mixing = mpo_coef[0] * mpo_mask[0].astype(F32)
    rows = 256 // width
    eye = jnp.eye(rows, dtype=F32)
    spread = (jnp.swapaxes(mixing, 1, 2)[:, :, None, :, None] * eye[None, None, :, None, :]).reshape(
        2, width * rows, width * rows
    )
    rising = mix_all(spread[1], blocks)
    store = outgoing(info_out, rising, a3, at3, slots)
    b3, bt3 = prepare(earlier[None])

    links = [neighbours(turn, count) for turn in range(4)]

    def exchange(leaving):
        return [lax.ppermute(leaving[turn], "block", links[turn]) for turn in range(4)]

    zero = jnp.zeros((CHUNK, LANE), F32)
    store, leaving = shuffle(jnp.int32(0), send, recv, [zero] * 4, store)
    stays = []
    for step in range(QUARTERS + 1):
        arrived = exchange(leaving)
        if step == 0:
            mixed = mix_all(spread[0], blocks)
            beside = mixed
        else:
            beside = staying(mixed, a3, at3, step - 1)
            stays.append(beside)
        store, leaving = shuffle(jnp.int32(step + 1), send, recv, arrived, store, (beside,))

    def more(carry):
        return carry[0] < steps[0]

    def onward(carry):
        step, store, leaving = carry
        arrived = exchange(leaving)
        store, leaving = shuffle(step + 1, send, recv, arrived, store)
        return step + 1, store, leaving

    _, store, _ = lax.while_loop(more, onward, (jnp.int32(QUARTERS + 1), store, leaving))

    whole, total = None, None
    for part in range(QUARTERS):
        fresh, whole = arriving(info_in, stays[part], b3, bt3, store, whole, part, width)
        partner = lax.ppermute(fresh, "section", [(0, 1), (1, 0)])
        total = center(info_in, center_coef[0], psi[0], fresh, partner, total, part)
    return whole[None], total[None]


def swapped(block, axis, distance):
    count = lax.axis_size(axis)
    route = []
    for low in range(count):
        high = low | 1 << distance
        if high != low and high < count:
            route += [(low, high), (high, low)]
    return lax.ppermute(block, axis, route)


def from_behind(value, axis, steps):
    count = lax.axis_size(axis)
    first, last = (max(0, -steps), min(count, count - steps))
    return lax.ppermute(value, axis, [(source, source + steps) for source in range(first, last)])


def ordered(is_upper, mine, theirs, axis_dim):
    return jnp.where(
        is_upper,
        jnp.concatenate([theirs, mine], axis=axis_dim),
        jnp.concatenate([mine, theirs], axis=axis_dim),
    )


def sandwich(masked, blocks):
    inner = jnp.einsum("wij,jk->wik", blocks, masked, precision=HIGH)
    return jnp.einsum("ji,wjk->wik", masked, inner, precision=HIGH)


def local(env, site, sector_tiles, mpo_mask, mpo_coef, psi, center_coef):
    nsector = sector_tiles.shape[0]
    group = lax.axis_size("block") // nsector
    levels = group.bit_length() - 1
    device = lax.axis_index("block")
    sector = device // group
    member = device % group
    section = lax.axis_index("section")
    width_local = env.shape[1]
    extent = env.shape[2]
    labels = jnp.arange(nsector, dtype=jnp.int32)
    counts = sector_tiles * TROW
    size_here = jnp.sum(jnp.where(labels == sector, counts, 0))
    size_next = jnp.sum(jnp.where(labels == sector + 1, counts, 0))
    span = jnp.arange(extent, dtype=jnp.int32)
    rows_now = site[0]
    wave_now = psi[0]
    for segment in range(levels):
        other_rows, other_wave = swapped((rows_now, wave_now), "block", segment)
        is_upper = member // 2**segment % 2 == 1
        rows_now = ordered(is_upper, rows_now, other_rows, 0)
        wave_now = ordered(is_upper, wave_now, other_wave, 0)
    row_keep = (span < size_here).astype(jnp.float32)
    masks = []
    for spin in range(2):
        limit = size_here if spin == 0 else size_next
        col_keep = (span < limit).astype(jnp.float32)
        masks.append(rows_now[:, spin, :] * row_keep[:, None] * col_keep[None, :])
    blocks = env[0]
    mixing = mpo_coef[0] * mpo_mask[0].astype(jnp.float32)
    collected = jnp.stack([sandwich(masks[0], blocks), sandwich(masks[1], blocks)])
    for segment in range(levels):
        other_terms = swapped(collected, "block", segment)
        is_upper = member // 2**segment % 2 == 1
        collected = ordered(is_upper, collected, other_terms, 1)
    own_cols = lax.dynamic_slice_in_dim(mixing, member * width_local, width_local, 2)
    reduced = jnp.einsum("xwv,xwij->xvij", own_cols, collected, precision=HIGH)
    arrived = from_behind(reduced[1], "block", group)
    fresh = reduced[0] + arrived
    partner = swapped(fresh, "section", 0)
    left_env = jnp.where(section == 0, fresh, partner)
    right_env = jnp.where(section == 0, partner, fresh)
    first = jnp.einsum("wij,jk->wik", left_env, wave_now, precision=HIGH)
    second = jnp.einsum("wij,wjk->wik", first, right_env, precision=HIGH)
    weights = lax.dynamic_slice_in_dim(center_coef[0], member * width_local, width_local, 0)
    summed = jnp.einsum("w,wik->ik", weights, second, precision=HIGH)
    for segment in reversed(range(levels)):
        half_rows = summed.shape[0] // 2
        lower_part = summed[:half_rows]
        upper_part = summed[half_rows:]
        is_upper = member // 2**segment % 2 == 1
        keeping = jnp.where(is_upper, upper_part, lower_part)
        sending = jnp.where(is_upper, lower_part, upper_part)
        summed = keeping + swapped(sending, "block", segment)
    return (fresh[None], summed[None])


def solution(mesh):
    placed = (
        P("section", "block", None, None),
        P("section", "block", None, None),
        P(),
        P("section", None, None),
        P("section", None, None, None),
        P("section", "block", None),
        P("section", None),
    )
    one_each = mesh.shape["block"] == 16
    return jax.shard_map(
        routed if one_each else local,
        mesh=mesh,
        in_specs=placed,
        out_specs=(P("section", "block", None, None), P("section", "block", None)),
        check_vma=False,
    )
```

```python
import functools

import jax
import jax.numpy as jnp
from jax import lax
from jax.experimental import pallas as pl
from jax.experimental.pallas import tpu as pltpu
from jax.sharding import PartitionSpec as P

TROW = 32
LANE = 128
CHUNK = 2048
STEPS = 128
DETOUR_END = 24
QUARTERS = 4
BYTES = 52 * 1024 * 1024

F32 = jnp.float32
BF16 = jnp.bfloat16
HIGH = lax.Precision.HIGHEST
SMEM_SPEC = pl.BlockSpec(memory_space=pltpu.SMEM)
ANY_SPEC = pl.BlockSpec(memory_space=pl.ANY)


def params():
    return pltpu.CompilerParams(vmem_limit_bytes=BYTES)


def halves(value):
    top = value.astype(BF16)
    rest = (value - top.astype(F32)).astype(BF16)
    return top, rest


def left3(value):
    top, rest = halves(value)
    return jnp.concatenate([top, top, rest], axis=1)


def right3(value):
    top, rest = halves(value)
    return jnp.concatenate([top, rest, top], axis=0)


def dot3(a, b):
    return jnp.dot(a, b, preferred_element_type=F32)


def hop(place, direction, depth):
    x, y, z = place & 1, place >> 1 & 1, place >> 2
    if direction == 0:
        x ^= 1
    elif direction == 1:
        y ^= 1
    else:
        z += 1 if direction == 2 else -1
    return x + 2 * y + 4 * z if 0 <= z < depth else None


ROUTES = {
    0: ((0,), (1, 0, 1), (2, 0, 3), (3, 0, 2)),
    1: ((0, 1), (1, 0), (2, 0, 1, 3), (3, 1, 0, 2), (2, 1, 0, 3), (3, 0, 1, 2)),
    2: ((0,), (1, 0, 1), (2, 0, 3), (3, 0, 2)),
    3: ((0, 1, 2), (1, 2, 0), (2, 0, 1), (2, 1, 0), (0, 2, 1), (1, 0, 2)),
}


def routes_of(pair, depth):
    found = []
    for turns in ROUTES[pair % 4]:
        place, hops = pair, []
        for turn in turns:
            hops.append((place, turn))
            place = hop(place, turn, depth)
            if place is None:
                break
        if place == pair + 1:
            found.append(hops)
    return found


def neighbours(direction, count):
    depth = count // 4
    pairs = []
    for place in range(count):
        target = hop(place, direction, depth)
        if target is not None:
            pairs.append((place, target))
    return pairs


def schedule_kernel(count, width, slots, tiles, me_ref, send, recv, info, busy, state):
    depth = count // 4
    me = me_ref[0]
    dump = STEPS * 4

    def clear(i, _):
        for j in range(8):
            send[i * 8 + j] = -1
            recv[i * 8 + j] = -1
        return 0

    lax.fori_loop(0, dump // 8 + 1, clear, 0)
    for i in range(count * 4):
        busy[i] = 0
    for i in range(3):
        state[i] = 0
    need, filled = [], []
    for pair in range(count - 1):
        small = jnp.minimum(tiles[pair], tiles[pair + 1])
        strips = (small + 3) >> 2
        filled.append(width * strips * small * TROW)
        need.append((filled[-1] + (CHUNK - 1)) // CHUNK)
    top = need[0]
    for value in need[1:]:
        top = jnp.maximum(top, value)

    def level(i, _):
        k = top - i

        @pl.when(state[1] >= 1 << (DETOUR_END + 1))
        def _():
            used = state[1]
            length = jnp.int32(0)
            for shift in (16, 8, 4, 2, 1):
                large = used >= 1 << shift
                length += jnp.where(large, shift, 0)
                used = jnp.where(large, used >> shift, used)
            state[0] = state[0] + length + 1
            state[1] = 0
            state[2] = state[2] + 1
            for j in range(count * 4):
                busy[j] = 0

        for pair in range(count - 1):

            @pl.when(need[pair] >= k)
            def _(pair=pair):
                ways = routes_of(pair, depth)
                number_of = need[pair] - k
                rows = QUARTERS * CHUNK * (number_of + 1)
                quarter = jnp.minimum(lax.div(rows + filled[pair] - 1, filled[pair]), QUARTERS) - 1
                early = (1 << quarter) - 1
                best = jnp.int32(0x7FFFFFFF)
                choice = jnp.int32(0)
                start = jnp.int32(0)
                detour_ok = state[2] < 2
                for number, hops in enumerate(ways):
                    taken = jnp.int32(0)
                    for late, (place, turn) in enumerate(hops):
                        taken = taken | (busy[place * 4 + turn] >> late)
                    last = 31 if number == 0 else DETOUR_END + 1
                    free = ~(taken | early) & ((1 << (last - len(hops) + 1)) - 1)
                    low = free & -free
                    key = low << (len(hops) - 1)
                    better = (low > 0) & (key < best)
                    if number > 0:
                        better = better & detour_ok
                    best = jnp.where(better, key, best)
                    choice = jnp.where(better, number, choice)
                    start = jnp.where(better, low, start)
                state[1] = state[1] | best
                when = jnp.int32(0)
                bit = start
                for shift in (16, 8, 4, 2, 1):
                    large = bit >= 1 << shift
                    when += jnp.where(large, shift, 0)
                    bit = jnp.where(large, bit >> shift, bit)
                step = state[0] + when
                for number, hops in enumerate(ways):

                    @pl.when(choice == number)
                    def _(hops=hops):
                        for late, (place, turn) in enumerate(hops):
                            link = place * 4 + turn
                            busy[link] = busy[link] | (start << late)
                            at = (step + late) * 4 + turn
                            if late == 0:
                                from_slot = number_of
                            else:
                                before = hops[late - 1][1]
                                from_slot = 2 * slots + before
                            if late == len(hops) - 1:
                                to_slot = slots + number_of
                            else:
                                to_slot = 2 * slots + turn
                            send[jnp.where(me == place, at, dump)] = from_slot
                            there = hop(place, turn, depth)
                            recv[jnp.where(me == there, at, dump)] = to_slot

        return 0

    lax.fori_loop(0, top, level, 0)
    used = state[1]
    length = jnp.int32(0)
    for shift in (16, 8, 4, 2, 1):
        large = used >= 1 << shift
        length += jnp.where(large, shift, 0)
        used = jnp.where(large, used >> shift, used)
    info[0] = state[0] + length + jnp.where(state[1] > 0, 1, 0)


def schedule(sector_tiles, me, count, width, slots):
    size = STEPS * 4 + 8
    return pl.pallas_call(
        functools.partial(schedule_kernel, count, width, slots),
        out_shape=(
            jax.ShapeDtypeStruct((size,), jnp.int32),
            jax.ShapeDtypeStruct((size,), jnp.int32),
            jax.ShapeDtypeStruct((8,), jnp.int32),
        ),
        in_specs=[SMEM_SPEC, SMEM_SPEC],
        out_specs=(SMEM_SPEC, SMEM_SPEC, SMEM_SPEC),
        scratch_shapes=[pltpu.SMEM((count * 4,), jnp.int32), pltpu.SMEM((8,), jnp.int32)],
        name="route_schedule",
    )(sector_tiles, me)


def shuffle_kernel(slots, step_ref, send, recv, *refs):
    arrived, store, leaving = refs[:4], refs[-8], refs[-7:-3]
    held, sems_in, sems_out = refs[-3:]
    step = step_ref[0]

    def part(slot):
        return store.at[pl.ds(jnp.clip(slot, 0, 2 * slots - 1) * CHUNK, CHUNK)]

    loads, saves = [], []
    for turn in range(4):
        slot = recv[jnp.maximum(step - 1, 0) * 4 + turn]
        present = (step > 0) & (slot >= 0)
        loads.append((present, pltpu.make_async_copy(arrived[turn], held.at[turn], sems_in.at[turn])))
        final = present & (slot < 2 * slots)
        saves.append((final, pltpu.make_async_copy(held.at[turn], part(slot), sems_out.at[turn])))
    for turn in range(4):
        slot = send[step * 4 + turn]
        own = (slot >= 0) & (slot < 2 * slots)
        loads.append((own, pltpu.make_async_copy(part(slot), held.at[4 + turn], sems_in.at[4 + turn])))
        source = jnp.where(slot >= 2 * slots, slot & 3, 4 + turn)
        saves.append((slot >= 0, pltpu.make_async_copy(held.at[source], leaving[turn], sems_out.at[4 + turn])))
    begin(loads)
    finish(loads)
    begin(saves)
    finish(saves)


def shuffle(step, send, recv, arrived, store, after=()):
    chunk = jax.ShapeDtypeStruct((CHUNK, LANE), F32)
    slots = store.shape[0] // (2 * CHUNK)
    out = pl.pallas_call(
        functools.partial(shuffle_kernel, slots),
        out_shape=(jax.ShapeDtypeStruct(store.shape, F32),) + (chunk,) * 4,
        in_specs=[SMEM_SPEC] * 3 + [ANY_SPEC] * (5 + len(after)),
        out_specs=(ANY_SPEC,) * 5,
        scratch_shapes=[
            pltpu.VMEM((8, CHUNK, LANE), F32),
            pltpu.SemaphoreType.DMA((8,)),
            pltpu.SemaphoreType.DMA((8,)),
        ],
        input_output_aliases={7: 0},
        cost_estimate=pl.CostEstimate(flops=0, bytes_accessed=8 * 1024 * 1024, transcendentals=0),
        name="shuffle_chunks",
    )(jnp.reshape(step, (1,)).astype(jnp.int32), send, recv, *arrived, store, *after)
    return out[0], out[1:]


def prepare_kernel(sizes, x_ref, a3_ref, at3_ref):
    value = x_ref[0]
    row = lax.broadcasted_iota(jnp.int32, value.shape, 0)
    col = lax.broadcasted_iota(jnp.int32, value.shape, 1)
    keep = (row < sizes[0]) & (col < sizes[1 + pl.program_id(0)])
    value = jnp.where(keep, value, 0.0)
    a3_ref[0] = right3(value)
    at3_ref[0] = left3(value.T)


def prepare(sizes, tensors):
    number, rows, cols = tensors.shape
    return pl.pallas_call(
        prepare_kernel,
        grid=(number,),
        out_shape=(
            jax.ShapeDtypeStruct((number, 3 * rows, cols), BF16),
            jax.ShapeDtypeStruct((number, cols, 3 * rows), BF16),
        ),
        in_specs=[SMEM_SPEC, pl.BlockSpec((1, rows, cols), lambda s: (s, 0, 0))],
        out_specs=(
            pl.BlockSpec((1, 3 * rows, cols), lambda s: (s, 0, 0)),
            pl.BlockSpec((1, cols, 3 * rows), lambda s: (s, 0, 0)),
        ),
        compiler_params=params(),
        name="split_site",
    )(sizes, tensors)


def mix_kernel(coef_ref, mask_ref, e_ref, f_ref, k3):
    width, rows, cols = e_ref.shape
    full = k3.shape[0]
    few = full // width

    @pl.when(pl.program_id(0) == 0)
    def _():
        mixing = coef_ref[0] * mask_ref[...].astype(F32)
        row = lax.broadcasted_iota(jnp.int32, (full, width), 0)
        col = lax.broadcasted_iota(jnp.int32, (full, width), 1)
        pick = jnp.where(lax.div(row, few) == col, 1.0, 0.0).astype(F32)
        tall = lax.dot_general(pick, mixing, (((1,), (1,)), ((), ())), precision=HIGH)
        wide = lax.dot_general(tall, pick, (((1,), (1,)), ((), ())), precision=HIGH)
        down = lax.broadcasted_iota(jnp.int32, (full, full), 0)
        across = lax.broadcasted_iota(jnp.int32, (full, full), 1)
        k3[...] = left3(jnp.where(lax.rem(down, few) == lax.rem(across, few), wide, 0.0))

    for start in range(0, rows, 2 * few):
        parts = [
            e_ref[:, at : at + few, :].reshape(full, cols) for at in (start, start + few)
        ]
        result = dot3(k3[...], right3(jnp.concatenate(parts, axis=1)))
        for number, at in enumerate((start, start + few)):
            f_ref[:, at : at + few, :] = result[:, number * cols : (number + 1) * cols].reshape(width, few, cols)


def mix_all(coef, mask, env, spin):
    width, extent, _ = env.shape
    full = 256
    rows = 4 * full // width
    block = pl.BlockSpec((width, rows, extent), lambda c: (0, c, 0))
    return pl.pallas_call(
        mix_kernel,
        grid=(extent // rows,),
        out_shape=jax.ShapeDtypeStruct(env.shape, F32),
        in_specs=[
            pl.BlockSpec((1, width, width), lambda c: (spin, 0, 0)),
            pl.BlockSpec((width, width), lambda c: (0, 0)),
            block,
        ],
        out_specs=block,
        scratch_shapes=[pltpu.VMEM((full, 3 * full), BF16)],
        compiler_params=params(),
        cost_estimate=pl.CostEstimate(flops=6 * 10**9, bytes_accessed=32 * 2**20, transcendentals=0),
        name="mix_environment",
    )(coef, mask, env)


def strip_copies(plane, size, store, base, number, jcount, sem, inward):
    found = []
    size = pl.multiple_of(size, TROW)
    for j in range(plane.shape[1] // LANE):
        start = base + (number * jcount + j) * size
        flat = store.at[pl.ds(pl.multiple_of(start, TROW), size)]
        corner = plane.at[pl.ds(0, size), pl.ds(j * LANE, LANE)]
        pair = (flat, corner) if inward else (corner, flat)
        found.append((j < jcount, pltpu.make_async_copy(*pair, sem)))
    return found


def begin(copies):
    for wanted, copy in copies:

        @pl.when(wanted)
        def _(copy=copy):
            copy.start()


def finish(copies):
    for wanted, copy in copies:

        @pl.when(wanted)
        def _(copy=copy):
            copy.wait()


def outgoing_kernel(part, info, f_ref, a3_ref, at3_ref, *refs):
    store, planes, sems = refs[-3:]
    w = pl.program_id(0)
    count = pl.num_programs(0)
    half = planes.shape[1] // 2
    mode, size, jcount = info[0], info[1], info[2]
    slot = lax.rem(w, 2)

    def copies(index, place):
        number = part * count + index
        return strip_copies(planes.at[place], size, store, 0, number, jcount, sems.at[place], False)

    @pl.when((mode > 0) & (w >= 2))
    def _():
        finish(copies(w - 2, slot))

    @pl.when((mode == 1) & (size <= half))
    def _():
        inner = dot3(left3(f_ref[0]), a3_ref[0, :, :half])
        planes[slot, :half, :half] = dot3(at3_ref[0, :half, :], right3(inner))

    @pl.when((mode == 1) & (size > half))
    def _():
        inner = dot3(left3(f_ref[0]), a3_ref[0])
        planes[slot] = dot3(at3_ref[0], right3(inner))

    @pl.when(mode == 2)
    def _():
        planes[slot] = f_ref[0]

    @pl.when(mode > 0)
    def _():
        begin(copies(w, slot))

        @pl.when(w == count - 1)
        def _():
            finish(copies(w - 1, 1 - slot))
            finish(copies(w, slot))


def outgoing(info, mixed, a3, at3, slots, store, part):
    width, extent, _ = mixed.shape
    planes = width // QUARTERS
    first = store is None
    return pl.pallas_call(
        functools.partial(outgoing_kernel, part),
        grid=(planes,),
        out_shape=jax.ShapeDtypeStruct((2 * slots * CHUNK, LANE), F32),
        in_specs=[
            SMEM_SPEC,
            pl.BlockSpec((1, extent, extent), lambda w: (part * planes + w, 0, 0)),
            pl.BlockSpec((1,) + a3.shape[1:], lambda w: (1, 0, 0)),
            pl.BlockSpec((1,) + at3.shape[1:], lambda w: (1, 0, 0)),
        ]
        + ([] if first else [ANY_SPEC]),
        out_specs=ANY_SPEC,
        scratch_shapes=[pltpu.VMEM((2, extent, extent), F32), pltpu.SemaphoreType.DMA((2,))],
        input_output_aliases={} if first else {4: 0},
        compiler_params=params(),
        cost_estimate=pl.CostEstimate(
            flops=planes * 12 * extent**3, bytes_accessed=planes * 8 * extent**2, transcendentals=0
        ),
        name="outgoing_terms",
    )(info, mixed, a3, at3, *([] if first else [store]))


def staying_kernel(f_ref, a3_ref, at3_ref, out_ref):
    planes, extent, _ = f_ref.shape
    inner = dot3(left3(f_ref[...].reshape(planes * extent, extent)), a3_ref[0])
    for i in range(planes):
        out_ref[i] = dot3(at3_ref[0], right3(inner[i * extent : (i + 1) * extent]))


def staying(mixed, a3, at3, part, parts):
    width, extent, _ = mixed.shape
    few = 4
    grid = width // parts // few
    return pl.pallas_call(
        staying_kernel,
        grid=(grid,),
        out_shape=jax.ShapeDtypeStruct((few * grid, extent, extent), F32),
        in_specs=[
            pl.BlockSpec((few, extent, extent), lambda w: (part * grid + w, 0, 0)),
            pl.BlockSpec((1,) + a3.shape[1:], lambda w: (0, 0, 0)),
            pl.BlockSpec((1,) + at3.shape[1:], lambda w: (0, 0, 0)),
        ],
        out_specs=pl.BlockSpec((few, extent, extent), lambda w: (w, 0, 0)),
        compiler_params=params(),
        cost_estimate=pl.CostEstimate(
            flops=grid * few * 12 * extent**3, bytes_accessed=grid * few * 8 * extent**2, transcendentals=0
        ),
        name="staying_terms",
    )(mixed, a3, at3)


def arriving_kernel(part, info, stay_ref, a3_ref, at3_ref, store, *refs):
    out_ref, whole_ref, planes, sems = refs[-4:]
    w = pl.program_id(0)
    count = pl.num_programs(0)
    few, extent, _ = stay_ref.shape
    mode, size, jcount, base = info[0], info[1], info[2], info[3]
    slot = lax.rem(w, 2)

    def copies(index, place):
        found = []
        for i in range(few):
            number = (part * count + index) * few + i
            found += strip_copies(planes.at[place, i], size, store, base, number, jcount, sems.at[place], True)
        return found

    @pl.when(w == 0)
    def _():
        planes[...] = jnp.zeros_like(planes)

        @pl.when(mode > 0)
        def _():
            begin(copies(w, slot))

    @pl.when((mode > 0) & (w + 1 < count))
    def _():
        begin(copies(w + 1, 1 - slot))

    @pl.when(mode > 0)
    def _():
        finish(copies(w, slot))

    @pl.when(mode == 0)
    def _():
        out_ref[...] = stay_ref[...]
        whole_ref[...] = stay_ref[...]

    @pl.when(mode == 1)
    def _():
        fresh = stay_ref[...] + planes[slot]
        out_ref[...] = fresh
        whole_ref[...] = fresh

    @pl.when(mode == 2)
    def _():
        inner = dot3(left3(planes[slot].reshape(few * extent, extent)), a3_ref[0])
        for i in range(few):
            fresh = stay_ref[i] + dot3(at3_ref[0], right3(inner[i * extent : (i + 1) * extent]))
            out_ref[i] = fresh
            whole_ref[i] = fresh


def arriving(info, stay, a3, at3, store, whole, part, width):
    planes, extent, _ = stay.shape
    first = whole is None
    few = 2
    grid = planes // few
    block = pl.BlockSpec((few, extent, extent), lambda w: (w, 0, 0))
    return pl.pallas_call(
        functools.partial(arriving_kernel, part),
        grid=(grid,),
        out_shape=(
            jax.ShapeDtypeStruct((planes, extent, extent), F32),
            jax.ShapeDtypeStruct((width, extent, extent), F32),
        ),
        in_specs=[
            SMEM_SPEC,
            block,
            pl.BlockSpec((1,) + a3.shape[1:], lambda w: (0, 0, 0)),
            pl.BlockSpec((1,) + at3.shape[1:], lambda w: (0, 0, 0)),
            ANY_SPEC,
        ]
        + ([] if first else [ANY_SPEC]),
        out_specs=(block, pl.BlockSpec((few, extent, extent), lambda w: (part * grid + w, 0, 0))),
        scratch_shapes=[pltpu.VMEM((2, few, extent, extent), F32), pltpu.SemaphoreType.DMA((2,))],
        input_output_aliases={} if first else {5: 1},
        compiler_params=params(),
        cost_estimate=pl.CostEstimate(
            flops=planes * 6 * extent**3, bytes_accessed=planes * 16 * extent**2, transcendentals=0
        ),
        name="arriving_terms",
    )(info, stay, a3, at3, store, *([] if first else [whole]))


def center_kernel(part, first, info, coef, psi_ref, own_ref, other_ref, *refs):
    out_ref, p3 = refs[-2:]
    w = pl.program_id(0)
    few, extent, _ = own_ref.shape

    @pl.when(w == 0)
    def _():
        p3[...] = right3(psi_ref[...])
        if first:
            out_ref[...] = jnp.zeros_like(out_ref)
        else:
            out_ref[...] = refs[0][...]

    def add(left_ref, right_ref):
        inner = dot3(left3(left_ref[...].reshape(few * extent, extent)), p3[...])
        lefts, rights = [], []
        for i in range(few):
            weight = coef[(part * pl.num_programs(0) + w) * few + i]
            lefts.append(left3(inner[i * extent : (i + 1) * extent] * weight))
            rights.append(right3(right_ref[i]))
        out_ref[...] += dot3(jnp.concatenate(lefts, axis=1), jnp.concatenate(rights, axis=0))

    pl.when(info[4] == 0)(lambda: add(own_ref, other_ref))
    pl.when(info[4] != 0)(lambda: add(other_ref, own_ref))


def center(info, coef, psi, own, other, before, part):
    planes, extent, _ = own.shape
    first = before is None
    few = 2
    whole = pl.BlockSpec((extent, extent), lambda w: (0, 0))
    block = pl.BlockSpec((few, extent, extent), lambda w: (w, 0, 0))
    return pl.pallas_call(
        functools.partial(center_kernel, part, first),
        grid=(planes // few,),
        out_shape=jax.ShapeDtypeStruct((extent, extent), F32),
        in_specs=[SMEM_SPEC, SMEM_SPEC, whole, block, block] + ([] if first else [whole]),
        out_specs=whole,
        scratch_shapes=[pltpu.VMEM((3 * extent, extent), BF16)],
        compiler_params=params(),
        cost_estimate=pl.CostEstimate(
            flops=planes * 12 * extent**3, bytes_accessed=planes * 8 * extent**2, transcendentals=0
        ),
        name="center_terms",
    )(info, coef, psi, own, other, *([] if first else [before]))


def routed(env, site, sector_tiles, mpo_mask, mpo_coef, psi, center_coef):
    count = sector_tiles.shape[0]
    sector = lax.axis_index("block")
    section = lax.axis_index("section")
    blocks = env[0]
    width, extent, _ = blocks.shape
    slots = width * extent * extent // (CHUNK * LANE)
    edge = jnp.zeros((1,), jnp.int32)
    around = lax.dynamic_slice(jnp.concatenate([edge, sector_tiles, edge]) * TROW, (sector,), (3,))
    size_last, size_here, size_next = around[0], around[1], around[2]
    me = jnp.reshape(sector, (1,)).astype(jnp.int32)
    send, recv, steps = schedule(sector_tiles, me, count, width, slots)

    def pair_info(here, there, present, base):
        small = jnp.minimum(here, there)
        mode = jnp.where(present, jnp.where(here < there, 2, 1), 0)
        strips = (small + LANE - 1) // LANE
        return jnp.stack([mode, small, strips, base, section]).astype(jnp.int32)

    info_out = pair_info(size_here, size_next, sector + 1 < count, 0)
    info_in = pair_info(size_last, size_here, sector > 0, slots * CHUNK)

    tensors = jnp.swapaxes(site[0], 0, 1)
    earlier = lax.ppermute(tensors[1], "block", [(q, q + 1) for q in range(count - 1)])
    a3, at3 = prepare(jnp.stack([size_here, size_here, size_next]), tensors)
    rising = mix_all(mpo_coef[0], mpo_mask[0], blocks, 1)
    store = outgoing(info_out, rising, a3, at3, slots, None, 0)
    b3, bt3 = prepare(jnp.stack([size_last, size_here]), earlier[None])

    links = [neighbours(turn, count) for turn in range(4)]

    def exchange(leaving):
        return [lax.ppermute(leaving[turn], "block", links[turn]) for turn in range(4)]

    zero = jnp.zeros((CHUNK, LANE), F32)
    store, leaving = shuffle(jnp.int32(0), send, recv, [zero] * 4, store)
    stays = []
    fixed = QUARTERS + 2
    for step in range(fixed):
        arrived = exchange(leaving)
        beside = ()
        if step < QUARTERS - 1:
            store = outgoing(info_out, rising, a3, at3, slots, store, step + 1)
        elif step == QUARTERS - 1:
            mixed = mix_all(mpo_coef[0], mpo_mask[0], blocks, 0)
            beside = (mixed,)
        else:
            stays.append(staying(mixed, a3, at3, step - QUARTERS, 2))
            beside = (stays[-1],)
        store, leaving = shuffle(jnp.int32(step + 1), send, recv, arrived, store, beside)

    def more(carry):
        return carry[0] < steps[0]

    def onward(carry):
        step, store, leaving = carry
        arrived = exchange(leaving)
        store, leaving = shuffle(step + 1, send, recv, arrived, store)
        return step + 1, store, leaving

    _, store, _ = lax.while_loop(more, onward, (jnp.int32(fixed), store, leaving))

    whole, total = None, None
    for part, stay in enumerate(stays):
        fresh, whole = arriving(info_in, stay, b3, bt3, store, whole, part, width)
        partner = lax.ppermute(fresh, "section", [(0, 1), (1, 0)])
        total = center(info_in, center_coef[0], psi[0], fresh, partner, total, part)
    return whole[None], total[None]


def swapped(block, axis, distance):
    count = lax.axis_size(axis)
    route = []
    for low in range(count):
        high = low | 1 << distance
        if high != low and high < count:
            route += [(low, high), (high, low)]
    return lax.ppermute(block, axis, route)


def from_behind(value, axis, steps):
    count = lax.axis_size(axis)
    first, last = (max(0, -steps), min(count, count - steps))
    return lax.ppermute(value, axis, [(source, source + steps) for source in range(first, last)])


def ordered(is_upper, mine, theirs, axis_dim):
    return jnp.where(
        is_upper,
        jnp.concatenate([theirs, mine], axis=axis_dim),
        jnp.concatenate([mine, theirs], axis=axis_dim),
    )


def sandwich(masked, blocks):
    inner = jnp.einsum("wij,jk->wik", blocks, masked, precision=HIGH)
    return jnp.einsum("ji,wjk->wik", masked, inner, precision=HIGH)


def local(env, site, sector_tiles, mpo_mask, mpo_coef, psi, center_coef):
    nsector = sector_tiles.shape[0]
    group = lax.axis_size("block") // nsector
    levels = group.bit_length() - 1
    device = lax.axis_index("block")
    sector = device // group
    member = device % group
    section = lax.axis_index("section")
    width_local = env.shape[1]
    extent = env.shape[2]
    labels = jnp.arange(nsector, dtype=jnp.int32)
    counts = sector_tiles * TROW
    size_here = jnp.sum(jnp.where(labels == sector, counts, 0))
    size_next = jnp.sum(jnp.where(labels == sector + 1, counts, 0))
    span = jnp.arange(extent, dtype=jnp.int32)
    rows_now = site[0]
    wave_now = psi[0]
    for segment in range(levels):
        other_rows, other_wave = swapped((rows_now, wave_now), "block", segment)
        is_upper = member // 2**segment % 2 == 1
        rows_now = ordered(is_upper, rows_now, other_rows, 0)
        wave_now = ordered(is_upper, wave_now, other_wave, 0)
    row_keep = (span < size_here).astype(jnp.float32)
    masks = []
    for spin in range(2):
        limit = size_here if spin == 0 else size_next
        col_keep = (span < limit).astype(jnp.float32)
        masks.append(rows_now[:, spin, :] * row_keep[:, None] * col_keep[None, :])
    blocks = env[0]
    mixing = mpo_coef[0] * mpo_mask[0].astype(jnp.float32)
    collected = jnp.stack([sandwich(masks[0], blocks), sandwich(masks[1], blocks)])
    for segment in range(levels):
        other_terms = swapped(collected, "block", segment)
        is_upper = member // 2**segment % 2 == 1
        collected = ordered(is_upper, collected, other_terms, 1)
    own_cols = lax.dynamic_slice_in_dim(mixing, member * width_local, width_local, 2)
    reduced = jnp.einsum("xwv,xwij->xvij", own_cols, collected, precision=HIGH)
    arrived = from_behind(reduced[1], "block", group)
    fresh = reduced[0] + arrived
    partner = swapped(fresh, "section", 0)
    left_env = jnp.where(section == 0, fresh, partner)
    right_env = jnp.where(section == 0, partner, fresh)
    first = jnp.einsum("wij,jk->wik", left_env, wave_now, precision=HIGH)
    second = jnp.einsum("wij,wjk->wik", first, right_env, precision=HIGH)
    weights = lax.dynamic_slice_in_dim(center_coef[0], member * width_local, width_local, 0)
    summed = jnp.einsum("w,wik->ik", weights, second, precision=HIGH)
    for segment in reversed(range(levels)):
        half_rows = summed.shape[0] // 2
        lower_part = summed[:half_rows]
        upper_part = summed[half_rows:]
        is_upper = member // 2**segment % 2 == 1
        keeping = jnp.where(is_upper, upper_part, lower_part)
        sending = jnp.where(is_upper, lower_part, upper_part)
        summed = keeping + swapped(sending, "block", segment)
    return (fresh[None], summed[None])


def solution(mesh):
    placed = (
        P("section", "block", None, None),
        P("section", "block", None, None),
        P(),
        P("section", None, None),
        P("section", None, None, None),
        P("section", "block", None),
        P("section", None),
    )
    one_each = mesh.shape["block"] == 16
    return jax.shard_map(
        routed if one_each else local,
        mesh=mesh,
        in_specs=placed,
        out_specs=(P("section", "block", None, None), P("section", "block", None)),
        check_vma=False,
    )
```

```python
import functools

import jax
import jax.numpy as jnp
from jax import lax
from jax.experimental import pallas as pl
from jax.experimental.pallas import tpu as pltpu
from jax.sharding import PartitionSpec as P

TROW = 32
LANE = 128
CHUNK = 2048
STEPS = 128
DETOUR_END = 24
PARTS = 2
BYTES = 52 * 1024 * 1024

F32 = jnp.float32
BF16 = jnp.bfloat16
HIGH = lax.Precision.HIGHEST
SMEM_SPEC = pl.BlockSpec(memory_space=pltpu.SMEM)
ANY_SPEC = pl.BlockSpec(memory_space=pl.ANY)


def size_at(tiles, which):
    count = tiles.shape[0]
    inside = (which >= 0) & (which < count)
    return jnp.where(inside, tiles[jnp.clip(which, 0, count - 1)] * TROW, 0)


def pair_info(tiles, low):
    count = tiles.shape[0]
    here, following = size_at(tiles, low), size_at(tiles, low + 1)
    small = jnp.minimum(here, following)
    present = (low >= 0) & (low + 1 < count)
    mode = jnp.where(present, jnp.where(here < following, 2, 1), 0)
    return mode, small, (small + (LANE - 1)) >> 7


def params():
    return pltpu.CompilerParams(vmem_limit_bytes=BYTES)


def halves(value):
    top = value.astype(BF16)
    rest = (value - top.astype(F32)).astype(BF16)
    return top, rest


def left3(value):
    top, rest = halves(value)
    return jnp.concatenate([top, top, rest], axis=1)


def right3(value):
    top, rest = halves(value)
    return jnp.concatenate([top, rest, top], axis=0)


def dot3(a, b):
    return jnp.dot(a, b, preferred_element_type=F32)


def hop(place, direction, depth):
    x, y, z = place & 1, place >> 1 & 1, place >> 2
    if direction == 0:
        x ^= 1
    elif direction == 1:
        y ^= 1
    else:
        z += 1 if direction == 2 else -1
    return x + 2 * y + 4 * z if 0 <= z < depth else None


ROUTES = {
    0: ((0,), (1, 0, 1), (2, 0, 3), (3, 0, 2)),
    1: ((0, 1), (1, 0), (2, 0, 1, 3), (3, 1, 0, 2), (2, 1, 0, 3), (3, 0, 1, 2)),
    2: ((0,), (1, 0, 1), (2, 0, 3), (3, 0, 2)),
    3: ((0, 1, 2), (1, 2, 0), (2, 0, 1), (2, 1, 0), (0, 2, 1), (1, 0, 2)),
}


def routes_of(pair, depth):
    found = []
    for turns in ROUTES[pair % 4]:
        place, hops = pair, []
        for turn in turns:
            hops.append((place, turn))
            place = hop(place, turn, depth)
            if place is None:
                break
        if place == pair + 1:
            found.append(hops)
    return found


def neighbours(direction, count):
    depth = count // 4
    pairs = []
    for place in range(count):
        target = hop(place, direction, depth)
        if target is not None:
            pairs.append((place, target))
    return pairs


def schedule_kernel(count, width, slots, tiles, place, send, recv, info, busy, state):
    depth = count // 4
    me = place[0]
    dump = STEPS * 4

    def clear(i, _):
        for j in range(8):
            send[i * 8 + j] = -1
            recv[i * 8 + j] = -1
        return 0

    lax.fori_loop(0, dump // 8 + 1, clear, 0)
    for i in range(count * 4):
        busy[i] = 0
    for i in range(4):
        state[i] = 0
    need, filled = [], []
    for pair in range(count - 1):
        small = jnp.minimum(tiles[pair], tiles[pair + 1])
        strips = (small + 3) >> 2
        filled.append(width * strips * small * TROW)
        need.append((filled[-1] + (CHUNK - 1)) // CHUNK)
    top = need[0]
    for value in need[1:]:
        top = jnp.maximum(top, value)

    def level(i, _):
        k = top - i

        @pl.when(state[1] >= 1 << (DETOUR_END + 1))
        def _():
            used = state[1]
            length = jnp.int32(0)
            for shift in (16, 8, 4, 2, 1):
                large = used >= 1 << shift
                length += jnp.where(large, shift, 0)
                used = jnp.where(large, used >> shift, used)
            state[0] = state[0] + length + 1
            state[1] = 0
            state[2] = state[2] + 1
            for j in range(count * 4):
                busy[j] = 0

        for pair in range(count - 1):

            @pl.when(need[pair] >= k)
            def _(pair=pair):
                ways = routes_of(pair, depth)
                number_of = need[pair] - k
                rows = PARTS * CHUNK * (number_of + 1)
                half_of = jnp.minimum(lax.div(rows + filled[pair] - 1, filled[pair]), PARTS) - 1
                early = (1 << half_of) - 1
                best = jnp.int32(0x7FFFFFFF)
                choice = jnp.int32(0)
                start = jnp.int32(0)
                detour_ok = state[2] < 2
                for number, hops in enumerate(ways):
                    taken = jnp.int32(0)
                    for late, (place, turn) in enumerate(hops):
                        taken = taken | (busy[place * 4 + turn] >> late)
                    last = 31 if number == 0 else DETOUR_END + 1
                    free = ~(taken | early) & ((1 << (last - len(hops) + 1)) - 1)
                    low = free & -free
                    key = low << (len(hops) - 1)
                    better = (low > 0) & (key < best)
                    if number > 0:
                        better = better & detour_ok
                    best = jnp.where(better, key, best)
                    choice = jnp.where(better, number, choice)
                    start = jnp.where(better, low, start)
                state[1] = state[1] | best
                when = jnp.int32(0)
                bit = start
                for shift in (16, 8, 4, 2, 1):
                    large = bit >= 1 << shift
                    when += jnp.where(large, shift, 0)
                    bit = jnp.where(large, bit >> shift, bit)
                step = state[0] + when
                for number, hops in enumerate(ways):

                    @pl.when(choice == number)
                    def _(hops=hops):
                        due = jnp.where(2 * CHUNK * number_of < filled[pair], step + len(hops) + 1, 0)
                        state[3] = jnp.maximum(state[3], due)
                        for late, (place, turn) in enumerate(hops):
                            link = place * 4 + turn
                            busy[link] = busy[link] | (start << late)
                            at = (step + late) * 4 + turn
                            if late == 0:
                                from_slot = number_of
                            else:
                                before = hops[late - 1][1]
                                from_slot = 2 * slots + before
                            if late == len(hops) - 1:
                                to_slot = slots + number_of
                            else:
                                to_slot = 2 * slots + turn
                            send[jnp.where(me == place, at, dump)] = from_slot
                            there = hop(place, turn, depth)
                            recv[jnp.where(me == there, at, dump)] = to_slot

        return 0

    lax.fori_loop(0, top, level, 0)
    used = state[1]
    length = jnp.int32(0)
    for shift in (16, 8, 4, 2, 1):
        large = used >= 1 << shift
        length += jnp.where(large, shift, 0)
        used = jnp.where(large, used >> shift, used)
    info[0] = jnp.maximum(state[0] + length + jnp.where(state[1] > 0, 1, 0), state[3])


def schedule(sector_tiles, place, count, width, slots):
    size = STEPS * 4 + 8
    return pl.pallas_call(
        functools.partial(schedule_kernel, count, width, slots),
        out_shape=(
            jax.ShapeDtypeStruct((size,), jnp.int32),
            jax.ShapeDtypeStruct((size,), jnp.int32),
            jax.ShapeDtypeStruct((8,), jnp.int32),
        ),
        in_specs=[SMEM_SPEC, SMEM_SPEC],
        out_specs=(SMEM_SPEC, SMEM_SPEC, SMEM_SPEC),
        scratch_shapes=[pltpu.SMEM((count * 4,), jnp.int32), pltpu.SMEM((8,), jnp.int32)],
        name="route_schedule",
    )(sector_tiles, place)


def shuffle_kernel(slots, fed, step_ref, send, recv, *refs):
    arrived, store, leaving = refs[:fed], refs[-8], refs[-7:-3]
    held, sems_in, sems_out = refs[-3:]
    step = step_ref[0]

    def part(slot):
        return store.at[pl.ds(jnp.clip(slot, 0, 2 * slots - 1) * CHUNK, CHUNK)]

    loads, saves = [], []
    for turn in range(fed):
        slot = recv[jnp.maximum(step - 1, 0) * 4 + turn]
        present = (step > 0) & (slot >= 0)
        loads.append((present, pltpu.make_async_copy(arrived[turn], held.at[turn], sems_in.at[turn])))
        final = present & (slot < 2 * slots)
        saves.append((final, pltpu.make_async_copy(held.at[turn], part(slot), sems_out.at[turn])))
    for turn in range(4):
        slot = send[step * 4 + turn]
        own = (slot >= 0) & (slot < 2 * slots)
        loads.append((own, pltpu.make_async_copy(part(slot), held.at[4 + turn], sems_in.at[4 + turn])))
        source = jnp.where(slot >= 2 * slots, slot & 3, 4 + turn)
        saves.append((slot >= 0, pltpu.make_async_copy(held.at[source], leaving[turn], sems_out.at[4 + turn])))
    begin(loads)
    finish(loads)
    begin(saves)
    finish(saves)


def shuffle(step, send, recv, arrived, store, after=()):
    chunk = jax.ShapeDtypeStruct((CHUNK, LANE), F32)
    slots = store.shape[0] // (2 * CHUNK)
    out = pl.pallas_call(
        functools.partial(shuffle_kernel, slots, len(arrived)),
        out_shape=(jax.ShapeDtypeStruct(store.shape, F32),) + (chunk,) * 4,
        in_specs=[SMEM_SPEC] * 3 + [ANY_SPEC] * (len(arrived) + 1 + len(after)),
        out_specs=(ANY_SPEC,) * 5,
        scratch_shapes=[
            pltpu.VMEM((8, CHUNK, LANE), F32),
            pltpu.SemaphoreType.DMA((8,)),
            pltpu.SemaphoreType.DMA((8,)),
        ],
        input_output_aliases={3 + len(arrived): 0},
        cost_estimate=pl.CostEstimate(flops=0, bytes_accessed=8 * 1024 * 1024, transcendentals=0),
        name="shuffle_chunks",
    )(jnp.reshape(step, (1,)).astype(jnp.int32), send, recv, *arrived, store, *after)
    return out[0], out[1:]


def prepare_kernel(low, column, tiles, place, x_ref, a3_ref, at3_ref):
    value = x_ref[0]
    row = lax.broadcasted_iota(jnp.int32, value.shape, 0)
    col = lax.broadcasted_iota(jnp.int32, value.shape, 1)
    keep = (row < size_at(tiles, place[0] + low)) & (col < size_at(tiles, place[0] + column))
    value = jnp.where(keep, value, 0.0)
    a3_ref[0] = right3(value)
    at3_ref[0] = left3(value.T)


def prepare(sector_tiles, place, tensors, which, low, column):
    _, rows, cols = tensors.shape
    return pl.pallas_call(
        functools.partial(prepare_kernel, low, column),
        grid=(1,),
        out_shape=(
            jax.ShapeDtypeStruct((1, 3 * rows, cols), BF16),
            jax.ShapeDtypeStruct((1, cols, 3 * rows), BF16),
        ),
        in_specs=[SMEM_SPEC, SMEM_SPEC, pl.BlockSpec((1, rows, cols), lambda s: (which, 0, 0))],
        out_specs=(
            pl.BlockSpec((1, 3 * rows, cols), lambda s: (0, 0, 0)),
            pl.BlockSpec((1, cols, 3 * rows), lambda s: (0, 0, 0)),
        ),
        compiler_params=params(),
        cost_estimate=pl.CostEstimate(flops=0, bytes_accessed=4 * 2**20, transcendentals=0),
        name="split_site",
    )(sector_tiles, place, tensors)


def mix_kernel(coef_ref, mask_ref, e_ref, f_ref, k3):
    width, rows, cols = e_ref.shape
    full = k3.shape[0]
    few = full // width

    @pl.when(pl.program_id(0) == 0)
    def _():
        mixing = coef_ref[0] * mask_ref[...].astype(F32)
        row = lax.broadcasted_iota(jnp.int32, (full, width), 0)
        col = lax.broadcasted_iota(jnp.int32, (full, width), 1)
        pick = jnp.where(lax.div(row, few) == col, 1.0, 0.0).astype(F32)
        tall = lax.dot_general(pick, mixing, (((1,), (1,)), ((), ())), precision=HIGH)
        wide = lax.dot_general(tall, pick, (((1,), (1,)), ((), ())), precision=HIGH)
        down = lax.broadcasted_iota(jnp.int32, (full, full), 0)
        across = lax.broadcasted_iota(jnp.int32, (full, full), 1)
        k3[...] = left3(jnp.where(lax.rem(down, few) == lax.rem(across, few), wide, 0.0))

    for start in range(0, rows, 2 * few):
        parts = [
            e_ref[:, at : at + few, :].reshape(full, cols) for at in (start, start + few)
        ]
        result = dot3(k3[...], right3(jnp.concatenate(parts, axis=1)))
        for number, at in enumerate((start, start + few)):
            f_ref[:, at : at + few, :] = result[:, number * cols : (number + 1) * cols].reshape(width, few, cols)


def mix_all(coef, mask, env, spin):
    width, extent, _ = env.shape
    full = 256
    rows = 2 * full // width
    block = pl.BlockSpec((width, rows, extent), lambda c: (0, c, 0))
    return pl.pallas_call(
        mix_kernel,
        grid=(extent // rows,),
        out_shape=jax.ShapeDtypeStruct(env.shape, F32),
        in_specs=[
            pl.BlockSpec((1, width, width), lambda c: (spin, 0, 0)),
            pl.BlockSpec((width, width), lambda c: (0, 0)),
            block,
        ],
        out_specs=block,
        scratch_shapes=[pltpu.VMEM((full, 3 * full), BF16)],
        compiler_params=params(),
        cost_estimate=pl.CostEstimate(flops=6 * 10**9, bytes_accessed=32 * 2**20, transcendentals=0),
        name="mix_environment",
    )(coef, mask, env)


def strip_copies(plane, size, store, base, number, jcount, sem, inward):
    found = []
    size = pl.multiple_of(size, TROW)
    for j in range(plane.shape[1] // LANE):
        start = base + (number * jcount + j) * size
        flat = store.at[pl.ds(pl.multiple_of(start, TROW), size)]
        corner = plane.at[pl.ds(0, size), pl.ds(j * LANE, LANE)]
        pair = (flat, corner) if inward else (corner, flat)
        found.append((j < jcount, pltpu.make_async_copy(*pair, sem)))
    return found


def begin(copies):
    for wanted, copy in copies:

        @pl.when(wanted)
        def _(copy=copy):
            copy.start()


def finish(copies):
    for wanted, copy in copies:

        @pl.when(wanted)
        def _(copy=copy):
            copy.wait()


def outgoing_kernel(part, tiles, place, f_ref, a3_ref, at3_ref, *refs):
    store, planes, sems = refs[-3:]
    w = pl.program_id(0)
    count = pl.num_programs(0)
    few, extent, _ = f_ref.shape
    half = extent // 2
    mode, size, jcount = pair_info(tiles, place[0])
    slot = lax.rem(w, 2)

    def copies(index, side):
        found = []
        for i in range(few):
            number = (part * count + index) * few + i
            found += strip_copies(planes.at[side, i], size, store, 0, number, jcount, sems.at[side], False)
        return found

    @pl.when((mode > 0) & (w >= 2))
    def _():
        finish(copies(w - 2, slot))

    def absorb(used):
        inner = dot3(left3(f_ref[...].reshape(few * extent, extent)), a3_ref[0, :, :used])
        for i in range(few):
            block = dot3(at3_ref[0, :used, :], right3(inner[i * extent : (i + 1) * extent]))
            planes[slot, i, :used, :used] = block

    pl.when((mode == 1) & (size <= half))(lambda: absorb(half))
    pl.when((mode == 1) & (size > half))(lambda: absorb(extent))

    @pl.when(mode == 2)
    def _():
        planes[slot] = f_ref[...]

    @pl.when(mode > 0)
    def _():
        begin(copies(w, slot))

        @pl.when(w == count - 1)
        def _():
            finish(copies(w - 1, 1 - slot))
            finish(copies(w, slot))


def outgoing(sector_tiles, place, mixed, a3, at3, slots, store, part):
    width, extent, _ = mixed.shape
    few = 2
    grid = width // PARTS // few
    first = store is None
    return pl.pallas_call(
        functools.partial(outgoing_kernel, part),
        grid=(grid,),
        out_shape=jax.ShapeDtypeStruct((2 * slots * CHUNK, LANE), F32),
        in_specs=[
            SMEM_SPEC,
            SMEM_SPEC,
            pl.BlockSpec((few, extent, extent), lambda w: (part * grid + w, 0, 0)),
            pl.BlockSpec((1,) + a3.shape[1:], lambda w: (0, 0, 0)),
            pl.BlockSpec((1,) + at3.shape[1:], lambda w: (0, 0, 0)),
        ]
        + ([] if first else [ANY_SPEC]),
        out_specs=ANY_SPEC,
        scratch_shapes=[pltpu.VMEM((2, few, extent, extent), F32), pltpu.SemaphoreType.DMA((2,))],
        input_output_aliases={} if first else {5: 0},
        compiler_params=params(),
        cost_estimate=pl.CostEstimate(
            flops=few * grid * 12 * extent**3, bytes_accessed=few * grid * 8 * extent**2, transcendentals=0
        ),
        name="outgoing_terms",
    )(sector_tiles, place, mixed, a3, at3, *([] if first else [store]))


def staying_kernel(f_ref, a3_ref, at3_ref, out_ref):
    planes, extent, _ = f_ref.shape
    a_top, a_rest = a3_ref[0, :extent, :], a3_ref[0, extent : 2 * extent, :]
    at_top, at_rest = at3_ref[0, :, :extent], at3_ref[0, :, 2 * extent :]
    top, rest = halves(f_ref[...].reshape(planes * extent, extent))
    inner = dot3(top, a_top) + dot3(top, a_rest) + dot3(rest, a_top)
    for i in range(planes):
        top, rest = halves(inner[i * extent : (i + 1) * extent])
        out_ref[i] = dot3(at_top, top) + dot3(at_top, rest) + dot3(at_rest, top)


def staying(mixed, a3, at3, part, parts):
    width, extent, _ = mixed.shape
    few = 2
    grid = width // parts // few
    return pl.pallas_call(
        staying_kernel,
        grid=(grid,),
        out_shape=jax.ShapeDtypeStruct((few * grid, extent, extent), F32),
        in_specs=[
            pl.BlockSpec((few, extent, extent), lambda w: (part * grid + w, 0, 0)),
            pl.BlockSpec((1,) + a3.shape[1:], lambda w: (0, 0, 0)),
            pl.BlockSpec((1,) + at3.shape[1:], lambda w: (0, 0, 0)),
        ],
        out_specs=pl.BlockSpec((few, extent, extent), lambda w: (w, 0, 0)),
        compiler_params=params(),
        cost_estimate=pl.CostEstimate(
            flops=grid * few * 12 * extent**3, bytes_accessed=grid * few * 8 * extent**2, transcendentals=0
        ),
        name="staying_terms",
    )(mixed, a3, at3)


def arriving_kernel(part, base, tiles, place, stay_ref, a3_ref, at3_ref, store, *refs):
    out_ref, whole_ref, planes, sems = refs[-4:]
    w = pl.program_id(0)
    count = pl.num_programs(0)
    few, extent, _ = stay_ref.shape
    mode, size, jcount = pair_info(tiles, place[0] - 1)
    slot = lax.rem(w, 2)

    def copies(index, side):
        found = []
        for i in range(few):
            number = (part * count + index) * few + i
            found += strip_copies(planes.at[side, i], size, store, base, number, jcount, sems.at[side], True)
        return found

    @pl.when(w == 0)
    def _():
        planes[...] = jnp.zeros_like(planes)

        @pl.when(mode > 0)
        def _():
            begin(copies(w, slot))

    @pl.when((mode > 0) & (w + 1 < count))
    def _():
        begin(copies(w + 1, 1 - slot))

    @pl.when(mode > 0)
    def _():
        finish(copies(w, slot))

    @pl.when(mode == 0)
    def _():
        out_ref[...] = stay_ref[...]
        whole_ref[...] = stay_ref[...]

    @pl.when(mode == 1)
    def _():
        fresh = stay_ref[...] + planes[slot]
        out_ref[...] = fresh
        whole_ref[...] = fresh

    @pl.when(mode == 2)
    def _():
        inner = dot3(left3(planes[slot].reshape(few * extent, extent)), a3_ref[0])
        for i in range(few):
            fresh = stay_ref[i] + dot3(at3_ref[0], right3(inner[i * extent : (i + 1) * extent]))
            out_ref[i] = fresh
            whole_ref[i] = fresh


def arriving(sector_tiles, place, stay, a3, at3, store, whole, part, width):
    planes, extent, _ = stay.shape
    first = whole is None
    few = 2
    grid = planes // few
    block = pl.BlockSpec((few, extent, extent), lambda w: (w, 0, 0))
    return pl.pallas_call(
        functools.partial(arriving_kernel, part, store.shape[0] // 2),
        grid=(grid,),
        out_shape=(
            jax.ShapeDtypeStruct((planes, extent, extent), F32),
            jax.ShapeDtypeStruct((width, extent, extent), F32),
        ),
        in_specs=[
            SMEM_SPEC,
            SMEM_SPEC,
            block,
            pl.BlockSpec((1,) + a3.shape[1:], lambda w: (0, 0, 0)),
            pl.BlockSpec((1,) + at3.shape[1:], lambda w: (0, 0, 0)),
            ANY_SPEC,
        ]
        + ([] if first else [ANY_SPEC]),
        out_specs=(block, pl.BlockSpec((few, extent, extent), lambda w: (part * grid + w, 0, 0))),
        scratch_shapes=[pltpu.VMEM((2, few, extent, extent), F32), pltpu.SemaphoreType.DMA((2,))],
        input_output_aliases={} if first else {6: 1},
        compiler_params=params(),
        cost_estimate=pl.CostEstimate(
            flops=planes * 6 * extent**3, bytes_accessed=planes * 16 * extent**2, transcendentals=0
        ),
        name="arriving_terms",
    )(sector_tiles, place, stay, a3, at3, store, *([] if first else [whole]))


def center_kernel(part, first, place, coef, psi_ref, own_ref, other_ref, *refs):
    out_ref, p3 = refs[-2:]
    w = pl.program_id(0)
    few, extent, _ = own_ref.shape

    @pl.when(w == 0)
    def _():
        p3[...] = right3(psi_ref[...])
        if first:
            out_ref[...] = jnp.zeros_like(out_ref)
        else:
            out_ref[...] = refs[0][...]

    def add(left_ref, right_ref):
        inner = dot3(left3(left_ref[...].reshape(few * extent, extent)), p3[...])
        lefts, rights = [], []
        for i in range(few):
            weight = coef[(part * pl.num_programs(0) + w) * few + i]
            lefts.append(left3(inner[i * extent : (i + 1) * extent] * weight))
            rights.append(right3(right_ref[i]))
        out_ref[...] += dot3(jnp.concatenate(lefts, axis=1), jnp.concatenate(rights, axis=0))

    pl.when(place[1] == 0)(lambda: add(own_ref, other_ref))
    pl.when(place[1] != 0)(lambda: add(other_ref, own_ref))


def center(place, coef, psi, own, other, before, part):
    planes, extent, _ = own.shape
    first = before is None
    few = 2
    whole = pl.BlockSpec((extent, extent), lambda w: (0, 0))
    block = pl.BlockSpec((few, extent, extent), lambda w: (w, 0, 0))
    return pl.pallas_call(
        functools.partial(center_kernel, part, first),
        grid=(planes // few,),
        out_shape=jax.ShapeDtypeStruct((extent, extent), F32),
        in_specs=[SMEM_SPEC, SMEM_SPEC, whole, block, block] + ([] if first else [whole]),
        out_specs=whole,
        scratch_shapes=[pltpu.VMEM((3 * extent, extent), BF16)],
        compiler_params=params(),
        cost_estimate=pl.CostEstimate(
            flops=planes * 12 * extent**3, bytes_accessed=planes * 8 * extent**2, transcendentals=0
        ),
        name="center_terms",
    )(place, coef, psi, own, other, *([] if first else [before]))


def routed(env, site, sector_tiles, mpo_mask, mpo_coef, psi, center_coef):
    count = sector_tiles.shape[0]
    sector = lax.axis_index("block")
    section = lax.axis_index("section")
    blocks = env[0]
    width, extent, _ = blocks.shape
    slots = width * extent * extent // (CHUNK * LANE)
    place = jnp.stack([sector, section]).astype(jnp.int32)
    send, recv, steps = schedule(sector_tiles, place, count, width, slots)
    tensors = jnp.swapaxes(site[0], 0, 1)
    earlier = lax.ppermute(tensors[1], "block", [(q, q + 1) for q in range(count - 1)])
    a3, at3 = prepare(sector_tiles, place, tensors, 1, 0, 1)
    rising = mix_all(mpo_coef[0], mpo_mask[0], blocks, 1)
    store = outgoing(sector_tiles, place, rising, a3, at3, slots, None, 0)

    links = [neighbours(turn, count) for turn in range(4)]

    def exchange(leaving):
        return [lax.ppermute(leaving[turn], "block", links[turn]) for turn in range(4)]

    store, leaving = shuffle(jnp.int32(0), send, recv, [], store, (earlier,))
    b3, bt3 = prepare(sector_tiles, place, earlier[None], 0, -1, 0)
    c3, ct3 = prepare(sector_tiles, place, tensors, 0, 0, 0)
    stays = []
    fixed = 2 + PARTS
    for step in range(fixed):
        arrived = exchange(leaving)
        beside = ()
        if step == 0:
            store = outgoing(sector_tiles, place, rising, a3, at3, slots, store, 1)
        elif step == 1:
            mixed = mix_all(mpo_coef[0], mpo_mask[0], blocks, 0)
            beside = (mixed,)
        else:
            stays.append(staying(mixed, c3, ct3, step - 2, PARTS))
            beside = (stays[-1],)
        store, leaving = shuffle(jnp.int32(step + 1), send, recv, arrived, store, beside)

    def more(carry):
        return carry[0] < steps[0] - 1

    def onward(carry):
        step, store, leaving = carry
        arrived = exchange(leaving)
        store, leaving = shuffle(step + 1, send, recv, arrived, store)
        return step + 1, store, leaving

    step, store, leaving = lax.while_loop(more, onward, (jnp.int32(fixed), store, leaving))

    def swap(fresh):
        return lax.ppermute(fresh, "section", [(0, 1), (1, 0)])

    arrived = exchange(leaving)
    fresh, whole = arriving(sector_tiles, place, stays[0], b3, bt3, store, None, 0, width)
    partner = swap(fresh)
    store, _ = shuffle(step + 1, send, recv, arrived, store, (fresh,))
    fresh_end, whole = arriving(sector_tiles, place, stays[1], b3, bt3, store, whole, 1, width)
    partner_end = swap(fresh_end)
    total = center(place, center_coef[0], psi[0], fresh, partner, None, 0)
    total = center(place, center_coef[0], psi[0], fresh_end, partner_end, total, 1)
    return whole[None], total[None]


def swapped(block, axis, distance):
    count = lax.axis_size(axis)
    route = []
    for low in range(count):
        high = low | 1 << distance
        if high != low and high < count:
            route += [(low, high), (high, low)]
    return lax.ppermute(block, axis, route)


def from_behind(value, axis, steps):
    count = lax.axis_size(axis)
    first, last = (max(0, -steps), min(count, count - steps))
    return lax.ppermute(value, axis, [(source, source + steps) for source in range(first, last)])


def ordered(is_upper, mine, theirs, axis_dim):
    return jnp.where(
        is_upper,
        jnp.concatenate([theirs, mine], axis=axis_dim),
        jnp.concatenate([mine, theirs], axis=axis_dim),
    )


def sandwich(masked, blocks):
    inner = jnp.einsum("wij,jk->wik", blocks, masked, precision=HIGH)
    return jnp.einsum("ji,wjk->wik", masked, inner, precision=HIGH)


def local(env, site, sector_tiles, mpo_mask, mpo_coef, psi, center_coef):
    nsector = sector_tiles.shape[0]
    group = lax.axis_size("block") // nsector
    levels = group.bit_length() - 1
    device = lax.axis_index("block")
    sector = device // group
    member = device % group
    section = lax.axis_index("section")
    width_local = env.shape[1]
    extent = env.shape[2]
    labels = jnp.arange(nsector, dtype=jnp.int32)
    counts = sector_tiles * TROW
    size_here = jnp.sum(jnp.where(labels == sector, counts, 0))
    size_next = jnp.sum(jnp.where(labels == sector + 1, counts, 0))
    span = jnp.arange(extent, dtype=jnp.int32)
    rows_now = site[0]
    wave_now = psi[0]
    for segment in range(levels):
        other_rows, other_wave = swapped((rows_now, wave_now), "block", segment)
        is_upper = member // 2**segment % 2 == 1
        rows_now = ordered(is_upper, rows_now, other_rows, 0)
        wave_now = ordered(is_upper, wave_now, other_wave, 0)
    row_keep = (span < size_here).astype(jnp.float32)
    masks = []
    for spin in range(2):
        limit = size_here if spin == 0 else size_next
        col_keep = (span < limit).astype(jnp.float32)
        masks.append(rows_now[:, spin, :] * row_keep[:, None] * col_keep[None, :])
    blocks = env[0]
    mixing = mpo_coef[0] * mpo_mask[0].astype(jnp.float32)
    collected = jnp.stack([sandwich(masks[0], blocks), sandwich(masks[1], blocks)])
    for segment in range(levels):
        other_terms = swapped(collected, "block", segment)
        is_upper = member // 2**segment % 2 == 1
        collected = ordered(is_upper, collected, other_terms, 1)
    own_cols = lax.dynamic_slice_in_dim(mixing, member * width_local, width_local, 2)
    reduced = jnp.einsum("xwv,xwij->xvij", own_cols, collected, precision=HIGH)
    arrived = from_behind(reduced[1], "block", group)
    fresh = reduced[0] + arrived
    partner = swapped(fresh, "section", 0)
    left_env = jnp.where(section == 0, fresh, partner)
    right_env = jnp.where(section == 0, partner, fresh)
    first = jnp.einsum("wij,jk->wik", left_env, wave_now, precision=HIGH)
    second = jnp.einsum("wij,wjk->wik", first, right_env, precision=HIGH)
    weights = lax.dynamic_slice_in_dim(center_coef[0], member * width_local, width_local, 0)
    summed = jnp.einsum("w,wik->ik", weights, second, precision=HIGH)
    for segment in reversed(range(levels)):
        half_rows = summed.shape[0] // 2
        lower_part = summed[:half_rows]
        upper_part = summed[half_rows:]
        is_upper = member // 2**segment % 2 == 1
        keeping = jnp.where(is_upper, upper_part, lower_part)
        sending = jnp.where(is_upper, lower_part, upper_part)
        summed = keeping + swapped(sending, "block", segment)
    return (fresh[None], summed[None])


def solution(mesh):
    placed = (
        P("section", "block", None, None),
        P("section", "block", None, None),
        P(),
        P("section", None, None),
        P("section", None, None, None),
        P("section", "block", None),
        P("section", None),
    )
    one_each = mesh.shape["block"] == 16
    return jax.shard_map(
        routed if one_each else local,
        mesh=mesh,
        in_specs=placed,
        out_specs=(P("section", "block", None, None), P("section", "block", None)),
        check_vma=False,
    )
```

```python
import functools

import jax
import jax.numpy as jnp
from jax import lax
from jax.experimental import pallas as pl
from jax.experimental.pallas import tpu as pltpu
from jax.sharding import PartitionSpec as P

TROW = 32
LANE = 128
CHUNK = 2048
STEPS = 128
DETOUR_END = 24
PARTS = 2
BYTES = 52 * 1024 * 1024

F32 = jnp.float32
BF16 = jnp.bfloat16
HIGH = lax.Precision.HIGHEST
SMEM_SPEC = pl.BlockSpec(memory_space=pltpu.SMEM)
ANY_SPEC = pl.BlockSpec(memory_space=pl.ANY)


def size_at(tiles, which):
    count = tiles.shape[0]
    inside = (which >= 0) & (which < count)
    return jnp.where(inside, tiles[jnp.clip(which, 0, count - 1)] * TROW, 0)


def pair_info(tiles, low):
    count = tiles.shape[0]
    here, following = size_at(tiles, low), size_at(tiles, low + 1)
    small = jnp.minimum(here, following)
    present = (low >= 0) & (low + 1 < count)
    mode = jnp.where(present, jnp.where(here < following, 2, 1), 0)
    return mode, small, (small + (LANE - 1)) >> 7


def params(extra=0):
    return pltpu.CompilerParams(vmem_limit_bytes=BYTES + extra)


def halves(value):
    top = value.astype(BF16)
    rest = (value - top.astype(F32)).astype(BF16)
    return top, rest


def left3(value):
    top, rest = halves(value)
    return jnp.concatenate([top, top, rest], axis=1)


def right3(value):
    top, rest = halves(value)
    return jnp.concatenate([top, rest, top], axis=0)


def dot3(a, b):
    return jnp.dot(a, b, preferred_element_type=F32)


def hop(place, direction, depth):
    x, y, z = place & 1, place >> 1 & 1, place >> 2
    if direction == 0:
        x ^= 1
    elif direction == 1:
        y ^= 1
    else:
        z += 1 if direction == 2 else -1
    return x + 2 * y + 4 * z if 0 <= z < depth else None


ROUTES = {
    0: ((0,), (1, 0, 1), (2, 0, 3), (3, 0, 2)),
    1: ((0, 1), (1, 0), (2, 0, 1, 3), (3, 1, 0, 2), (2, 1, 0, 3), (3, 0, 1, 2)),
    2: ((0,), (1, 0, 1), (2, 0, 3), (3, 0, 2)),
    3: ((0, 1, 2), (1, 2, 0), (2, 0, 1), (2, 1, 0), (0, 2, 1), (1, 0, 2)),
}


def routes_of(pair, depth):
    found = []
    for turns in ROUTES[pair % 4]:
        place, hops = pair, []
        for turn in turns:
            hops.append((place, turn))
            place = hop(place, turn, depth)
            if place is None:
                break
        if place == pair + 1:
            found.append(hops)
    return found


def neighbours(direction, count):
    depth = count // 4
    pairs = []
    for place in range(count):
        target = hop(place, direction, depth)
        if target is not None:
            pairs.append((place, target))
    return pairs


def schedule_kernel(count, width, slots, tiles, place, send, recv, info, busy, state):
    depth = count // 4
    me = place[0]
    dump = STEPS * 4

    def clear(i, _):
        for j in range(8):
            send[i * 8 + j] = -1
            recv[i * 8 + j] = -1
        return 0

    lax.fori_loop(0, dump // 8 + 1, clear, 0)
    for i in range(count * 4):
        busy[i] = 0
    for i in range(4):
        state[i] = 0
    need, filled = [], []
    for pair in range(count - 1):
        small = jnp.minimum(tiles[pair], tiles[pair + 1])
        strips = (small + 3) >> 2
        filled.append(width * strips * small * TROW)
        need.append((filled[-1] + (CHUNK - 1)) // CHUNK)
    top = need[0]
    for value in need[1:]:
        top = jnp.maximum(top, value)

    def level(i, _):
        k = top - i

        @pl.when(state[1] >= 1 << (DETOUR_END + 1))
        def _():
            used = state[1]
            length = jnp.int32(0)
            for shift in (16, 8, 4, 2, 1):
                large = used >= 1 << shift
                length += jnp.where(large, shift, 0)
                used = jnp.where(large, used >> shift, used)
            state[0] = state[0] + length + 1
            state[1] = 0
            state[2] = state[2] + 1
            for j in range(count * 4):
                busy[j] = 0

        for pair in range(count - 1):

            @pl.when(need[pair] >= k)
            def _(pair=pair):
                ways = routes_of(pair, depth)
                number_of = need[pair] - k
                rows = PARTS * CHUNK * (number_of + 1)
                half_of = jnp.minimum(lax.div(rows + filled[pair] - 1, filled[pair]), PARTS) - 1
                early = (1 << half_of) - 1
                best = jnp.int32(0x7FFFFFFF)
                choice = jnp.int32(0)
                start = jnp.int32(0)
                detour_ok = state[2] < 2
                for number, hops in enumerate(ways):
                    taken = jnp.int32(0)
                    for late, (place, turn) in enumerate(hops):
                        taken = taken | (busy[place * 4 + turn] >> late)
                    last = 31 if number == 0 else DETOUR_END + 1
                    free = ~(taken | early) & ((1 << (last - len(hops) + 1)) - 1)
                    low = free & -free
                    key = low << (len(hops) - 1)
                    better = (low > 0) & (key < best)
                    if number > 0:
                        better = better & detour_ok
                    best = jnp.where(better, key, best)
                    choice = jnp.where(better, number, choice)
                    start = jnp.where(better, low, start)
                state[1] = state[1] | best
                when = jnp.int32(0)
                bit = start
                for shift in (16, 8, 4, 2, 1):
                    large = bit >= 1 << shift
                    when += jnp.where(large, shift, 0)
                    bit = jnp.where(large, bit >> shift, bit)
                step = state[0] + when
                for number, hops in enumerate(ways):

                    @pl.when(choice == number)
                    def _(hops=hops):
                        due = jnp.where(2 * CHUNK * number_of < filled[pair], step + len(hops) + 1, 0)
                        state[3] = jnp.maximum(state[3], due)
                        for late, (place, turn) in enumerate(hops):
                            link = place * 4 + turn
                            busy[link] = busy[link] | (start << late)
                            at = (step + late) * 4 + turn
                            if late == 0:
                                from_slot = number_of
                            else:
                                before = hops[late - 1][1]
                                from_slot = 2 * slots + before
                            if late == len(hops) - 1:
                                to_slot = slots + number_of
                            else:
                                to_slot = 2 * slots + turn
                            send[jnp.where(me == place, at, dump)] = from_slot
                            there = hop(place, turn, depth)
                            recv[jnp.where(me == there, at, dump)] = to_slot

        return 0

    lax.fori_loop(0, top, level, 0)
    used = state[1]
    length = jnp.int32(0)
    for shift in (16, 8, 4, 2, 1):
        large = used >= 1 << shift
        length += jnp.where(large, shift, 0)
        used = jnp.where(large, used >> shift, used)
    info[0] = jnp.maximum(state[0] + length + jnp.where(state[1] > 0, 1, 0), state[3])


def schedule(sector_tiles, place, count, width, slots):
    size = STEPS * 4 + 8
    return pl.pallas_call(
        functools.partial(schedule_kernel, count, width, slots),
        out_shape=(
            jax.ShapeDtypeStruct((size,), jnp.int32),
            jax.ShapeDtypeStruct((size,), jnp.int32),
            jax.ShapeDtypeStruct((8,), jnp.int32),
        ),
        in_specs=[SMEM_SPEC, SMEM_SPEC],
        out_specs=(SMEM_SPEC, SMEM_SPEC, SMEM_SPEC),
        scratch_shapes=[pltpu.SMEM((count * 4,), jnp.int32), pltpu.SMEM((8,), jnp.int32)],
        name="route_schedule",
    )(sector_tiles, place)


def shuffle_kernel(slots, fed, step_ref, send, recv, *refs):
    arrived, store, leaving = refs[:fed], refs[-8], refs[-7:-3]
    held, sems_in, sems_out = refs[-3:]
    step = step_ref[0]

    def part(slot):
        return store.at[pl.ds(jnp.clip(slot, 0, 2 * slots - 1) * CHUNK, CHUNK)]

    loads, saves = [], []
    for turn in range(fed):
        slot = recv[jnp.maximum(step - 1, 0) * 4 + turn]
        present = (step > 0) & (slot >= 0)
        loads.append((present, pltpu.make_async_copy(arrived[turn], held.at[turn], sems_in.at[turn])))
        final = present & (slot < 2 * slots)
        saves.append((final, pltpu.make_async_copy(held.at[turn], part(slot), sems_out.at[turn])))
    for turn in range(4):
        slot = send[step * 4 + turn]
        own = (slot >= 0) & (slot < 2 * slots)
        loads.append((own, pltpu.make_async_copy(part(slot), held.at[4 + turn], sems_in.at[4 + turn])))
        source = jnp.where(slot >= 2 * slots, slot & 3, 4 + turn)
        saves.append((slot >= 0, pltpu.make_async_copy(held.at[source], leaving[turn], sems_out.at[4 + turn])))
    begin(loads)
    finish(loads)
    begin(saves)
    finish(saves)


def shuffle(step, send, recv, arrived, store, after=()):
    chunk = jax.ShapeDtypeStruct((CHUNK, LANE), F32)
    slots = store.shape[0] // (2 * CHUNK)
    out = pl.pallas_call(
        functools.partial(shuffle_kernel, slots, len(arrived)),
        out_shape=(jax.ShapeDtypeStruct(store.shape, F32),) + (chunk,) * 4,
        in_specs=[SMEM_SPEC] * 3 + [ANY_SPEC] * (len(arrived) + 1 + len(after)),
        out_specs=(ANY_SPEC,) * 5,
        scratch_shapes=[
            pltpu.VMEM((8, CHUNK, LANE), F32),
            pltpu.SemaphoreType.DMA((8,)),
            pltpu.SemaphoreType.DMA((8,)),
        ],
        input_output_aliases={3 + len(arrived): 0},
        cost_estimate=pl.CostEstimate(flops=0, bytes_accessed=8 * 1024 * 1024, transcendentals=0),
        name="shuffle_chunks",
    )(jnp.reshape(step, (1,)).astype(jnp.int32), send, recv, *arrived, store, *after)
    return out[0], out[1:]


def prepare_kernel(low, column, spin, tiles, place, x_ref, a3_ref, at3_ref, *raw_ref):
    value = x_ref[0] if spin is None else x_ref[0, :, spin, :]
    for ref in raw_ref:
        ref[0] = value
    row = lax.broadcasted_iota(jnp.int32, value.shape, 0)
    col = lax.broadcasted_iota(jnp.int32, value.shape, 1)
    keep = (row < size_at(tiles, place[0] + low)) & (col < size_at(tiles, place[0] + column))
    value = jnp.where(keep, value, 0.0)
    a3_ref[0] = right3(value)
    at3_ref[0] = left3(value.T)


def prepare(sector_tiles, place, tensor, low, column, spin=None, keep_raw=False):
    rows, cols = tensor.shape[1], tensor.shape[-1]
    shapes = [((1, 3 * rows, cols), BF16), ((1, cols, 3 * rows), BF16)]
    if keep_raw:
        shapes.append(((1, rows, cols), F32))
    block = pl.BlockSpec(tensor.shape, lambda s: (0,) * tensor.ndim)
    return pl.pallas_call(
        functools.partial(prepare_kernel, low, column, spin),
        grid=(1,),
        out_shape=tuple(jax.ShapeDtypeStruct(*shape) for shape in shapes),
        in_specs=[SMEM_SPEC, SMEM_SPEC, block],
        out_specs=tuple(pl.BlockSpec(shape, lambda s: (0, 0, 0)) for shape, _ in shapes),
        compiler_params=params(),
        cost_estimate=pl.CostEstimate(flops=0, bytes_accessed=4 * 2**20, transcendentals=0),
        name="split_site",
    )(sector_tiles, place, tensor)


def mix_kernel(coef_ref, mask_ref, e_ref, f_ref, k2):
    width, rows, cols = e_ref.shape
    few = 8
    full = width * few

    @pl.when(pl.program_id(0) == 0)
    def _():
        mixing = coef_ref[0] * mask_ref[...].astype(F32)
        row = lax.broadcasted_iota(jnp.int32, (full, width), 0)
        col = lax.broadcasted_iota(jnp.int32, (full, width), 1)
        pick = jnp.where(lax.div(row, few) == col, 1.0, 0.0).astype(F32)
        tall = lax.dot_general(pick, mixing, (((1,), (1,)), ((), ())), precision=HIGH)
        wide = lax.dot_general(tall, pick, (((1,), (1,)), ((), ())), precision=HIGH)
        down = lax.broadcasted_iota(jnp.int32, (full, full), 0)
        across = lax.broadcasted_iota(jnp.int32, (full, full), 1)
        top, rest = halves(jnp.where(lax.rem(down, few) == lax.rem(across, few), wide, 0.0))
        k2[:full, :full] = top
        k2[:full, full:] = top
        k2[full:, :full] = rest
        k2[full:, full:] = jnp.zeros_like(rest)

    for start in range(0, rows, 2 * few):
        parts = [
            e_ref[:, at : at + few, :].reshape(full, cols) for at in (start, start + few)
        ]
        top, rest = halves(jnp.concatenate(parts, axis=1))
        both = dot3(k2[...], jnp.concatenate([top, rest], axis=0))
        result = both[:full] + both[full:]
        for number, at in enumerate((start, start + few)):
            f_ref[:, at : at + few, :] = result[:, number * cols : (number + 1) * cols].reshape(width, few, cols)


def mix_all(coef, mask, env, spin):
    width, extent, _ = env.shape
    rows = 64
    block = pl.BlockSpec((width, rows, extent), lambda c: (0, c, 0))
    return pl.pallas_call(
        mix_kernel,
        grid=(extent // rows,),
        out_shape=jax.ShapeDtypeStruct(env.shape, F32),
        in_specs=[
            pl.BlockSpec((1, width, width), lambda c: (spin, 0, 0)),
            pl.BlockSpec((width, width), lambda c: (0, 0)),
            block,
        ],
        out_specs=block,
        scratch_shapes=[pltpu.VMEM((2 * 8 * width, 2 * 8 * width), BF16)],
        compiler_params=params(),
        cost_estimate=pl.CostEstimate(flops=4 * 10**9, bytes_accessed=32 * 2**20, transcendentals=0),
        name="mix_environment",
    )(coef, mask, env)


def sandwich3(planes, a3, at3):
    few, used, _ = planes.shape
    extent = a3.shape[0] // 3
    a_top, a_rest = a3[:used], a3[extent : extent + used]
    at_top, at_rest = at3[:, :used], at3[:, 2 * extent : 2 * extent + used]
    top, rest = halves(planes.reshape(few * used, used))
    inner = dot3(top, a_top) + dot3(top, a_rest) + dot3(rest, a_top)
    found = []
    for i in range(few):
        top, rest = halves(inner[i * used : (i + 1) * used])
        found.append(dot3(at_top, top) + dot3(at_top, rest) + dot3(at_rest, top))
    return found


def strip_copies(plane, size, store, base, number, jcount, sem, inward):
    found = []
    size = pl.multiple_of(size, TROW)
    for j in range(plane.shape[1] // LANE):
        start = base + (number * jcount + j) * size
        flat = store.at[pl.ds(pl.multiple_of(start, TROW), size)]
        corner = plane.at[pl.ds(0, size), pl.ds(j * LANE, LANE)]
        pair = (flat, corner) if inward else (corner, flat)
        found.append((j < jcount, pltpu.make_async_copy(*pair, sem)))
    return found


def begin(copies):
    for wanted, copy in copies:

        @pl.when(wanted)
        def _(copy=copy):
            copy.start()


def finish(copies):
    for wanted, copy in copies:

        @pl.when(wanted)
        def _(copy=copy):
            copy.wait()


def outgoing_kernel(part, tiles, place, f_ref, a3_ref, at3_ref, *refs):
    store, planes, sems = refs[-3:]
    w = pl.program_id(0)
    count = pl.num_programs(0)
    few, extent, _ = f_ref.shape
    half = extent // 2
    mode, size, jcount = pair_info(tiles, place[0])
    slot = lax.rem(w, 2)

    def copies(index, side):
        found = []
        for i in range(few):
            number = (part * count + index) * few + i
            found += strip_copies(planes.at[side, i], size, store, 0, number, jcount, sems.at[side], False)
        return found

    @pl.when((mode > 0) & (w >= 2))
    def _():
        finish(copies(w - 2, slot))

    def absorb(used):
        for i, block in enumerate(sandwich3(f_ref[...], a3_ref[0, :, :used], at3_ref[0, :used, :])):
            planes[slot, i, :used, :used] = block

    pl.when((mode == 1) & (size <= half))(lambda: absorb(half))
    pl.when((mode == 1) & (size > half))(lambda: absorb(extent))

    @pl.when(mode == 2)
    def _():
        planes[slot] = f_ref[...]

    @pl.when(mode > 0)
    def _():
        begin(copies(w, slot))

        @pl.when(w == count - 1)
        def _():
            finish(copies(w - 1, 1 - slot))
            finish(copies(w, slot))


def outgoing(sector_tiles, place, mixed, a3, at3, slots, store, part):
    width, extent, _ = mixed.shape
    few = 2
    grid = width // PARTS // few
    first = store is None
    return pl.pallas_call(
        functools.partial(outgoing_kernel, part),
        grid=(grid,),
        out_shape=jax.ShapeDtypeStruct((2 * slots * CHUNK, LANE), F32),
        in_specs=[
            SMEM_SPEC,
            SMEM_SPEC,
            pl.BlockSpec((few, extent, extent), lambda w: (part * grid + w, 0, 0)),
            pl.BlockSpec((1,) + a3.shape[1:], lambda w: (0, 0, 0)),
            pl.BlockSpec((1,) + at3.shape[1:], lambda w: (0, 0, 0)),
        ]
        + ([] if first else [ANY_SPEC]),
        out_specs=ANY_SPEC,
        scratch_shapes=[pltpu.VMEM((2, few, extent, extent), F32), pltpu.SemaphoreType.DMA((2,))],
        input_output_aliases={} if first else {5: 0},
        compiler_params=params(),
        cost_estimate=pl.CostEstimate(
            flops=few * grid * 12 * extent**3, bytes_accessed=few * grid * 8 * extent**2, transcendentals=0
        ),
        name="outgoing_terms",
    )(sector_tiles, place, mixed, a3, at3, *([] if first else [store]))


def staying_kernel(f_ref, a3_ref, at3_ref, out_ref):
    for i, block in enumerate(sandwich3(f_ref[...], a3_ref[0], at3_ref[0])):
        out_ref[i] = block


def staying(mixed, a3, at3, part, parts):
    width, extent, _ = mixed.shape
    few = 2
    grid = width // parts // few
    return pl.pallas_call(
        staying_kernel,
        grid=(grid,),
        out_shape=jax.ShapeDtypeStruct((few * grid, extent, extent), F32),
        in_specs=[
            pl.BlockSpec((few, extent, extent), lambda w: (part * grid + w, 0, 0)),
            pl.BlockSpec((1,) + a3.shape[1:], lambda w: (0, 0, 0)),
            pl.BlockSpec((1,) + at3.shape[1:], lambda w: (0, 0, 0)),
        ],
        out_specs=pl.BlockSpec((few, extent, extent), lambda w: (w, 0, 0)),
        compiler_params=params(),
        cost_estimate=pl.CostEstimate(
            flops=grid * few * 12 * extent**3, bytes_accessed=grid * few * 8 * extent**2, transcendentals=0
        ),
        name="staying_terms",
    )(mixed, a3, at3)


def arriving_kernel(part, base, tiles, place, stay_ref, a3_ref, at3_ref, store, *refs):
    out_ref, whole_ref, planes, sems = refs[-4:]
    w = pl.program_id(0)
    count = pl.num_programs(0)
    few, extent, _ = stay_ref.shape
    mode, size, jcount = pair_info(tiles, place[0] - 1)
    slot = lax.rem(w, 2)

    def copies(index, side):
        found = []
        for i in range(few):
            number = (part * count + index) * few + i
            found += strip_copies(planes.at[side, i], size, store, base, number, jcount, sems.at[side], True)
        return found

    @pl.when(w == 0)
    def _():
        planes[...] = jnp.zeros_like(planes)

        @pl.when(mode > 0)
        def _():
            begin(copies(w, slot))

    @pl.when((mode > 0) & (w + 1 < count))
    def _():
        begin(copies(w + 1, 1 - slot))

    @pl.when(mode > 0)
    def _():
        finish(copies(w, slot))

    @pl.when(mode == 0)
    def _():
        out_ref[...] = stay_ref[...]
        whole_ref[...] = stay_ref[...]

    @pl.when(mode == 1)
    def _():
        fresh = stay_ref[...] + planes[slot]
        out_ref[...] = fresh
        whole_ref[...] = fresh

    def absorb(used):
        for i, block in enumerate(sandwich3(planes[slot, :, :used, :used], a3_ref[0], at3_ref[0])):
            fresh = stay_ref[i] + block
            out_ref[i] = fresh
            whole_ref[i] = fresh

    pl.when((mode == 2) & (size <= extent // 2))(lambda: absorb(extent // 2))
    pl.when((mode == 2) & (size > extent // 2))(lambda: absorb(extent))


def arriving(sector_tiles, place, stay, a3, at3, store, whole, part, width):
    planes, extent, _ = stay.shape
    first = whole is None
    few = 2
    grid = planes // few
    block = pl.BlockSpec((few, extent, extent), lambda w: (w, 0, 0))
    return pl.pallas_call(
        functools.partial(arriving_kernel, part, store.shape[0] // 2),
        grid=(grid,),
        out_shape=(
            jax.ShapeDtypeStruct((planes, extent, extent), F32),
            jax.ShapeDtypeStruct((width, extent, extent), F32),
        ),
        in_specs=[
            SMEM_SPEC,
            SMEM_SPEC,
            block,
            pl.BlockSpec((1,) + a3.shape[1:], lambda w: (0, 0, 0)),
            pl.BlockSpec((1,) + at3.shape[1:], lambda w: (0, 0, 0)),
            ANY_SPEC,
        ]
        + ([] if first else [ANY_SPEC]),
        out_specs=(block, pl.BlockSpec((few, extent, extent), lambda w: (part * grid + w, 0, 0))),
        scratch_shapes=[pltpu.VMEM((2, few, extent, extent), F32), pltpu.SemaphoreType.DMA((2,))],
        input_output_aliases={} if first else {6: 1},
        compiler_params=params(),
        cost_estimate=pl.CostEstimate(
            flops=planes * 6 * extent**3, bytes_accessed=planes * 16 * extent**2, transcendentals=0
        ),
        name="arriving_terms",
    )(sector_tiles, place, stay, a3, at3, store, *([] if first else [whole]))


def center_kernel(part, first, place, coef, psi_ref, own_ref, other_ref, *refs):
    out_ref, p3 = refs[-2:]
    w = pl.program_id(0)
    few, extent, _ = own_ref.shape

    @pl.when(w == 0)
    def _():
        p3[...] = right3(psi_ref[...])
        if first:
            out_ref[...] = jnp.zeros_like(out_ref)
        else:
            out_ref[...] = refs[0][...]

    def add(left_ref, right_ref):
        inner = dot3(left3(left_ref[...].reshape(few * extent, extent)), p3[...])
        lefts, rights = [], []
        for i in range(few):
            weight = coef[(part * pl.num_programs(0) + w) * few + i]
            lefts.append(left3(inner[i * extent : (i + 1) * extent] * weight))
            rights.append(right3(right_ref[i]))
        out_ref[...] += dot3(jnp.concatenate(lefts, axis=1), jnp.concatenate(rights, axis=0))

    pl.when(place[1] == 0)(lambda: add(own_ref, other_ref))
    pl.when(place[1] != 0)(lambda: add(other_ref, own_ref))


def center(place, coef, psi, own, other, before, part):
    planes, extent, _ = own.shape
    first = before is None
    few = 2
    whole = pl.BlockSpec((extent, extent), lambda w: (0, 0))
    block = pl.BlockSpec((few, extent, extent), lambda w: (w, 0, 0))
    return pl.pallas_call(
        functools.partial(center_kernel, part, first),
        grid=(planes // few,),
        out_shape=jax.ShapeDtypeStruct((extent, extent), F32),
        in_specs=[SMEM_SPEC, SMEM_SPEC, whole, block, block] + ([] if first else [whole]),
        out_specs=whole,
        scratch_shapes=[pltpu.VMEM((3 * extent, extent), BF16)],
        compiler_params=params(8 * 1024 * 1024),
        cost_estimate=pl.CostEstimate(
            flops=planes * 12 * extent**3, bytes_accessed=planes * 8 * extent**2, transcendentals=0
        ),
        name="center_terms",
    )(place, coef, psi, own, other, *([] if first else [before]))


def routed(env, site, sector_tiles, mpo_mask, mpo_coef, psi, center_coef):
    count = sector_tiles.shape[0]
    sector = lax.axis_index("block")
    section = lax.axis_index("section")
    blocks = env[0]
    width, extent, _ = blocks.shape
    slots = width * extent * extent // (CHUNK * LANE)
    place = jnp.stack([sector, section]).astype(jnp.int32)
    send, recv, steps = schedule(sector_tiles, place, count, width, slots)
    a3, at3, rise = prepare(sector_tiles, place, site, 0, 1, 1, True)
    earlier = lax.ppermute(rise, "block", [(q, q + 1) for q in range(count - 1)])
    rising = mix_all(mpo_coef[0], mpo_mask[0], blocks, 1)
    store = outgoing(sector_tiles, place, rising, a3, at3, slots, None, 0)

    links = [neighbours(turn, count) for turn in range(4)]

    def exchange(leaving):
        return [lax.ppermute(leaving[turn], "block", links[turn]) for turn in range(4)]

    store, leaving = shuffle(jnp.int32(0), send, recv, [], store, (earlier,))
    b3, bt3 = prepare(sector_tiles, place, earlier, -1, 0)
    c3, ct3 = prepare(sector_tiles, place, site, 0, 0, 0)
    stays = []
    fixed = 2 + PARTS
    for step in range(fixed):
        arrived = exchange(leaving)
        beside = ()
        if step == 0:
            store = outgoing(sector_tiles, place, rising, a3, at3, slots, store, 1)
        elif step == 1:
            mixed = mix_all(mpo_coef[0], mpo_mask[0], blocks, 0)
            beside = (mixed,)
        else:
            stays.append(staying(mixed, c3, ct3, step - 2, PARTS))
            beside = (stays[-1],)
        store, leaving = shuffle(jnp.int32(step + 1), send, recv, arrived, store, beside)

    def more(carry):
        return carry[0] < steps[0] - 1

    def onward(carry):
        step, store, leaving = carry
        arrived = exchange(leaving)
        store, leaving = shuffle(step + 1, send, recv, arrived, store)
        return step + 1, store, leaving

    step, store, leaving = lax.while_loop(more, onward, (jnp.int32(fixed), store, leaving))

    def swap(fresh):
        return lax.ppermute(fresh, "section", [(0, 1), (1, 0)])

    arrived = exchange(leaving)
    fresh, whole = arriving(sector_tiles, place, stays[0], b3, bt3, store, None, 0, width)
    partner = swap(fresh)
    store, _ = shuffle(step + 1, send, recv, arrived, store, (fresh,))
    fresh_end, whole = arriving(sector_tiles, place, stays[1], b3, bt3, store, whole, 1, width)
    partner_end = swap(fresh_end)
    total = center(place, center_coef[0], psi[0], fresh, partner, None, 0)
    total = center(place, center_coef[0], psi[0], fresh_end, partner_end, total, 1)
    return whole[None], total[None]


def swapped(block, axis, distance):
    count = lax.axis_size(axis)
    route = []
    for low in range(count):
        high = low | 1 << distance
        if high != low and high < count:
            route += [(low, high), (high, low)]
    return lax.ppermute(block, axis, route)


def from_behind(value, axis, steps):
    count = lax.axis_size(axis)
    first, last = (max(0, -steps), min(count, count - steps))
    return lax.ppermute(value, axis, [(source, source + steps) for source in range(first, last)])


def ordered(is_upper, mine, theirs, axis_dim):
    return jnp.where(
        is_upper,
        jnp.concatenate([theirs, mine], axis=axis_dim),
        jnp.concatenate([mine, theirs], axis=axis_dim),
    )


def sandwich(masked, blocks):
    inner = jnp.einsum("wij,jk->wik", blocks, masked, precision=HIGH)
    return jnp.einsum("ji,wjk->wik", masked, inner, precision=HIGH)


def local(env, site, sector_tiles, mpo_mask, mpo_coef, psi, center_coef):
    nsector = sector_tiles.shape[0]
    group = lax.axis_size("block") // nsector
    levels = group.bit_length() - 1
    device = lax.axis_index("block")
    sector = device // group
    member = device % group
    section = lax.axis_index("section")
    width_local = env.shape[1]
    extent = env.shape[2]
    labels = jnp.arange(nsector, dtype=jnp.int32)
    counts = sector_tiles * TROW
    size_here = jnp.sum(jnp.where(labels == sector, counts, 0))
    size_next = jnp.sum(jnp.where(labels == sector + 1, counts, 0))
    span = jnp.arange(extent, dtype=jnp.int32)
    rows_now = site[0]
    wave_now = psi[0]
    for segment in range(levels):
        other_rows, other_wave = swapped((rows_now, wave_now), "block", segment)
        is_upper = member // 2**segment % 2 == 1
        rows_now = ordered(is_upper, rows_now, other_rows, 0)
        wave_now = ordered(is_upper, wave_now, other_wave, 0)
    row_keep = (span < size_here).astype(jnp.float32)
    masks = []
    for spin in range(2):
        limit = size_here if spin == 0 else size_next
        col_keep = (span < limit).astype(jnp.float32)
        masks.append(rows_now[:, spin, :] * row_keep[:, None] * col_keep[None, :])
    blocks = env[0]
    mixing = mpo_coef[0] * mpo_mask[0].astype(jnp.float32)
    collected = jnp.stack([sandwich(masks[0], blocks), sandwich(masks[1], blocks)])
    for segment in range(levels):
        other_terms = swapped(collected, "block", segment)
        is_upper = member // 2**segment % 2 == 1
        collected = ordered(is_upper, collected, other_terms, 1)
    own_cols = lax.dynamic_slice_in_dim(mixing, member * width_local, width_local, 2)
    reduced = jnp.einsum("xwv,xwij->xvij", own_cols, collected, precision=HIGH)
    arrived = from_behind(reduced[1], "block", group)
    fresh = reduced[0] + arrived
    partner = swapped(fresh, "section", 0)
    left_env = jnp.where(section == 0, fresh, partner)
    right_env = jnp.where(section == 0, partner, fresh)
    first = jnp.einsum("wij,jk->wik", left_env, wave_now, precision=HIGH)
    second = jnp.einsum("wij,wjk->wik", first, right_env, precision=HIGH)
    weights = lax.dynamic_slice_in_dim(center_coef[0], member * width_local, width_local, 0)
    summed = jnp.einsum("w,wik->ik", weights, second, precision=HIGH)
    for segment in reversed(range(levels)):
        half_rows = summed.shape[0] // 2
        lower_part = summed[:half_rows]
        upper_part = summed[half_rows:]
        is_upper = member // 2**segment % 2 == 1
        keeping = jnp.where(is_upper, upper_part, lower_part)
        sending = jnp.where(is_upper, lower_part, upper_part)
        summed = keeping + swapped(sending, "block", segment)
    return (fresh[None], summed[None])


def solution(mesh):
    placed = (
        P("section", "block", None, None),
        P("section", "block", None, None),
        P(),
        P("section", None, None),
        P("section", None, None, None),
        P("section", "block", None),
        P("section", None),
    )
    one_each = mesh.shape["block"] == 16
    return jax.shard_map(
        routed if one_each else local,
        mesh=mesh,
        in_specs=placed,
        out_specs=(P("section", "block", None, None), P("section", "block", None)),
        check_vma=False,
    )
```

```python
import functools

import jax
import jax.numpy as jnp
from jax import lax
from jax.experimental import pallas as pl
from jax.experimental.pallas import tpu as pltpu
from jax.sharding import PartitionSpec as P

TROW = 32
LANE = 128
CHUNK = 2048
STEPS = 128
DETOUR_END = 24
PARTS = 2
BYTES = 52 * 1024 * 1024

F32 = jnp.float32
BF16 = jnp.bfloat16
HIGH = lax.Precision.HIGHEST
SMEM_SPEC = pl.BlockSpec(memory_space=pltpu.SMEM)
ANY_SPEC = pl.BlockSpec(memory_space=pl.ANY)


def size_at(tiles, which):
    count = tiles.shape[0]
    inside = (which >= 0) & (which < count)
    return jnp.where(inside, tiles[jnp.clip(which, 0, count - 1)] * TROW, 0)


def pair_info(tiles, low):
    count = tiles.shape[0]
    here, following = size_at(tiles, low), size_at(tiles, low + 1)
    small = jnp.minimum(here, following)
    present = (low >= 0) & (low + 1 < count)
    mode = jnp.where(present, jnp.where(here < following, 2, 1), 0)
    return mode, small, (small + (LANE - 1)) >> 7


def params(extra=0):
    return pltpu.CompilerParams(vmem_limit_bytes=BYTES + extra)


def halves(value):
    top = value.astype(BF16)
    rest = (value - top.astype(F32)).astype(BF16)
    return top, rest


def left3(value):
    top, rest = halves(value)
    return jnp.concatenate([top, top, rest], axis=1)


def right3(value):
    top, rest = halves(value)
    return jnp.concatenate([top, rest, top], axis=0)


def dot3(a, b):
    return jnp.dot(a, b, preferred_element_type=F32)


def hop(place, turn, depth):
    x, y, z = place & 1, place >> 1 & 1, place >> 2
    if turn == 0:
        x ^= 1
    elif turn == 1:
        y ^= 1
    elif turn == 2:
        z ^= 1
    else:
        z += 1 if z & 1 else -1
    return x + 2 * y + 4 * z if 0 <= z < depth else None


ROUTES = {
    0: ((0,), (1, 0, 1), (2, 0, 3), (3, 0, 2)),
    1: ((0, 1), (1, 0), (2, 0, 1, 3), (3, 1, 0, 2), (2, 1, 0, 3), (3, 0, 1, 2)),
    2: ((0,), (1, 0, 1), (2, 0, 3), (3, 0, 2)),
    3: ((0, 1, 2), (1, 2, 0), (2, 0, 1), (2, 1, 0), (0, 2, 1), (1, 0, 2)),
}


def routes_of(pair, depth):
    found = []
    for turns in ROUTES[pair % 4]:
        place, hops = pair, []
        for turn in turns:
            if turn >= 2:
                turn = 2 if (place >> 2 & 1) == turn - 2 else 3
            hops.append((place, turn))
            place = hop(place, turn, depth)
            if place is None:
                break
        if place == pair + 1:
            found.append(hops)
    return found


def neighbours(direction, count):
    depth = count // 4
    pairs = []
    for place in range(count):
        target = hop(place, direction, depth)
        if target is not None:
            pairs.append((place, target))
    return pairs


def schedule_kernel(count, width, slots, tiles, place, send, recv, info, busy, state):
    depth = count // 4
    me = place[0]
    dump = STEPS * 4

    def clear(i, _):
        for j in range(8):
            send[i * 8 + j] = -1
            recv[i * 8 + j] = -1
        return 0

    lax.fori_loop(0, dump // 8 + 1, clear, 0)
    for i in range(count * 4):
        busy[i] = 0
    for i in range(4):
        state[i] = 0
    need, filled = [], []
    for pair in range(count - 1):
        small = jnp.minimum(tiles[pair], tiles[pair + 1])
        strips = (small + 3) >> 2
        filled.append(width * strips * small * TROW)
        need.append((filled[-1] + (CHUNK - 1)) // CHUNK)
    top = need[0]
    for value in need[1:]:
        top = jnp.maximum(top, value)

    def level(i, _):
        k = top - i

        @pl.when(state[1] >= 1 << (DETOUR_END + 1))
        def _():
            used = state[1]
            length = jnp.int32(0)
            for shift in (16, 8, 4, 2, 1):
                large = used >= 1 << shift
                length += jnp.where(large, shift, 0)
                used = jnp.where(large, used >> shift, used)
            state[0] = state[0] + length + 1
            state[1] = 0
            state[2] = state[2] + 1
            for j in range(count * 4):
                busy[j] = 0

        for pair in range(count - 1):

            @pl.when(need[pair] >= k)
            def _(pair=pair):
                ways = routes_of(pair, depth)
                number_of = need[pair] - k
                rows = PARTS * CHUNK * (number_of + 1)
                half_of = jnp.minimum(lax.div(rows + filled[pair] - 1, filled[pair]), PARTS) - 1
                early = (1 << half_of) - 1
                best = jnp.int32(0x7FFFFFFF)
                choice = jnp.int32(0)
                start = jnp.int32(0)
                detour_ok = state[2] < 2
                for number, hops in enumerate(ways):
                    taken = jnp.int32(0)
                    for late, (place, turn) in enumerate(hops):
                        taken = taken | (busy[place * 4 + turn] >> late)
                    last = 31 if number == 0 else DETOUR_END + 1
                    free = ~(taken | early) & ((1 << (last - len(hops) + 1)) - 1)
                    low = free & -free
                    key = low << (len(hops) - 1)
                    better = (low > 0) & (key < best)
                    if number > 0:
                        better = better & detour_ok
                    best = jnp.where(better, key, best)
                    choice = jnp.where(better, number, choice)
                    start = jnp.where(better, low, start)
                state[1] = state[1] | best
                when = jnp.int32(0)
                bit = start
                for shift in (16, 8, 4, 2, 1):
                    large = bit >= 1 << shift
                    when += jnp.where(large, shift, 0)
                    bit = jnp.where(large, bit >> shift, bit)
                step = state[0] + when
                for number, hops in enumerate(ways):

                    @pl.when(choice == number)
                    def _(hops=hops):
                        due = jnp.where(2 * CHUNK * number_of < filled[pair], step + len(hops) + 1, 0)
                        state[3] = jnp.maximum(state[3], due)
                        for late, (place, turn) in enumerate(hops):
                            link = place * 4 + turn
                            busy[link] = busy[link] | (start << late)
                            at = (step + late) * 4 + turn
                            if late == 0:
                                from_slot = number_of
                            else:
                                before = hops[late - 1][1]
                                from_slot = 2 * slots + before
                            if late == len(hops) - 1:
                                to_slot = slots + number_of
                            else:
                                to_slot = 2 * slots + turn
                            send[jnp.where(me == place, at, dump)] = from_slot
                            there = hop(place, turn, depth)
                            recv[jnp.where(me == there, at, dump)] = to_slot

        return 0

    lax.fori_loop(0, top, level, 0)
    used = state[1]
    length = jnp.int32(0)
    for shift in (16, 8, 4, 2, 1):
        large = used >= 1 << shift
        length += jnp.where(large, shift, 0)
        used = jnp.where(large, used >> shift, used)
    info[0] = jnp.maximum(state[0] + length + jnp.where(state[1] > 0, 1, 0), state[3])


def schedule(sector_tiles, place, count, width, slots):
    size = STEPS * 4 + 8
    return pl.pallas_call(
        functools.partial(schedule_kernel, count, width, slots),
        out_shape=(
            jax.ShapeDtypeStruct((size,), jnp.int32),
            jax.ShapeDtypeStruct((size,), jnp.int32),
            jax.ShapeDtypeStruct((8,), jnp.int32),
        ),
        in_specs=[SMEM_SPEC, SMEM_SPEC],
        out_specs=(SMEM_SPEC, SMEM_SPEC, SMEM_SPEC),
        scratch_shapes=[pltpu.SMEM((count * 4,), jnp.int32), pltpu.SMEM((8,), jnp.int32)],
        name="route_schedule",
    )(sector_tiles, place)


def shuffle_kernel(slots, fed, step_ref, send, recv, *refs):
    arrived, store, leaving = refs[:fed], refs[-8], refs[-7:-3]
    held, sems_in, sems_out = refs[-3:]
    step = step_ref[0]

    def part(slot):
        return store.at[pl.ds(jnp.clip(slot, 0, 2 * slots - 1) * CHUNK, CHUNK)]

    loads, saves = [], []
    for turn in range(fed):
        slot = recv[jnp.maximum(step - 1, 0) * 4 + turn]
        present = (step > 0) & (slot >= 0)
        loads.append((present, pltpu.make_async_copy(arrived[turn], held.at[turn], sems_in.at[turn])))
        final = present & (slot < 2 * slots)
        saves.append((final, pltpu.make_async_copy(held.at[turn], part(slot), sems_out.at[turn])))
    for turn in range(4):
        slot = send[step * 4 + turn]
        own = (slot >= 0) & (slot < 2 * slots)
        loads.append((own, pltpu.make_async_copy(part(slot), held.at[4 + turn], sems_in.at[4 + turn])))
        source = jnp.where(slot >= 2 * slots, slot & 3, 4 + turn)
        saves.append((slot >= 0, pltpu.make_async_copy(held.at[source], leaving[turn], sems_out.at[4 + turn])))
    begin(loads)
    finish(loads)
    begin(saves)
    finish(saves)


def shuffle(step, send, recv, arrived, store, after=()):
    chunk = jax.ShapeDtypeStruct((CHUNK, LANE), F32)
    slots = store.shape[0] // (2 * CHUNK)
    out = pl.pallas_call(
        functools.partial(shuffle_kernel, slots, len(arrived)),
        out_shape=(jax.ShapeDtypeStruct(store.shape, F32),) + (chunk,) * 4,
        in_specs=[SMEM_SPEC] * 3 + [ANY_SPEC] * (len(arrived) + 1 + len(after)),
        out_specs=(ANY_SPEC,) * 5,
        scratch_shapes=[
            pltpu.VMEM((8, CHUNK, LANE), F32),
            pltpu.SemaphoreType.DMA((8,)),
            pltpu.SemaphoreType.DMA((8,)),
        ],
        input_output_aliases={3 + len(arrived): 0},
        cost_estimate=pl.CostEstimate(flops=0, bytes_accessed=8 * 1024 * 1024, transcendentals=0),
        name="shuffle_chunks",
    )(jnp.reshape(step, (1,)).astype(jnp.int32), send, recv, *arrived, store, *after)
    return out[0], out[1:]


def prepare_kernel(low, column, spin, tiles, place, x_ref, a3_ref, at3_ref, *raw_ref):
    value = x_ref[0] if spin is None else x_ref[0, :, spin, :]
    for ref in raw_ref:
        ref[0] = value
    row = lax.broadcasted_iota(jnp.int32, value.shape, 0)
    col = lax.broadcasted_iota(jnp.int32, value.shape, 1)
    keep = (row < size_at(tiles, place[0] + low)) & (col < size_at(tiles, place[0] + column))

    def split():
        masked = jnp.where(keep, value, 0.0)
        a3_ref[0] = right3(masked)
        at3_ref[0] = left3(masked.T)

    if low < 0:
        pl.when(pair_info(tiles, place[0] + low)[0] == 2)(split)
    else:
        split()


def prepare(sector_tiles, place, tensor, low, column, spin=None, keep_raw=False):
    rows, cols = tensor.shape[1], tensor.shape[-1]
    shapes = [((1, 3 * rows, cols), BF16), ((1, cols, 3 * rows), BF16)]
    if keep_raw:
        shapes.append(((1, rows, cols), F32))
    block = pl.BlockSpec(tensor.shape, lambda s: (0,) * tensor.ndim)
    return pl.pallas_call(
        functools.partial(prepare_kernel, low, column, spin),
        grid=(1,),
        out_shape=tuple(jax.ShapeDtypeStruct(*shape) for shape in shapes),
        in_specs=[SMEM_SPEC, SMEM_SPEC, block],
        out_specs=tuple(pl.BlockSpec(shape, lambda s: (0, 0, 0)) for shape, _ in shapes),
        compiler_params=params(),
        cost_estimate=pl.CostEstimate(flops=0, bytes_accessed=4 * 2**20, transcendentals=0),
        name="split_site",
    )(sector_tiles, place, tensor)


def mix_kernel(coef_ref, mask_ref, e_ref, f_ref, k2):
    width, rows, cols = e_ref.shape
    few = 8
    full = width * few

    @pl.when(pl.program_id(0) == 0)
    def _():
        mixing = coef_ref[0] * mask_ref[...].astype(F32)
        row = lax.broadcasted_iota(jnp.int32, (full, width), 0)
        col = lax.broadcasted_iota(jnp.int32, (full, width), 1)
        pick = jnp.where(lax.div(row, few) == col, 1.0, 0.0).astype(F32)
        tall = lax.dot_general(pick, mixing, (((1,), (1,)), ((), ())), precision=HIGH)
        wide = lax.dot_general(tall, pick, (((1,), (1,)), ((), ())), precision=HIGH)
        down = lax.broadcasted_iota(jnp.int32, (full, full), 0)
        across = lax.broadcasted_iota(jnp.int32, (full, full), 1)
        top, rest = halves(jnp.where(lax.rem(down, few) == lax.rem(across, few), wide, 0.0))
        k2[:full, :full] = top
        k2[:full, full:] = top
        k2[full:, :full] = rest
        k2[full:, full:] = jnp.zeros_like(rest)

    starts = range(0, rows, few)
    parts = [e_ref[:, at : at + few, :].reshape(full, cols) for at in starts]
    top, rest = halves(jnp.concatenate(parts, axis=1))
    both = dot3(k2[...], jnp.concatenate([top, rest], axis=0))
    result = both[:full] + both[full:]
    for number, at in enumerate(starts):
        f_ref[:, at : at + few, :] = result[:, number * cols : (number + 1) * cols].reshape(width, few, cols)


def mix_all(coef, mask, env, spin):
    width, extent, _ = env.shape
    rows = 64
    block = pl.BlockSpec((width, rows, extent), lambda c: (0, c, 0))
    return pl.pallas_call(
        mix_kernel,
        grid=(extent // rows,),
        out_shape=jax.ShapeDtypeStruct(env.shape, F32),
        in_specs=[
            pl.BlockSpec((1, width, width), lambda c: (spin, 0, 0)),
            pl.BlockSpec((width, width), lambda c: (0, 0)),
            block,
        ],
        out_specs=block,
        scratch_shapes=[pltpu.VMEM((2 * 8 * width, 2 * 8 * width), BF16)],
        compiler_params=params(),
        cost_estimate=pl.CostEstimate(flops=4 * 10**9, bytes_accessed=32 * 2**20, transcendentals=0),
        name="mix_environment",
    )(coef, mask, env)


def sandwich3(planes, a3, at3):
    few, used, _ = planes.shape
    extent = a3.shape[0] // 3
    a_top, a_rest = a3[:used], a3[extent : extent + used]
    at_top, at_rest = at3[:, :used], at3[:, 2 * extent : 2 * extent + used]
    top, rest = halves(planes.reshape(few * used, used))
    inner = dot3(top, a_top) + dot3(top, a_rest) + dot3(rest, a_top)
    found = []
    for i in range(few):
        top, rest = halves(inner[i * used : (i + 1) * used])
        found.append(dot3(at_top, top) + dot3(at_top, rest) + dot3(at_rest, top))
    return found


def strip_copies(plane, size, store, base, number, jcount, sem, inward):
    found = []
    size = pl.multiple_of(size, TROW)
    for j in range(plane.shape[1] // LANE):
        start = base + (number * jcount + j) * size
        flat = store.at[pl.ds(pl.multiple_of(start, TROW), size)]
        corner = plane.at[pl.ds(0, size), pl.ds(j * LANE, LANE)]
        pair = (flat, corner) if inward else (corner, flat)
        found.append((j < jcount, pltpu.make_async_copy(*pair, sem)))
    return found


def begin(copies):
    for wanted, copy in copies:

        @pl.when(wanted)
        def _(copy=copy):
            copy.start()


def finish(copies):
    for wanted, copy in copies:

        @pl.when(wanted)
        def _(copy=copy):
            copy.wait()


def outgoing_kernel(part, tiles, place, f_ref, a3_ref, at3_ref, *refs):
    store, planes, sems = refs[-3:]
    w = pl.program_id(0)
    count = pl.num_programs(0)
    few, extent, _ = f_ref.shape
    half = extent // 2
    mode, size, jcount = pair_info(tiles, place[0])
    slot = lax.rem(w, 2)

    def copies(index, side):
        found = []
        for i in range(few):
            number = (part * count + index) * few + i
            found += strip_copies(planes.at[side, i], size, store, 0, number, jcount, sems.at[side], False)
        return found

    @pl.when((mode > 0) & (w >= 2))
    def _():
        finish(copies(w - 2, slot))

    def absorb(used):
        for i, block in enumerate(sandwich3(f_ref[...], a3_ref[0, :, :used], at3_ref[0, :used, :])):
            planes[slot, i, :used, :used] = block

    pl.when((mode == 1) & (size <= half))(lambda: absorb(half))
    pl.when((mode == 1) & (size > half))(lambda: absorb(extent))

    @pl.when(mode == 2)
    def _():
        planes[slot] = f_ref[...]

    @pl.when(mode > 0)
    def _():
        begin(copies(w, slot))

        @pl.when(w == count - 1)
        def _():
            finish(copies(w - 1, 1 - slot))
            finish(copies(w, slot))


def outgoing(sector_tiles, place, mixed, a3, at3, slots, store, part):
    width, extent, _ = mixed.shape
    few = 2
    grid = width // PARTS // few
    first = store is None
    return pl.pallas_call(
        functools.partial(outgoing_kernel, part),
        grid=(grid,),
        out_shape=jax.ShapeDtypeStruct((2 * slots * CHUNK, LANE), F32),
        in_specs=[
            SMEM_SPEC,
            SMEM_SPEC,
            pl.BlockSpec((few, extent, extent), lambda w: (part * grid + w, 0, 0)),
            pl.BlockSpec((1,) + a3.shape[1:], lambda w: (0, 0, 0)),
            pl.BlockSpec((1,) + at3.shape[1:], lambda w: (0, 0, 0)),
        ]
        + ([] if first else [ANY_SPEC]),
        out_specs=ANY_SPEC,
        scratch_shapes=[pltpu.VMEM((2, few, extent, extent), F32), pltpu.SemaphoreType.DMA((2,))],
        input_output_aliases={} if first else {5: 0},
        compiler_params=params(),
        cost_estimate=pl.CostEstimate(
            flops=few * grid * 12 * extent**3, bytes_accessed=few * grid * 8 * extent**2, transcendentals=0
        ),
        name="outgoing_terms",
    )(sector_tiles, place, mixed, a3, at3, *([] if first else [store]))


def staying_kernel(f_ref, a3_ref, at3_ref, out_ref):
    for i, block in enumerate(sandwich3(f_ref[...], a3_ref[0], at3_ref[0])):
        out_ref[i] = block


def staying(mixed, a3, at3, part, parts):
    width, extent, _ = mixed.shape
    few = 2
    grid = width // parts // few
    return pl.pallas_call(
        staying_kernel,
        grid=(grid,),
        out_shape=jax.ShapeDtypeStruct((few * grid, extent, extent), F32),
        in_specs=[
            pl.BlockSpec((few, extent, extent), lambda w: (part * grid + w, 0, 0)),
            pl.BlockSpec((1,) + a3.shape[1:], lambda w: (0, 0, 0)),
            pl.BlockSpec((1,) + at3.shape[1:], lambda w: (0, 0, 0)),
        ],
        out_specs=pl.BlockSpec((few, extent, extent), lambda w: (w, 0, 0)),
        compiler_params=params(),
        cost_estimate=pl.CostEstimate(
            flops=grid * few * 12 * extent**3, bytes_accessed=grid * few * 8 * extent**2, transcendentals=0
        ),
        name="staying_terms",
    )(mixed, a3, at3)


def arriving_kernel(part, base, tiles, place, stay_ref, a3_ref, at3_ref, store, *refs):
    out_ref, whole_ref, planes, sems = refs[-4:]
    w = pl.program_id(0)
    count = pl.num_programs(0)
    few, extent, _ = stay_ref.shape
    mode, size, jcount = pair_info(tiles, place[0] - 1)
    slot = lax.rem(w, 2)

    def copies(index, side):
        found = []
        for i in range(few):
            number = (part * count + index) * few + i
            found += strip_copies(planes.at[side, i], size, store, base, number, jcount, sems.at[side], True)
        return found

    @pl.when(w == 0)
    def _():
        planes[...] = jnp.zeros_like(planes)

        @pl.when(mode > 0)
        def _():
            begin(copies(w, slot))

    @pl.when((mode > 0) & (w + 1 < count))
    def _():
        begin(copies(w + 1, 1 - slot))

    @pl.when(mode > 0)
    def _():
        finish(copies(w, slot))

    @pl.when(mode == 0)
    def _():
        out_ref[...] = stay_ref[...]
        whole_ref[...] = stay_ref[...]

    @pl.when(mode == 1)
    def _():
        fresh = stay_ref[...] + planes[slot]
        out_ref[...] = fresh
        whole_ref[...] = fresh

    def absorb(used):
        for i, block in enumerate(sandwich3(planes[slot, :, :used, :used], a3_ref[0], at3_ref[0])):
            fresh = stay_ref[i] + block
            out_ref[i] = fresh
            whole_ref[i] = fresh

    pl.when((mode == 2) & (size <= extent // 2))(lambda: absorb(extent // 2))
    pl.when((mode == 2) & (size > extent // 2))(lambda: absorb(extent))


def arriving(sector_tiles, place, stay, a3, at3, store, whole, part, width):
    planes, extent, _ = stay.shape
    first = whole is None
    few = 2
    grid = planes // few
    block = pl.BlockSpec((few, extent, extent), lambda w: (w, 0, 0))
    return pl.pallas_call(
        functools.partial(arriving_kernel, part, store.shape[0] // 2),
        grid=(grid,),
        out_shape=(
            jax.ShapeDtypeStruct((planes, extent, extent), F32),
            jax.ShapeDtypeStruct((width, extent, extent), F32),
        ),
        in_specs=[
            SMEM_SPEC,
            SMEM_SPEC,
            block,
            pl.BlockSpec((1,) + a3.shape[1:], lambda w: (0, 0, 0)),
            pl.BlockSpec((1,) + at3.shape[1:], lambda w: (0, 0, 0)),
            ANY_SPEC,
        ]
        + ([] if first else [ANY_SPEC]),
        out_specs=(block, pl.BlockSpec((few, extent, extent), lambda w: (part * grid + w, 0, 0))),
        scratch_shapes=[pltpu.VMEM((2, few, extent, extent), F32), pltpu.SemaphoreType.DMA((2,))],
        input_output_aliases={} if first else {6: 1},
        compiler_params=params(),
        cost_estimate=pl.CostEstimate(
            flops=planes * 6 * extent**3, bytes_accessed=planes * 16 * extent**2, transcendentals=0
        ),
        name="arriving_terms",
    )(sector_tiles, place, stay, a3, at3, store, *([] if first else [whole]))


def center_kernel(part, first, place, coef, psi_ref, own_ref, other_ref, *refs):
    out_ref, p3 = refs[-2:]
    w = pl.program_id(0)
    few, extent, _ = own_ref.shape

    @pl.when(w == 0)
    def _():
        p3[...] = right3(psi_ref[...])
        if first:
            out_ref[...] = jnp.zeros_like(out_ref)
        else:
            out_ref[...] = refs[0][...]

    def add(left_ref, right_ref):
        inner = dot3(left3(left_ref[...].reshape(few * extent, extent)), p3[...])
        lefts, rights = [], []
        for i in range(few):
            weight = coef[(part * pl.num_programs(0) + w) * few + i]
            lefts.append(left3(inner[i * extent : (i + 1) * extent] * weight))
            rights.append(right3(right_ref[i]))
        out_ref[...] += dot3(jnp.concatenate(lefts, axis=1), jnp.concatenate(rights, axis=0))

    pl.when(place[1] == 0)(lambda: add(own_ref, other_ref))
    pl.when(place[1] != 0)(lambda: add(other_ref, own_ref))


def center(place, coef, psi, own, other, before, part):
    planes, extent, _ = own.shape
    first = before is None
    few = 2
    whole = pl.BlockSpec((extent, extent), lambda w: (0, 0))
    block = pl.BlockSpec((few, extent, extent), lambda w: (w, 0, 0))
    return pl.pallas_call(
        functools.partial(center_kernel, part, first),
        grid=(planes // few,),
        out_shape=jax.ShapeDtypeStruct((extent, extent), F32),
        in_specs=[SMEM_SPEC, SMEM_SPEC, whole, block, block] + ([] if first else [whole]),
        out_specs=whole,
        scratch_shapes=[pltpu.VMEM((3 * extent, extent), BF16)],
        compiler_params=params(8 * 1024 * 1024),
        cost_estimate=pl.CostEstimate(
            flops=planes * 12 * extent**3, bytes_accessed=planes * 8 * extent**2, transcendentals=0
        ),
        name="center_terms",
    )(place, coef, psi, own, other, *([] if first else [before]))


def routed(env, site, sector_tiles, mpo_mask, mpo_coef, psi, center_coef):
    count = sector_tiles.shape[0]
    sector = lax.axis_index("block")
    section = lax.axis_index("section")
    blocks = env[0]
    width, extent, _ = blocks.shape
    slots = width * extent * extent // (CHUNK * LANE)
    place = jnp.stack([sector, section]).astype(jnp.int32)
    send, recv, steps = schedule(sector_tiles, place, count, width, slots)
    a3, at3, rise = prepare(sector_tiles, place, site, 0, 1, 1, True)
    earlier = lax.ppermute(rise, "block", [(q, q + 1) for q in range(count - 1)])
    rising = mix_all(mpo_coef[0], mpo_mask[0], blocks, 1)
    store = outgoing(sector_tiles, place, rising, a3, at3, slots, None, 0)

    links = [neighbours(turn, count) for turn in range(4)]

    def exchange(leaving):
        return [lax.ppermute(leaving[turn], "block", links[turn]) for turn in range(4)]

    store, leaving = shuffle(jnp.int32(0), send, recv, [], store, (earlier,))
    b3, bt3 = prepare(sector_tiles, place, earlier, -1, 0)
    c3, ct3 = prepare(sector_tiles, place, site, 0, 0, 0)
    stays = []
    fixed = 2 + PARTS
    for step in range(fixed):
        arrived = exchange(leaving)
        beside = ()
        if step == 0:
            store = outgoing(sector_tiles, place, rising, a3, at3, slots, store, 1)
        elif step == 1:
            mixed = mix_all(mpo_coef[0], mpo_mask[0], blocks, 0)
            beside = (mixed,)
        else:
            stays.append(staying(mixed, c3, ct3, step - 2, PARTS))
            beside = (stays[-1],)
        store, leaving = shuffle(jnp.int32(step + 1), send, recv, arrived, store, beside)

    def more(carry):
        return carry[0] < steps[0] - 1

    def onward(carry):
        step, store, leaving = carry
        arrived = exchange(leaving)
        store, leaving = shuffle(step + 1, send, recv, arrived, store)
        return step + 1, store, leaving

    step, store, leaving = lax.while_loop(more, onward, (jnp.int32(fixed), store, leaving))

    def swap(fresh):
        return lax.ppermute(fresh, "section", [(0, 1), (1, 0)])

    arrived = exchange(leaving)
    fresh, whole = arriving(sector_tiles, place, stays[0], b3, bt3, store, None, 0, width)
    partner = swap(fresh)
    store, _ = shuffle(step + 1, send, recv, arrived, store, (fresh,))
    fresh_end, whole = arriving(sector_tiles, place, stays[1], b3, bt3, store, whole, 1, width)
    partner_end = swap(fresh_end)
    total = center(place, center_coef[0], psi[0], fresh, partner, None, 0)
    total = center(place, center_coef[0], psi[0], fresh_end, partner_end, total, 1)
    return whole[None], total[None]


def swapped(block, axis, distance):
    count = lax.axis_size(axis)
    route = []
    for low in range(count):
        high = low | 1 << distance
        if high != low and high < count:
            route += [(low, high), (high, low)]
    return lax.ppermute(block, axis, route)


def from_behind(value, axis, steps):
    count = lax.axis_size(axis)
    first, last = (max(0, -steps), min(count, count - steps))
    return lax.ppermute(value, axis, [(source, source + steps) for source in range(first, last)])


def ordered(is_upper, mine, theirs, axis_dim):
    return jnp.where(
        is_upper,
        jnp.concatenate([theirs, mine], axis=axis_dim),
        jnp.concatenate([mine, theirs], axis=axis_dim),
    )


def sandwich(masked, blocks):
    inner = jnp.einsum("wij,jk->wik", blocks, masked, precision=HIGH)
    return jnp.einsum("ji,wjk->wik", masked, inner, precision=HIGH)


def local(env, site, sector_tiles, mpo_mask, mpo_coef, psi, center_coef):
    nsector = sector_tiles.shape[0]
    group = lax.axis_size("block") // nsector
    levels = group.bit_length() - 1
    device = lax.axis_index("block")
    sector = device // group
    member = device % group
    section = lax.axis_index("section")
    width_local = env.shape[1]
    extent = env.shape[2]
    labels = jnp.arange(nsector, dtype=jnp.int32)
    counts = sector_tiles * TROW
    size_here = jnp.sum(jnp.where(labels == sector, counts, 0))
    size_next = jnp.sum(jnp.where(labels == sector + 1, counts, 0))
    span = jnp.arange(extent, dtype=jnp.int32)
    rows_now = site[0]
    wave_now = psi[0]
    for segment in range(levels):
        other_rows, other_wave = swapped((rows_now, wave_now), "block", segment)
        is_upper = member // 2**segment % 2 == 1
        rows_now = ordered(is_upper, rows_now, other_rows, 0)
        wave_now = ordered(is_upper, wave_now, other_wave, 0)
    row_keep = (span < size_here).astype(jnp.float32)
    masks = []
    for spin in range(2):
        limit = size_here if spin == 0 else size_next
        col_keep = (span < limit).astype(jnp.float32)
        masks.append(rows_now[:, spin, :] * row_keep[:, None] * col_keep[None, :])
    blocks = env[0]
    mixing = mpo_coef[0] * mpo_mask[0].astype(jnp.float32)
    collected = jnp.stack([sandwich(masks[0], blocks), sandwich(masks[1], blocks)])
    for segment in range(levels):
        other_terms = swapped(collected, "block", segment)
        is_upper = member // 2**segment % 2 == 1
        collected = ordered(is_upper, collected, other_terms, 1)
    own_cols = lax.dynamic_slice_in_dim(mixing, member * width_local, width_local, 2)
    reduced = jnp.einsum("xwv,xwij->xvij", own_cols, collected, precision=HIGH)
    arrived = from_behind(reduced[1], "block", group)
    fresh = reduced[0] + arrived
    partner = swapped(fresh, "section", 0)
    left_env = jnp.where(section == 0, fresh, partner)
    right_env = jnp.where(section == 0, partner, fresh)
    first = jnp.einsum("wij,jk->wik", left_env, wave_now, precision=HIGH)
    second = jnp.einsum("wij,wjk->wik", first, right_env, precision=HIGH)
    weights = lax.dynamic_slice_in_dim(center_coef[0], member * width_local, width_local, 0)
    summed = jnp.einsum("w,wik->ik", weights, second, precision=HIGH)
    for segment in reversed(range(levels)):
        half_rows = summed.shape[0] // 2
        lower_part = summed[:half_rows]
        upper_part = summed[half_rows:]
        is_upper = member // 2**segment % 2 == 1
        keeping = jnp.where(is_upper, upper_part, lower_part)
        sending = jnp.where(is_upper, lower_part, upper_part)
        summed = keeping + swapped(sending, "block", segment)
    return (fresh[None], summed[None])


def solution(mesh):
    placed = (
        P("section", "block", None, None),
        P("section", "block", None, None),
        P(),
        P("section", None, None),
        P("section", None, None, None),
        P("section", "block", None),
        P("section", None),
    )
    one_each = mesh.shape["block"] == 16
    return jax.shard_map(
        routed if one_each else local,
        mesh=mesh,
        in_specs=placed,
        out_specs=(P("section", "block", None, None), P("section", "block", None)),
        check_vma=False,
    )
```

```python
import functools

import jax
import jax.numpy as jnp
from jax import lax
from jax.experimental import pallas as pl
from jax.experimental.pallas import tpu as pltpu
from jax.sharding import PartitionSpec as P

TROW = 32
LANE = 128
CHUNK = 2048
STEPS = 128
DETOUR_END = 24
PARTS = 2
BYTES = 52 * 1024 * 1024

F32 = jnp.float32
BF16 = jnp.bfloat16
HIGH = lax.Precision.HIGHEST
SMEM_SPEC = pl.BlockSpec(memory_space=pltpu.SMEM)
ANY_SPEC = pl.BlockSpec(memory_space=pl.ANY)


def size_at(tiles, which):
    count = tiles.shape[0]
    inside = (which >= 0) & (which < count)
    return jnp.where(inside, tiles[jnp.clip(which, 0, count - 1)] * TROW, 0)


def pair_info(tiles, low):
    count = tiles.shape[0]
    here, following = size_at(tiles, low), size_at(tiles, low + 1)
    small = jnp.minimum(here, following)
    present = (low >= 0) & (low + 1 < count)
    mode = jnp.where(present, jnp.where(here < following, 2, 1), 0)
    return mode, small, (small + (LANE - 1)) >> 7


def params(extra=0):
    return pltpu.CompilerParams(vmem_limit_bytes=BYTES + extra)


def halves(value):
    top = value.astype(BF16)
    rest = (value - top.astype(F32)).astype(BF16)
    return top, rest


def left3(value):
    top, rest = halves(value)
    return jnp.concatenate([top, top, rest], axis=1)


def right3(value):
    top, rest = halves(value)
    return jnp.concatenate([top, rest, top], axis=0)


def dot3(a, b):
    return jnp.dot(a, b, preferred_element_type=F32)


def hop(place, turn, depth):
    x, y, z = place & 1, place >> 1 & 1, place >> 2
    if turn == 0:
        x ^= 1
    elif turn == 1:
        y ^= 1
    elif turn == 2:
        z ^= 1
    else:
        z += 1 if z & 1 else -1
    return x + 2 * y + 4 * z if 0 <= z < depth else None


ROUTES = {
    0: ((0,), (1, 0, 1), (2, 0, 3), (3, 0, 2)),
    1: ((0, 1), (1, 0), (2, 0, 1, 3), (3, 1, 0, 2), (2, 1, 0, 3), (3, 0, 1, 2)),
    2: ((0,), (1, 0, 1), (2, 0, 3), (3, 0, 2)),
    3: ((0, 1, 2), (1, 2, 0), (2, 0, 1), (2, 1, 0), (0, 2, 1), (1, 0, 2)),
}


def routes_of(pair, depth):
    found = []
    for turns in ROUTES[pair % 4]:
        place, hops = pair, []
        for turn in turns:
            if turn >= 2:
                turn = 2 if (place >> 2 & 1) == turn - 2 else 3
            hops.append((place, turn))
            place = hop(place, turn, depth)
            if place is None:
                break
        if place == pair + 1:
            found.append(hops)
    return found


def neighbours(direction, count):
    depth = count // 4
    pairs = []
    for place in range(count):
        target = hop(place, direction, depth)
        if target is not None:
            pairs.append((place, target))
    return pairs


def schedule_kernel(count, width, slots, tiles, place, send, recv, info, busy, state):
    depth = count // 4
    me = place[0]
    dump = STEPS * 4

    def clear(i, _):
        for j in range(8):
            send[i * 8 + j] = -1
            recv[i * 8 + j] = -1
        return 0

    lax.fori_loop(0, dump // 8 + 1, clear, 0)
    for i in range(count * 4):
        busy[i] = 0
    for i in range(4):
        state[i] = 0
    need, filled = [], []
    for pair in range(count - 1):
        small = jnp.minimum(tiles[pair], tiles[pair + 1])
        strips = (small + 3) >> 2
        filled.append(width * strips * small * TROW)
        need.append((filled[-1] + (CHUNK - 1)) // CHUNK)
    top = need[0]
    for value in need[1:]:
        top = jnp.maximum(top, value)

    def level(i, _):
        k = top - i

        @pl.when(state[1] >= 1 << (DETOUR_END + 1))
        def _():
            used = state[1]
            length = jnp.int32(0)
            for shift in (16, 8, 4, 2, 1):
                large = used >= 1 << shift
                length += jnp.where(large, shift, 0)
                used = jnp.where(large, used >> shift, used)
            state[0] = state[0] + length + 1
            state[1] = 0
            state[2] = state[2] + 1
            for j in range(count * 4):
                busy[j] = 0

        for pair in range(count - 1):

            @pl.when(need[pair] >= k)
            def _(pair=pair):
                ways = routes_of(pair, depth)
                number_of = need[pair] - k
                rows = PARTS * CHUNK * (number_of + 1)
                half_of = jnp.minimum(lax.div(rows + filled[pair] - 1, filled[pair]), PARTS) - 1
                early = (1 << half_of) - 1
                best = jnp.int32(0x7FFFFFFF)
                choice = jnp.int32(0)
                start = jnp.int32(0)
                detour_ok = state[2] < 2
                for number, hops in enumerate(ways):
                    taken = jnp.int32(0)
                    for late, (place, turn) in enumerate(hops):
                        taken = taken | (busy[place * 4 + turn] >> late)
                    last = 31 if number == 0 else DETOUR_END + 1
                    free = ~(taken | early) & ((1 << (last - len(hops) + 1)) - 1)
                    low = free & -free
                    key = low << (len(hops) - 1)
                    better = (low > 0) & (key < best)
                    if number > 0:
                        better = better & detour_ok
                    best = jnp.where(better, key, best)
                    choice = jnp.where(better, number, choice)
                    start = jnp.where(better, low, start)
                state[1] = state[1] | best
                when = jnp.int32(0)
                bit = start
                for shift in (16, 8, 4, 2, 1):
                    large = bit >= 1 << shift
                    when += jnp.where(large, shift, 0)
                    bit = jnp.where(large, bit >> shift, bit)
                step = state[0] + when
                for number, hops in enumerate(ways):

                    @pl.when(choice == number)
                    def _(hops=hops):
                        due = jnp.where(2 * CHUNK * number_of < filled[pair], step + len(hops) + 1, 0)
                        state[3] = jnp.maximum(state[3], due)
                        for late, (place, turn) in enumerate(hops):
                            link = place * 4 + turn
                            busy[link] = busy[link] | (start << late)
                            at = (step + late) * 4 + turn
                            if late == 0:
                                from_slot = number_of
                            else:
                                before = hops[late - 1][1]
                                from_slot = 2 * slots + before
                            if late == len(hops) - 1:
                                to_slot = slots + number_of
                            else:
                                to_slot = 2 * slots + turn
                            send[jnp.where(me == place, at, dump)] = from_slot
                            there = hop(place, turn, depth)
                            recv[jnp.where(me == there, at, dump)] = to_slot

        return 0

    lax.fori_loop(0, top, level, 0)
    used = state[1]
    length = jnp.int32(0)
    for shift in (16, 8, 4, 2, 1):
        large = used >= 1 << shift
        length += jnp.where(large, shift, 0)
        used = jnp.where(large, used >> shift, used)
    info[0] = jnp.maximum(state[0] + length + jnp.where(state[1] > 0, 1, 0), state[3])


def schedule(sector_tiles, place, count, width, slots):
    size = STEPS * 4 + 8
    return pl.pallas_call(
        functools.partial(schedule_kernel, count, width, slots),
        out_shape=(
            jax.ShapeDtypeStruct((size,), jnp.int32),
            jax.ShapeDtypeStruct((size,), jnp.int32),
            jax.ShapeDtypeStruct((8,), jnp.int32),
        ),
        in_specs=[SMEM_SPEC, SMEM_SPEC],
        out_specs=(SMEM_SPEC, SMEM_SPEC, SMEM_SPEC),
        scratch_shapes=[pltpu.SMEM((count * 4,), jnp.int32), pltpu.SMEM((8,), jnp.int32)],
        name="route_schedule",
    )(sector_tiles, place)


def shuffle_kernel(slots, fed, step_ref, send, recv, *refs):
    arrived, store, leaving = refs[:fed], refs[-8], refs[-7:-3]
    held, sems_in, sems_out = refs[-3:]
    step = step_ref[0]

    def part(slot):
        return store.at[pl.ds(jnp.clip(slot, 0, 2 * slots - 1) * CHUNK, CHUNK)]

    loads, saves = [], []
    for turn in range(fed):
        slot = recv[jnp.maximum(step - 1, 0) * 4 + turn]
        present = (step > 0) & (slot >= 0)
        loads.append((present, pltpu.make_async_copy(arrived[turn], held.at[turn], sems_in.at[turn])))
        final = present & (slot < 2 * slots)
        saves.append((final, pltpu.make_async_copy(held.at[turn], part(slot), sems_out.at[turn])))
    for turn in range(4):
        slot = send[step * 4 + turn]
        own = (slot >= 0) & (slot < 2 * slots)
        loads.append((own, pltpu.make_async_copy(part(slot), held.at[4 + turn], sems_in.at[4 + turn])))
        source = jnp.where(slot >= 2 * slots, slot & 3, 4 + turn)
        saves.append((slot >= 0, pltpu.make_async_copy(held.at[source], leaving[turn], sems_out.at[4 + turn])))
    begin(loads)
    finish(loads)
    begin(saves)
    finish(saves)


def shuffle(step, send, recv, arrived, store, after=()):
    chunk = jax.ShapeDtypeStruct((CHUNK, LANE), F32)
    slots = store.shape[0] // (2 * CHUNK)
    out = pl.pallas_call(
        functools.partial(shuffle_kernel, slots, len(arrived)),
        out_shape=(jax.ShapeDtypeStruct(store.shape, F32),) + (chunk,) * 4,
        in_specs=[SMEM_SPEC] * 3 + [ANY_SPEC] * (len(arrived) + 1 + len(after)),
        out_specs=(ANY_SPEC,) * 5,
        scratch_shapes=[
            pltpu.VMEM((8, CHUNK, LANE), F32),
            pltpu.SemaphoreType.DMA((8,)),
            pltpu.SemaphoreType.DMA((8,)),
        ],
        input_output_aliases={3 + len(arrived): 0},
        cost_estimate=pl.CostEstimate(flops=0, bytes_accessed=8 * 1024 * 1024, transcendentals=0),
        name="shuffle_chunks",
    )(jnp.reshape(step, (1,)).astype(jnp.int32), send, recv, *arrived, store, *after)
    return out[0], out[1:]


def prepare_kernel(low, column, spin, tiles, place, x_ref, a3_ref, at3_ref, *raw_ref):
    value = x_ref[0] if spin is None else x_ref[0, :, spin, :]
    for ref in raw_ref:
        ref[0] = value
    row = lax.broadcasted_iota(jnp.int32, value.shape, 0)
    col = lax.broadcasted_iota(jnp.int32, value.shape, 1)
    keep = (row < size_at(tiles, place[0] + low)) & (col < size_at(tiles, place[0] + column))

    def split():
        masked = jnp.where(keep, value, 0.0)
        a3_ref[0] = right3(masked)
        at3_ref[0] = left3(masked.T)

    if low < 0:
        pl.when(pair_info(tiles, place[0] + low)[0] == 2)(split)
    else:
        split()


def prepare(sector_tiles, place, tensor, low, column, spin=None, keep_raw=False):
    rows, cols = tensor.shape[1], tensor.shape[-1]
    shapes = [((1, 3 * rows, cols), BF16), ((1, cols, 3 * rows), BF16)]
    if keep_raw:
        shapes.append(((1, rows, cols), F32))
    block = pl.BlockSpec(tensor.shape, lambda s: (0,) * tensor.ndim)
    return pl.pallas_call(
        functools.partial(prepare_kernel, low, column, spin),
        grid=(1,),
        out_shape=tuple(jax.ShapeDtypeStruct(*shape) for shape in shapes),
        in_specs=[SMEM_SPEC, SMEM_SPEC, block],
        out_specs=tuple(pl.BlockSpec(shape, lambda s: (0, 0, 0)) for shape, _ in shapes),
        compiler_params=params(),
        cost_estimate=pl.CostEstimate(flops=0, bytes_accessed=4 * 2**20, transcendentals=0),
        name="split_site",
    )(sector_tiles, place, tensor)


def mix_kernel(coef_ref, mask_ref, *refs):
    e_refs, f_ref, k2 = refs[:-2], refs[-2], refs[-1]
    width, rows, cols = f_ref.shape
    few = 8
    full = width * few

    @pl.when(pl.program_id(0) == 0)
    def _():
        mixing = coef_ref[0] * mask_ref[...].astype(F32)
        row = lax.broadcasted_iota(jnp.int32, (full, width), 0)
        col = lax.broadcasted_iota(jnp.int32, (full, width), 1)
        pick = jnp.where(lax.div(row, few) == col, 1.0, 0.0).astype(F32)
        tall = lax.dot_general(pick, mixing, (((1,), (1,)), ((), ())), precision=HIGH)
        wide = lax.dot_general(tall, pick, (((1,), (1,)), ((), ())), precision=HIGH)
        down = lax.broadcasted_iota(jnp.int32, (full, full), 0)
        across = lax.broadcasted_iota(jnp.int32, (full, full), 1)
        top, rest = halves(jnp.where(lax.rem(down, few) == lax.rem(across, few), wide, 0.0))
        k2[:full, :full] = top
        k2[:full, full:] = top
        k2[full:, :full] = rest
        k2[full:, full:] = jnp.zeros_like(rest)

    starts = range(0, rows, few)
    parts = []
    for at in starts:
        planes = [e_ref[:, at : at + few, :] for e_ref in e_refs]
        parts.append(jnp.concatenate(planes, axis=0).reshape(full, cols))
    top, rest = halves(jnp.concatenate(parts, axis=1))
    both = dot3(k2[...], jnp.concatenate([top, rest], axis=0))
    result = both[:full] + both[full:]
    for number, at in enumerate(starts):
        f_ref[:, at : at + few, :] = result[:, number * cols : (number + 1) * cols].reshape(width, few, cols)


def mix_all(coef, mask, env, spin):
    width, extent, _ = env.shape
    rows = 64
    groups = 4

    def some(group):
        return pl.BlockSpec((width // groups, rows, extent), lambda c: (group, c, 0))

    return pl.pallas_call(
        mix_kernel,
        grid=(extent // rows,),
        out_shape=jax.ShapeDtypeStruct(env.shape, F32),
        in_specs=[
            pl.BlockSpec((1, width, width), lambda c: (spin, 0, 0)),
            pl.BlockSpec((width, width), lambda c: (0, 0)),
        ]
        + [some(group) for group in range(groups)],
        out_specs=pl.BlockSpec((width, rows, extent), lambda c: (0, c, 0)),
        scratch_shapes=[pltpu.VMEM((2 * 8 * width, 2 * 8 * width), BF16)],
        compiler_params=params(),
        cost_estimate=pl.CostEstimate(flops=4 * 10**9, bytes_accessed=32 * 2**20, transcendentals=0),
        name="mix_environment",
    )(coef, mask, *[env] * groups)


def sandwich3(planes, a3, at3):
    few, used, _ = planes.shape
    extent = a3.shape[0] // 3
    a_top, a_rest = a3[:used], a3[extent : extent + used]
    at_top, at_rest = at3[:, :used], at3[:, 2 * extent : 2 * extent + used]
    top, rest = halves(planes.reshape(few * used, used))
    inner = dot3(top, a_top) + dot3(top, a_rest) + dot3(rest, a_top)
    found = []
    for i in range(few):
        top, rest = halves(inner[i * used : (i + 1) * used])
        found.append(dot3(at_top, top) + dot3(at_top, rest) + dot3(at_rest, top))
    return found


def strip_copies(plane, size, store, base, number, jcount, sem, inward):
    found = []
    size = pl.multiple_of(size, TROW)
    for j in range(plane.shape[1] // LANE):
        start = base + (number * jcount + j) * size
        flat = store.at[pl.ds(pl.multiple_of(start, TROW), size)]
        corner = plane.at[pl.ds(0, size), pl.ds(j * LANE, LANE)]
        pair = (flat, corner) if inward else (corner, flat)
        found.append((j < jcount, pltpu.make_async_copy(*pair, sem)))
    return found


def begin(copies):
    for wanted, copy in copies:

        @pl.when(wanted)
        def _(copy=copy):
            copy.start()


def finish(copies):
    for wanted, copy in copies:

        @pl.when(wanted)
        def _(copy=copy):
            copy.wait()


def outgoing_kernel(part, tiles, place, f_ref, a3_ref, at3_ref, *refs):
    store, planes, sems = refs[-3:]
    w = pl.program_id(0)
    count = pl.num_programs(0)
    few, extent, _ = f_ref.shape
    half = extent // 2
    mode, size, jcount = pair_info(tiles, place[0])
    slot = lax.rem(w, 2)

    def copies(index, side):
        found = []
        for i in range(few):
            number = (part * count + index) * few + i
            found += strip_copies(planes.at[side, i], size, store, 0, number, jcount, sems.at[side], False)
        return found

    @pl.when((mode > 0) & (w >= 2))
    def _():
        finish(copies(w - 2, slot))

    def absorb(used):
        for i, block in enumerate(sandwich3(f_ref[...], a3_ref[0, :, :used], at3_ref[0, :used, :])):
            planes[slot, i, :used, :used] = block

    pl.when((mode == 1) & (size <= half))(lambda: absorb(half))
    pl.when((mode == 1) & (size > half))(lambda: absorb(extent))

    @pl.when(mode == 2)
    def _():
        planes[slot] = f_ref[...]

    @pl.when(mode > 0)
    def _():
        begin(copies(w, slot))

        @pl.when(w == count - 1)
        def _():
            finish(copies(w - 1, 1 - slot))
            finish(copies(w, slot))


def outgoing(sector_tiles, place, mixed, a3, at3, slots, store, part):
    width, extent, _ = mixed.shape
    few = 2
    grid = width // PARTS // few
    first = store is None
    return pl.pallas_call(
        functools.partial(outgoing_kernel, part),
        grid=(grid,),
        out_shape=jax.ShapeDtypeStruct((2 * slots * CHUNK, LANE), F32),
        in_specs=[
            SMEM_SPEC,
            SMEM_SPEC,
            pl.BlockSpec((few, extent, extent), lambda w: (part * grid + w, 0, 0)),
            pl.BlockSpec((1,) + a3.shape[1:], lambda w: (0, 0, 0)),
            pl.BlockSpec((1,) + at3.shape[1:], lambda w: (0, 0, 0)),
        ]
        + ([] if first else [ANY_SPEC]),
        out_specs=ANY_SPEC,
        scratch_shapes=[pltpu.VMEM((2, few, extent, extent), F32), pltpu.SemaphoreType.DMA((2,))],
        input_output_aliases={} if first else {5: 0},
        compiler_params=params(),
        cost_estimate=pl.CostEstimate(
            flops=few * grid * 12 * extent**3, bytes_accessed=few * grid * 8 * extent**2, transcendentals=0
        ),
        name="outgoing_terms",
    )(sector_tiles, place, mixed, a3, at3, *([] if first else [store]))


def staying_kernel(f_ref, a3_ref, at3_ref, out_ref):
    for i, block in enumerate(sandwich3(f_ref[...], a3_ref[0], at3_ref[0])):
        out_ref[i] = block


def staying(mixed, a3, at3, part, parts):
    width, extent, _ = mixed.shape
    few = 2
    grid = width // parts // few
    return pl.pallas_call(
        staying_kernel,
        grid=(grid,),
        out_shape=jax.ShapeDtypeStruct((few * grid, extent, extent), F32),
        in_specs=[
            pl.BlockSpec((few, extent, extent), lambda w: (part * grid + w, 0, 0)),
            pl.BlockSpec((1,) + a3.shape[1:], lambda w: (0, 0, 0)),
            pl.BlockSpec((1,) + at3.shape[1:], lambda w: (0, 0, 0)),
        ],
        out_specs=pl.BlockSpec((few, extent, extent), lambda w: (w, 0, 0)),
        compiler_params=params(),
        cost_estimate=pl.CostEstimate(
            flops=grid * few * 12 * extent**3, bytes_accessed=grid * few * 8 * extent**2, transcendentals=0
        ),
        name="staying_terms",
    )(mixed, a3, at3)


def arriving_kernel(part, base, tiles, place, stay_ref, a3_ref, at3_ref, store, *refs):
    out_ref, whole_ref, planes, sems = refs[-4:]
    w = pl.program_id(0)
    count = pl.num_programs(0)
    few, extent, _ = stay_ref.shape
    mode, size, jcount = pair_info(tiles, place[0] - 1)
    slot = lax.rem(w, 2)

    def copies(index, side):
        found = []
        for i in range(few):
            number = (part * count + index) * few + i
            found += strip_copies(planes.at[side, i], size, store, base, number, jcount, sems.at[side], True)
        return found

    @pl.when(w == 0)
    def _():
        planes[...] = jnp.zeros_like(planes)

        @pl.when(mode > 0)
        def _():
            begin(copies(w, slot))

    @pl.when((mode > 0) & (w + 1 < count))
    def _():
        begin(copies(w + 1, 1 - slot))

    @pl.when(mode > 0)
    def _():
        finish(copies(w, slot))

    @pl.when(mode == 0)
    def _():
        out_ref[...] = stay_ref[...]
        whole_ref[...] = stay_ref[...]

    @pl.when(mode == 1)
    def _():
        fresh = stay_ref[...] + planes[slot]
        out_ref[...] = fresh
        whole_ref[...] = fresh

    def absorb(used):
        for i, block in enumerate(sandwich3(planes[slot, :, :used, :used], a3_ref[0], at3_ref[0])):
            fresh = stay_ref[i] + block
            out_ref[i] = fresh
            whole_ref[i] = fresh

    pl.when((mode == 2) & (size <= extent // 2))(lambda: absorb(extent // 2))
    pl.when((mode == 2) & (size > extent // 2))(lambda: absorb(extent))


def arriving(sector_tiles, place, stay, a3, at3, store, whole, part, width):
    planes, extent, _ = stay.shape
    first = whole is None
    few = 2
    grid = planes // few
    block = pl.BlockSpec((few, extent, extent), lambda w: (w, 0, 0))
    return pl.pallas_call(
        functools.partial(arriving_kernel, part, store.shape[0] // 2),
        grid=(grid,),
        out_shape=(
            jax.ShapeDtypeStruct((planes, extent, extent), F32),
            jax.ShapeDtypeStruct((width, extent, extent), F32),
        ),
        in_specs=[
            SMEM_SPEC,
            SMEM_SPEC,
            block,
            pl.BlockSpec((1,) + a3.shape[1:], lambda w: (0, 0, 0)),
            pl.BlockSpec((1,) + at3.shape[1:], lambda w: (0, 0, 0)),
            ANY_SPEC,
        ]
        + ([] if first else [ANY_SPEC]),
        out_specs=(block, pl.BlockSpec((few, extent, extent), lambda w: (part * grid + w, 0, 0))),
        scratch_shapes=[pltpu.VMEM((2, few, extent, extent), F32), pltpu.SemaphoreType.DMA((2,))],
        input_output_aliases={} if first else {6: 1},
        compiler_params=params(),
        cost_estimate=pl.CostEstimate(
            flops=planes * 6 * extent**3, bytes_accessed=planes * 16 * extent**2, transcendentals=0
        ),
        name="arriving_terms",
    )(sector_tiles, place, stay, a3, at3, store, *([] if first else [whole]))


def center_kernel(part, first, place, coef, psi_ref, own_ref, other_ref, *refs):
    out_ref, p3 = refs[-2:]
    w = pl.program_id(0)
    few, extent, _ = own_ref.shape

    @pl.when(w == 0)
    def _():
        p3[...] = right3(psi_ref[...])
        if first:
            out_ref[...] = jnp.zeros_like(out_ref)
        else:
            out_ref[...] = refs[0][...]

    def add(left_ref, right_ref):
        top, rest = halves(left_ref[...].reshape(few * extent, extent))
        p_top, p_rest = p3[:extent], p3[extent : 2 * extent]
        inner = dot3(top, p_top) + dot3(top, p_rest) + dot3(rest, p_top)
        lefts, rights = [], []
        for i in range(few):
            weight = coef[(part * pl.num_programs(0) + w) * few + i]
            lefts.append(left3(inner[i * extent : (i + 1) * extent] * weight))
            rights.append(right3(right_ref[i]))
        out_ref[...] += dot3(jnp.concatenate(lefts, axis=1), jnp.concatenate(rights, axis=0))

    pl.when(place[1] == 0)(lambda: add(own_ref, other_ref))
    pl.when(place[1] != 0)(lambda: add(other_ref, own_ref))


def center(place, coef, psi, own, other, before, part):
    planes, extent, _ = own.shape
    first = before is None
    few = 2
    whole = pl.BlockSpec((extent, extent), lambda w: (0, 0))
    block = pl.BlockSpec((few, extent, extent), lambda w: (w, 0, 0))
    return pl.pallas_call(
        functools.partial(center_kernel, part, first),
        grid=(planes // few,),
        out_shape=jax.ShapeDtypeStruct((extent, extent), F32),
        in_specs=[SMEM_SPEC, SMEM_SPEC, whole, block, block] + ([] if first else [whole]),
        out_specs=whole,
        scratch_shapes=[pltpu.VMEM((3 * extent, extent), BF16)],
        compiler_params=params(8 * 1024 * 1024),
        cost_estimate=pl.CostEstimate(
            flops=planes * 12 * extent**3, bytes_accessed=planes * 8 * extent**2, transcendentals=0
        ),
        name="center_terms",
    )(place, coef, psi, own, other, *([] if first else [before]))


def routed(env, site, sector_tiles, mpo_mask, mpo_coef, psi, center_coef):
    count = sector_tiles.shape[0]
    sector = lax.axis_index("block")
    section = lax.axis_index("section")
    blocks = env[0]
    width, extent, _ = blocks.shape
    slots = width * extent * extent // (CHUNK * LANE)
    place = jnp.stack([sector, section]).astype(jnp.int32)
    send, recv, steps = schedule(sector_tiles, place, count, width, slots)
    a3, at3, rise = prepare(sector_tiles, place, site, 0, 1, 1, True)
    earlier = lax.ppermute(rise, "block", [(q, q + 1) for q in range(count - 1)])
    rising = mix_all(mpo_coef[0], mpo_mask[0], blocks, 1)
    store = outgoing(sector_tiles, place, rising, a3, at3, slots, None, 0)

    links = [neighbours(turn, count) for turn in range(4)]

    def exchange(leaving):
        return [lax.ppermute(leaving[turn], "block", links[turn]) for turn in range(4)]

    store, leaving = shuffle(jnp.int32(0), send, recv, [], store, (earlier,))
    c3, ct3 = prepare(sector_tiles, place, site, 0, 0, 0)
    stays = []
    fixed = 2 + PARTS
    for step in range(fixed):
        arrived = exchange(leaving)
        beside = ()
        if step == 0:
            store = outgoing(sector_tiles, place, rising, a3, at3, slots, store, 1)
        elif step == 1:
            mixed = mix_all(mpo_coef[0], mpo_mask[0], blocks, 0)
            beside = (mixed,)
        else:
            stays.append(staying(mixed, c3, ct3, step - 2, PARTS))
            beside = (stays[-1],)
        store, leaving = shuffle(jnp.int32(step + 1), send, recv, arrived, store, beside)

    def more(carry):
        return carry[0] < steps[0] - 1

    def onward(carry):
        step, store, leaving = carry
        arrived = exchange(leaving)
        store, leaving = shuffle(step + 1, send, recv, arrived, store)
        return step + 1, store, leaving

    step, store, leaving = lax.while_loop(more, onward, (jnp.int32(fixed), store, leaving))

    def swap(fresh):
        return lax.ppermute(fresh, "section", [(0, 1), (1, 0)])

    arrived = exchange(leaving)
    late_place, _ = lax.optimization_barrier((place, step))
    b3, bt3 = prepare(sector_tiles, late_place, earlier, -1, 0)
    fresh, whole = arriving(sector_tiles, place, stays[0], b3, bt3, store, None, 0, width)
    partner = swap(fresh)
    store, _ = shuffle(step + 1, send, recv, arrived, store, (fresh,))
    fresh_end, whole = arriving(sector_tiles, place, stays[1], b3, bt3, store, whole, 1, width)
    partner_end = swap(fresh_end)
    total = center(place, center_coef[0], psi[0], fresh, partner, None, 0)
    total = center(place, center_coef[0], psi[0], fresh_end, partner_end, total, 1)
    return whole[None], total[None]


def swapped(block, axis, distance):
    count = lax.axis_size(axis)
    route = []
    for low in range(count):
        high = low | 1 << distance
        if high != low and high < count:
            route += [(low, high), (high, low)]
    return lax.ppermute(block, axis, route)


def from_behind(value, axis, steps):
    count = lax.axis_size(axis)
    first, last = (max(0, -steps), min(count, count - steps))
    return lax.ppermute(value, axis, [(source, source + steps) for source in range(first, last)])


def ordered(is_upper, mine, theirs, axis_dim):
    return jnp.where(
        is_upper,
        jnp.concatenate([theirs, mine], axis=axis_dim),
        jnp.concatenate([mine, theirs], axis=axis_dim),
    )


def sandwich(masked, blocks):
    inner = jnp.einsum("wij,jk->wik", blocks, masked, precision=HIGH)
    return jnp.einsum("ji,wjk->wik", masked, inner, precision=HIGH)


def local(env, site, sector_tiles, mpo_mask, mpo_coef, psi, center_coef):
    nsector = sector_tiles.shape[0]
    group = lax.axis_size("block") // nsector
    levels = group.bit_length() - 1
    device = lax.axis_index("block")
    sector = device // group
    member = device % group
    section = lax.axis_index("section")
    width_local = env.shape[1]
    extent = env.shape[2]
    labels = jnp.arange(nsector, dtype=jnp.int32)
    counts = sector_tiles * TROW
    size_here = jnp.sum(jnp.where(labels == sector, counts, 0))
    size_next = jnp.sum(jnp.where(labels == sector + 1, counts, 0))
    span = jnp.arange(extent, dtype=jnp.int32)
    rows_now = site[0]
    wave_now = psi[0]
    for segment in range(levels):
        other_rows, other_wave = swapped((rows_now, wave_now), "block", segment)
        is_upper = member // 2**segment % 2 == 1
        rows_now = ordered(is_upper, rows_now, other_rows, 0)
        wave_now = ordered(is_upper, wave_now, other_wave, 0)
    row_keep = (span < size_here).astype(jnp.float32)
    masks = []
    for spin in range(2):
        limit = size_here if spin == 0 else size_next
        col_keep = (span < limit).astype(jnp.float32)
        masks.append(rows_now[:, spin, :] * row_keep[:, None] * col_keep[None, :])
    blocks = env[0]
    mixing = mpo_coef[0] * mpo_mask[0].astype(jnp.float32)
    collected = jnp.stack([sandwich(masks[0], blocks), sandwich(masks[1], blocks)])
    for segment in range(levels):
        other_terms = swapped(collected, "block", segment)
        is_upper = member // 2**segment % 2 == 1
        collected = ordered(is_upper, collected, other_terms, 1)
    own_cols = lax.dynamic_slice_in_dim(mixing, member * width_local, width_local, 2)
    reduced = jnp.einsum("xwv,xwij->xvij", own_cols, collected, precision=HIGH)
    arrived = from_behind(reduced[1], "block", group)
    fresh = reduced[0] + arrived
    partner = swapped(fresh, "section", 0)
    left_env = jnp.where(section == 0, fresh, partner)
    right_env = jnp.where(section == 0, partner, fresh)
    first = jnp.einsum("wij,jk->wik", left_env, wave_now, precision=HIGH)
    second = jnp.einsum("wij,wjk->wik", first, right_env, precision=HIGH)
    weights = lax.dynamic_slice_in_dim(center_coef[0], member * width_local, width_local, 0)
    summed = jnp.einsum("w,wik->ik", weights, second, precision=HIGH)
    for segment in reversed(range(levels)):
        half_rows = summed.shape[0] // 2
        lower_part = summed[:half_rows]
        upper_part = summed[half_rows:]
        is_upper = member // 2**segment % 2 == 1
        keeping = jnp.where(is_upper, upper_part, lower_part)
        sending = jnp.where(is_upper, lower_part, upper_part)
        summed = keeping + swapped(sending, "block", segment)
    return (fresh[None], summed[None])


def solution(mesh):
    placed = (
        P("section", "block", None, None),
        P("section", "block", None, None),
        P(),
        P("section", None, None),
        P("section", None, None, None),
        P("section", "block", None),
        P("section", None),
    )
    one_each = mesh.shape["block"] == 16
    return jax.shard_map(
        routed if one_each else local,
        mesh=mesh,
        in_specs=placed,
        out_specs=(P("section", "block", None, None), P("section", "block", None)),
        check_vma=False,
    )
```

```python
import functools

import jax
import jax.numpy as jnp
from jax import lax
from jax.experimental import pallas as pl
from jax.experimental.pallas import tpu as pltpu
from jax.sharding import PartitionSpec as P

TROW = 32
LANE = 128
CHUNK = 2048
STEPS = 128
DETOUR_END = 24
PARTS = 2
BYTES = 49 * 1024 * 1024

F32 = jnp.float32
BF16 = jnp.bfloat16
HIGH = lax.Precision.HIGHEST
SMEM_SPEC = pl.BlockSpec(memory_space=pltpu.SMEM)
ANY_SPEC = pl.BlockSpec(memory_space=pl.ANY)


def size_at(tiles, which):
    count = tiles.shape[0]
    inside = (which >= 0) & (which < count)
    return jnp.where(inside, tiles[jnp.clip(which, 0, count - 1)] * TROW, 0)


def pair_info(tiles, low):
    count = tiles.shape[0]
    here, following = size_at(tiles, low), size_at(tiles, low + 1)
    small = jnp.minimum(here, following)
    present = (low >= 0) & (low + 1 < count)
    mode = jnp.where(present, jnp.where(here < following, 2, 1), 0)
    return mode, small, (small + (LANE - 1)) >> 7


def params(extra=0):
    return pltpu.CompilerParams(vmem_limit_bytes=BYTES + extra)


def halves(value):
    top = value.astype(BF16)
    rest = (value - top.astype(F32)).astype(BF16)
    return top, rest


def left3(value):
    top, rest = halves(value)
    return jnp.concatenate([top, top, rest], axis=1)


def right3(value):
    top, rest = halves(value)
    return jnp.concatenate([top, rest, top], axis=0)


def dot3(a, b):
    return jnp.dot(a, b, preferred_element_type=F32)


def hop(place, turn, depth):
    x, y, z = place & 1, place >> 1 & 1, place >> 2
    if turn == 0:
        x ^= 1
    elif turn == 1:
        y ^= 1
    elif turn == 2:
        z ^= 1
    else:
        z += 1 if z & 1 else -1
    return x + 2 * y + 4 * z if 0 <= z < depth else None


ROUTES = {
    0: ((0,), (1, 0, 1), (2, 0, 3), (3, 0, 2)),
    1: ((0, 1), (1, 0), (2, 0, 1, 3), (3, 1, 0, 2), (2, 1, 0, 3), (3, 0, 1, 2)),
    2: ((0,), (1, 0, 1), (2, 0, 3), (3, 0, 2)),
    3: ((0, 1, 2), (1, 2, 0), (2, 0, 1), (2, 1, 0), (0, 2, 1), (1, 0, 2)),
}


def routes_of(pair, depth):
    found = []
    for turns in ROUTES[pair % 4]:
        place, hops = pair, []
        for turn in turns:
            if turn >= 2:
                turn = 2 if (place >> 2 & 1) == turn - 2 else 3
            hops.append((place, turn))
            place = hop(place, turn, depth)
            if place is None:
                break
        if place == pair + 1:
            found.append(hops)
    return found


def neighbours(direction, count):
    depth = count // 4
    pairs = []
    for place in range(count):
        target = hop(place, direction, depth)
        if target is not None:
            pairs.append((place, target))
    return pairs


def schedule_kernel(count, width, slots, tiles, place, send, recv, info, busy, state):
    depth = count // 4
    me = place[0]
    dump = STEPS * 4

    def clear(i, _):
        for j in range(8):
            send[i * 8 + j] = -1
            recv[i * 8 + j] = -1
        return 0

    lax.fori_loop(0, dump // 8 + 1, clear, 0)
    for i in range(count * 4):
        busy[i] = 0
    for i in range(4):
        state[i] = 0
    need, filled = [], []
    for pair in range(count - 1):
        small = jnp.minimum(tiles[pair], tiles[pair + 1])
        strips = (small + 3) >> 2
        filled.append(width * strips * small * TROW)
        need.append((filled[-1] + (CHUNK - 1)) // CHUNK)
    top = need[0]
    for value in need[1:]:
        top = jnp.maximum(top, value)

    def level(i, _):
        k = top - i

        @pl.when(state[1] >= 1 << (DETOUR_END + 1))
        def _():
            used = state[1]
            length = jnp.int32(0)
            for shift in (16, 8, 4, 2, 1):
                large = used >= 1 << shift
                length += jnp.where(large, shift, 0)
                used = jnp.where(large, used >> shift, used)
            state[0] = state[0] + length + 1
            state[1] = 0
            state[2] = state[2] + 1
            for j in range(count * 4):
                busy[j] = 0

        for pair in range(count - 1):

            @pl.when(need[pair] >= k)
            def _(pair=pair):
                ways = routes_of(pair, depth)
                number_of = need[pair] - k
                rows = PARTS * CHUNK * (number_of + 1)
                half_of = jnp.minimum(lax.div(rows + filled[pair] - 1, filled[pair]), PARTS) - 1
                early = (1 << half_of) - 1
                best = jnp.int32(0x7FFFFFFF)
                choice = jnp.int32(0)
                start = jnp.int32(0)
                detour_ok = state[2] < 2
                for number, hops in enumerate(ways):
                    taken = jnp.int32(0)
                    for late, (place, turn) in enumerate(hops):
                        taken = taken | (busy[place * 4 + turn] >> late)
                    last = 31 if number == 0 else DETOUR_END + 1
                    free = ~(taken | early) & ((1 << (last - len(hops) + 1)) - 1)
                    low = free & -free
                    key = low << (len(hops) - 1)
                    better = (low > 0) & (key < best)
                    if number > 0:
                        better = better & detour_ok
                    best = jnp.where(better, key, best)
                    choice = jnp.where(better, number, choice)
                    start = jnp.where(better, low, start)
                state[1] = state[1] | best
                when = jnp.int32(0)
                bit = start
                for shift in (16, 8, 4, 2, 1):
                    large = bit >= 1 << shift
                    when += jnp.where(large, shift, 0)
                    bit = jnp.where(large, bit >> shift, bit)
                step = state[0] + when
                for number, hops in enumerate(ways):

                    @pl.when(choice == number)
                    def _(hops=hops):
                        due = jnp.where(2 * CHUNK * number_of < filled[pair], step + len(hops) + 1, 0)
                        state[3] = jnp.maximum(state[3], due)
                        for late, (place, turn) in enumerate(hops):
                            link = place * 4 + turn
                            busy[link] = busy[link] | (start << late)
                            at = (step + late) * 4 + turn
                            if late == 0:
                                from_slot = number_of
                            else:
                                before = hops[late - 1][1]
                                from_slot = 2 * slots + before
                            if late == len(hops) - 1:
                                to_slot = slots + number_of
                            else:
                                to_slot = 2 * slots + turn
                            send[jnp.where(me == place, at, dump)] = from_slot
                            there = hop(place, turn, depth)
                            recv[jnp.where(me == there, at, dump)] = to_slot

        return 0

    lax.fori_loop(0, top, level, 0)
    used = state[1]
    length = jnp.int32(0)
    for shift in (16, 8, 4, 2, 1):
        large = used >= 1 << shift
        length += jnp.where(large, shift, 0)
        used = jnp.where(large, used >> shift, used)
    info[0] = jnp.maximum(state[0] + length + jnp.where(state[1] > 0, 1, 0), state[3])


def schedule(sector_tiles, place, count, width, slots):
    size = STEPS * 4 + 8
    return pl.pallas_call(
        functools.partial(schedule_kernel, count, width, slots),
        out_shape=(
            jax.ShapeDtypeStruct((size,), jnp.int32),
            jax.ShapeDtypeStruct((size,), jnp.int32),
            jax.ShapeDtypeStruct((8,), jnp.int32),
        ),
        in_specs=[SMEM_SPEC, SMEM_SPEC],
        out_specs=(SMEM_SPEC, SMEM_SPEC, SMEM_SPEC),
        scratch_shapes=[pltpu.SMEM((count * 4,), jnp.int32), pltpu.SMEM((8,), jnp.int32)],
        name="route_schedule",
    )(sector_tiles, place)


def shuffle_kernel(slots, fed, step_ref, send, recv, *refs):
    arrived, store, leaving = refs[:fed], refs[-8], refs[-7:-3]
    held, sems_in, sems_out = refs[-3:]
    step = step_ref[0]

    def part(slot):
        return store.at[pl.ds(jnp.clip(slot, 0, 2 * slots - 1) * CHUNK, CHUNK)]

    loads, saves = [], []
    for turn in range(fed):
        slot = recv[jnp.maximum(step - 1, 0) * 4 + turn]
        present = (step > 0) & (slot >= 0)
        loads.append((present, pltpu.make_async_copy(arrived[turn], held.at[turn], sems_in.at[turn])))
        final = present & (slot < 2 * slots)
        saves.append((final, pltpu.make_async_copy(held.at[turn], part(slot), sems_out.at[turn])))
    for turn in range(4):
        slot = send[step * 4 + turn]
        own = (slot >= 0) & (slot < 2 * slots)
        loads.append((own, pltpu.make_async_copy(part(slot), held.at[4 + turn], sems_in.at[4 + turn])))
        source = jnp.where(slot >= 2 * slots, slot & 3, 4 + turn)
        saves.append((slot >= 0, pltpu.make_async_copy(held.at[source], leaving[turn], sems_out.at[4 + turn])))
    begin(loads)
    finish(loads)
    begin(saves)
    finish(saves)


def shuffle(step, send, recv, arrived, store, after=()):
    chunk = jax.ShapeDtypeStruct((CHUNK, LANE), F32)
    slots = store.shape[0] // (2 * CHUNK)
    out = pl.pallas_call(
        functools.partial(shuffle_kernel, slots, len(arrived)),
        out_shape=(jax.ShapeDtypeStruct(store.shape, F32),) + (chunk,) * 4,
        in_specs=[SMEM_SPEC] * 3 + [ANY_SPEC] * (len(arrived) + 1 + len(after)),
        out_specs=(ANY_SPEC,) * 5,
        scratch_shapes=[
            pltpu.VMEM((8, CHUNK, LANE), F32),
            pltpu.SemaphoreType.DMA((8,)),
            pltpu.SemaphoreType.DMA((8,)),
        ],
        input_output_aliases={3 + len(arrived): 0},
        cost_estimate=pl.CostEstimate(flops=0, bytes_accessed=8 * 1024 * 1024, transcendentals=0),
        name="shuffle_chunks",
    )(jnp.reshape(step, (1,)).astype(jnp.int32), send, recv, *arrived, store, *after)
    return out[0], out[1:]


def prepare_kernel(low, column, spin, tiles, place, x_ref, a3_ref, at3_ref, *raw_ref):
    value = x_ref[0] if spin is None else x_ref[0, :, spin, :]
    for ref in raw_ref:
        ref[0] = value
    row = lax.broadcasted_iota(jnp.int32, value.shape, 0)
    col = lax.broadcasted_iota(jnp.int32, value.shape, 1)
    keep = (row < size_at(tiles, place[0] + low)) & (col < size_at(tiles, place[0] + column))

    def split():
        masked = jnp.where(keep, value, 0.0)
        a3_ref[0] = right3(masked)
        at3_ref[0] = left3(masked.T)

    if low < 0:
        pl.when(pair_info(tiles, place[0] + low)[0] == 2)(split)
    else:
        split()


def prepare(sector_tiles, place, tensor, low, column, spin=None, keep_raw=False):
    rows, cols = tensor.shape[1], tensor.shape[-1]
    shapes = [((1, 3 * rows, cols), BF16), ((1, cols, 3 * rows), BF16)]
    if keep_raw:
        shapes.append(((1, rows, cols), F32))
    block = pl.BlockSpec(tensor.shape, lambda s: (0,) * tensor.ndim)
    return pl.pallas_call(
        functools.partial(prepare_kernel, low, column, spin),
        grid=(1,),
        out_shape=tuple(jax.ShapeDtypeStruct(*shape) for shape in shapes),
        in_specs=[SMEM_SPEC, SMEM_SPEC, block],
        out_specs=tuple(pl.BlockSpec(shape, lambda s: (0, 0, 0)) for shape, _ in shapes),
        compiler_params=params(),
        cost_estimate=pl.CostEstimate(flops=0, bytes_accessed=4 * 2**20, transcendentals=0),
        name="split_site",
    )(sector_tiles, place, tensor)


def mix_kernel(mixing_ref, *refs):
    e_refs, f_ref, k2 = refs[:-2], refs[-2], refs[-1]
    width, rows, cols = f_ref.shape
    few = 8
    full = width * few

    @pl.when(pl.program_id(0) == 0)
    def _():
        mixing = mixing_ref[0]
        row = lax.broadcasted_iota(jnp.int32, (full, width), 0)
        col = lax.broadcasted_iota(jnp.int32, (full, width), 1)
        pick = jnp.where(lax.div(row, few) == col, 1.0, 0.0).astype(F32)
        tall = lax.dot_general(pick, mixing, (((1,), (1,)), ((), ())), precision=HIGH)
        wide = lax.dot_general(tall, pick, (((1,), (1,)), ((), ())), precision=HIGH)
        down = lax.broadcasted_iota(jnp.int32, (full, full), 0)
        across = lax.broadcasted_iota(jnp.int32, (full, full), 1)
        top, rest = halves(jnp.where(lax.rem(down, few) == lax.rem(across, few), wide, 0.0))
        k2[:full, :full] = top
        k2[:full, full:] = top
        k2[full:, :full] = rest
        k2[full:, full:] = jnp.zeros_like(rest)

    starts = range(0, rows, few)
    parts = []
    for at in starts:
        planes = [e_ref[:, at : at + few, :] for e_ref in e_refs]
        parts.append(jnp.concatenate(planes, axis=0).reshape(full, cols))
    top, rest = halves(jnp.concatenate(parts, axis=1))
    both = dot3(k2[...], jnp.concatenate([top, rest], axis=0))
    result = both[:full] + both[full:]
    for number, at in enumerate(starts):
        f_ref[:, at : at + few, :] = result[:, number * cols : (number + 1) * cols].reshape(width, few, cols)


def mix_all(mixing, env, spin):
    width, extent, _ = env.shape
    rows = 64
    groups = 4

    def some(group):
        return pl.BlockSpec((width // groups, rows, extent), lambda c: (group, c, 0))

    return pl.pallas_call(
        mix_kernel,
        grid=(extent // rows,),
        out_shape=jax.ShapeDtypeStruct(env.shape, F32),
        in_specs=[
            pl.BlockSpec((1, width, width), lambda c: (spin, 0, 0)),
        ]
        + [some(group) for group in range(groups)],
        out_specs=pl.BlockSpec((width, rows, extent), lambda c: (0, c, 0)),
        scratch_shapes=[pltpu.VMEM((2 * 8 * width, 2 * 8 * width), BF16)],
        compiler_params=params(),
        cost_estimate=pl.CostEstimate(flops=4 * 10**9, bytes_accessed=32 * 2**20, transcendentals=0),
        name="mix_environment",
    )(mixing, *[env] * groups)


def sandwich3(planes, a3, at3):
    few, used, _ = planes.shape
    extent = a3.shape[0] // 3
    a_top, a_rest = a3[:used], a3[extent : extent + used]
    at_top, at_rest = at3[:, :used], at3[:, 2 * extent : 2 * extent + used]
    top, rest = halves(planes.reshape(few * used, used))
    inner = dot3(top, a_top) + dot3(top, a_rest) + dot3(rest, a_top)
    found = []
    for i in range(few):
        top, rest = halves(inner[i * used : (i + 1) * used])
        found.append(dot3(at_top, top) + dot3(at_top, rest) + dot3(at_rest, top))
    return found


def strip_copies(plane, size, store, base, number, jcount, sem, inward):
    found = []
    size = pl.multiple_of(size, TROW)
    for j in range(plane.shape[1] // LANE):
        start = base + (number * jcount + j) * size
        flat = store.at[pl.ds(pl.multiple_of(start, TROW), size)]
        corner = plane.at[pl.ds(0, size), pl.ds(j * LANE, LANE)]
        pair = (flat, corner) if inward else (corner, flat)
        found.append((j < jcount, pltpu.make_async_copy(*pair, sem)))
    return found


def begin(copies):
    for wanted, copy in copies:

        @pl.when(wanted)
        def _(copy=copy):
            copy.start()


def finish(copies):
    for wanted, copy in copies:

        @pl.when(wanted)
        def _(copy=copy):
            copy.wait()


def outgoing_kernel(part, tiles, place, f_ref, a3_ref, at3_ref, *refs):
    store, planes, sems = refs[-3:]
    w = pl.program_id(0)
    count = pl.num_programs(0)
    few, extent, _ = f_ref.shape
    half = extent // 2
    mode, size, jcount = pair_info(tiles, place[0])
    slot = lax.rem(w, 2)

    def copies(index, side):
        found = []
        for i in range(few):
            number = (part * count + index) * few + i
            found += strip_copies(planes.at[side, i], size, store, 0, number, jcount, sems.at[side], False)
        return found

    @pl.when((mode > 0) & (w >= 2))
    def _():
        finish(copies(w - 2, slot))

    def absorb(used):
        for i, block in enumerate(sandwich3(f_ref[...], a3_ref[0, :, :used], at3_ref[0, :used, :])):
            planes[slot, i, :used, :used] = block

    pl.when((mode == 1) & (size <= half))(lambda: absorb(half))
    pl.when((mode == 1) & (size > half))(lambda: absorb(extent))

    @pl.when(mode == 2)
    def _():
        planes[slot] = f_ref[...]

    @pl.when(mode > 0)
    def _():
        begin(copies(w, slot))

        @pl.when(w == count - 1)
        def _():
            finish(copies(w - 1, 1 - slot))
            finish(copies(w, slot))


def outgoing(sector_tiles, place, mixed, a3, at3, slots, store, part):
    width, extent, _ = mixed.shape
    few = 2
    grid = width // PARTS // few
    first = store is None
    return pl.pallas_call(
        functools.partial(outgoing_kernel, part),
        grid=(grid,),
        out_shape=jax.ShapeDtypeStruct((2 * slots * CHUNK, LANE), F32),
        in_specs=[
            SMEM_SPEC,
            SMEM_SPEC,
            pl.BlockSpec((few, extent, extent), lambda w: (part * grid + w, 0, 0)),
            pl.BlockSpec((1,) + a3.shape[1:], lambda w: (0, 0, 0)),
            pl.BlockSpec((1,) + at3.shape[1:], lambda w: (0, 0, 0)),
        ]
        + ([] if first else [ANY_SPEC]),
        out_specs=ANY_SPEC,
        scratch_shapes=[pltpu.VMEM((2, few, extent, extent), F32), pltpu.SemaphoreType.DMA((2,))],
        input_output_aliases={} if first else {5: 0},
        compiler_params=params(),
        cost_estimate=pl.CostEstimate(
            flops=few * grid * 12 * extent**3, bytes_accessed=few * grid * 8 * extent**2, transcendentals=0
        ),
        name="outgoing_terms",
    )(sector_tiles, place, mixed, a3, at3, *([] if first else [store]))


def staying_kernel(f_ref, a3_ref, at3_ref, out_ref):
    for i, block in enumerate(sandwich3(f_ref[...], a3_ref[0], at3_ref[0])):
        out_ref[i] = block


def staying(mixed, a3, at3, part, parts):
    width, extent, _ = mixed.shape
    few = 2
    grid = width // parts // few
    return pl.pallas_call(
        staying_kernel,
        grid=(grid,),
        out_shape=jax.ShapeDtypeStruct((few * grid, extent, extent), F32),
        in_specs=[
            pl.BlockSpec((few, extent, extent), lambda w: (part * grid + w, 0, 0)),
            pl.BlockSpec((1,) + a3.shape[1:], lambda w: (0, 0, 0)),
            pl.BlockSpec((1,) + at3.shape[1:], lambda w: (0, 0, 0)),
        ],
        out_specs=pl.BlockSpec((few, extent, extent), lambda w: (w, 0, 0)),
        compiler_params=params(),
        cost_estimate=pl.CostEstimate(
            flops=grid * few * 12 * extent**3, bytes_accessed=grid * few * 8 * extent**2, transcendentals=0
        ),
        name="staying_terms",
    )(mixed, a3, at3)


def arriving_kernel(part, base, tiles, place, stay_ref, a3_ref, at3_ref, store, *refs):
    out_ref, whole_ref, planes, sems = refs[-4:]
    w = pl.program_id(0)
    count = pl.num_programs(0)
    few, extent, _ = stay_ref.shape
    mode, size, jcount = pair_info(tiles, place[0] - 1)
    slot = lax.rem(w, 2)

    def copies(index, side):
        found = []
        for i in range(few):
            number = (part * count + index) * few + i
            found += strip_copies(planes.at[side, i], size, store, base, number, jcount, sems.at[side], True)
        return found

    @pl.when(w == 0)
    def _():
        planes[...] = jnp.zeros_like(planes)

        @pl.when(mode > 0)
        def _():
            begin(copies(w, slot))

    @pl.when((mode > 0) & (w + 1 < count))
    def _():
        begin(copies(w + 1, 1 - slot))

    @pl.when(mode > 0)
    def _():
        finish(copies(w, slot))

    @pl.when(mode == 0)
    def _():
        out_ref[...] = stay_ref[...]
        whole_ref[...] = stay_ref[...]

    @pl.when(mode == 1)
    def _():
        fresh = stay_ref[...] + planes[slot]
        out_ref[...] = fresh
        whole_ref[...] = fresh

    def absorb(used):
        for i, block in enumerate(sandwich3(planes[slot, :, :used, :used], a3_ref[0], at3_ref[0])):
            fresh = stay_ref[i] + block
            out_ref[i] = fresh
            whole_ref[i] = fresh

    pl.when((mode == 2) & (size <= extent // 2))(lambda: absorb(extent // 2))
    pl.when((mode == 2) & (size > extent // 2))(lambda: absorb(extent))


def arriving(sector_tiles, place, stay, a3, at3, store, whole, part, width):
    planes, extent, _ = stay.shape
    first = whole is None
    few = 2
    grid = planes // few
    block = pl.BlockSpec((few, extent, extent), lambda w: (w, 0, 0))
    return pl.pallas_call(
        functools.partial(arriving_kernel, part, store.shape[0] // 2),
        grid=(grid,),
        out_shape=(
            jax.ShapeDtypeStruct((planes, extent, extent), F32),
            jax.ShapeDtypeStruct((width, extent, extent), F32),
        ),
        in_specs=[
            SMEM_SPEC,
            SMEM_SPEC,
            block,
            pl.BlockSpec((1,) + a3.shape[1:], lambda w: (0, 0, 0)),
            pl.BlockSpec((1,) + at3.shape[1:], lambda w: (0, 0, 0)),
            ANY_SPEC,
        ]
        + ([] if first else [ANY_SPEC]),
        out_specs=(block, pl.BlockSpec((few, extent, extent), lambda w: (part * grid + w, 0, 0))),
        scratch_shapes=[pltpu.VMEM((2, few, extent, extent), F32), pltpu.SemaphoreType.DMA((2,))],
        input_output_aliases={} if first else {6: 1},
        compiler_params=params(),
        cost_estimate=pl.CostEstimate(
            flops=planes * 6 * extent**3, bytes_accessed=planes * 16 * extent**2, transcendentals=0
        ),
        name="arriving_terms",
    )(sector_tiles, place, stay, a3, at3, store, *([] if first else [whole]))


def center_kernel(part, first, place, coef, psi_ref, own_ref, other_ref, *refs):
    out_ref, p3 = refs[-2:]
    w = pl.program_id(0)
    few, extent, _ = own_ref.shape

    @pl.when(w == 0)
    def _():
        p3[...] = right3(psi_ref[...])
        if first:
            out_ref[...] = jnp.zeros_like(out_ref)
        else:
            out_ref[...] = refs[0][...]

    def add(left_ref, right_ref):
        top, rest = halves(left_ref[...].reshape(few * extent, extent))
        p_top, p_rest = p3[:extent], p3[extent : 2 * extent]
        inner = dot3(top, p_top) + dot3(top, p_rest) + dot3(rest, p_top)
        lefts, rights = [], []
        for i in range(few):
            weight = coef[(part * pl.num_programs(0) + w) * few + i]
            lefts.append(left3(inner[i * extent : (i + 1) * extent] * weight))
            rights.append(right3(right_ref[i]))
        out_ref[...] += dot3(jnp.concatenate(lefts, axis=1), jnp.concatenate(rights, axis=0))

    pl.when(place[1] == 0)(lambda: add(own_ref, other_ref))
    pl.when(place[1] != 0)(lambda: add(other_ref, own_ref))


def center(place, coef, psi, own, other, before, part):
    planes, extent, _ = own.shape
    first = before is None
    few = 2
    whole = pl.BlockSpec((extent, extent), lambda w: (0, 0))
    block = pl.BlockSpec((few, extent, extent), lambda w: (w, 0, 0))
    return pl.pallas_call(
        functools.partial(center_kernel, part, first),
        grid=(planes // few,),
        out_shape=jax.ShapeDtypeStruct((extent, extent), F32),
        in_specs=[SMEM_SPEC, SMEM_SPEC, whole, block, block] + ([] if first else [whole]),
        out_specs=whole,
        scratch_shapes=[pltpu.VMEM((3 * extent, extent), BF16)],
        compiler_params=params(8 * 1024 * 1024),
        cost_estimate=pl.CostEstimate(
            flops=planes * 12 * extent**3, bytes_accessed=planes * 8 * extent**2, transcendentals=0
        ),
        name="center_terms",
    )(place, coef, psi, own, other, *([] if first else [before]))


def routed(env, site, sector_tiles, mpo_mask, mpo_coef, psi, center_coef):
    count = sector_tiles.shape[0]
    sector = lax.axis_index("block")
    section = lax.axis_index("section")
    blocks = env[0]
    width, extent, _ = blocks.shape
    slots = width * extent * extent // (CHUNK * LANE)
    place = jnp.stack([sector, section]).astype(jnp.int32)
    send, recv, steps = schedule(sector_tiles, place, count, width, slots)
    a3, at3, rise = prepare(sector_tiles, place, site, 0, 1, 1, True)
    earlier = lax.ppermute(rise, "block", [(q, q + 1) for q in range(count - 1)])
    mixing = mpo_coef[0] * mpo_mask[0].astype(F32)
    rising = mix_all(mixing, blocks, 1)
    store = outgoing(sector_tiles, place, rising, a3, at3, slots, None, 0)

    links = [neighbours(turn, count) for turn in range(4)]

    def exchange(leaving):
        return [lax.ppermute(leaving[turn], "block", links[turn]) for turn in range(4)]

    store, leaving = shuffle(jnp.int32(0), send, recv, [], store, (earlier,))
    c3, ct3 = prepare(sector_tiles, place, site, 0, 0, 0)
    stays = []
    fixed = 2 + PARTS
    for step in range(fixed):
        arrived = exchange(leaving)
        beside = ()
        if step == 0:
            store = outgoing(sector_tiles, place, rising, a3, at3, slots, store, 1)
        elif step == 1:
            mixed = mix_all(mixing, blocks, 0)
            beside = (mixed,)
        else:
            stays.append(staying(mixed, c3, ct3, step - 2, PARTS))
            beside = (stays[-1],)
        store, leaving = shuffle(jnp.int32(step + 1), send, recv, arrived, store, beside)

    def more(carry):
        return carry[0] < steps[0] - 1

    def onward(carry):
        step, store, leaving = carry
        arrived = exchange(leaving)
        store, leaving = shuffle(step + 1, send, recv, arrived, store)
        return step + 1, store, leaving

    step, store, leaving = lax.while_loop(more, onward, (jnp.int32(fixed), store, leaving))

    def swap(fresh):
        return lax.ppermute(fresh, "section", [(0, 1), (1, 0)])

    arrived = exchange(leaving)
    late_place, _ = lax.optimization_barrier((place, step))
    b3, bt3 = prepare(sector_tiles, late_place, earlier, -1, 0)
    fresh, whole = arriving(sector_tiles, place, stays[0], b3, bt3, store, None, 0, width)
    partner = swap(fresh)
    store, _ = shuffle(step + 1, send, recv, arrived, store, (fresh,))
    fresh_end, whole = arriving(sector_tiles, place, stays[1], b3, bt3, store, whole, 1, width)
    partner_end = swap(fresh_end)
    total = center(place, center_coef[0], psi[0], fresh, partner, None, 0)
    total = center(place, center_coef[0], psi[0], fresh_end, partner_end, total, 1)
    return whole[None], total[None]


def swapped(block, axis, distance):
    count = lax.axis_size(axis)
    route = []
    for low in range(count):
        high = low | 1 << distance
        if high != low and high < count:
            route += [(low, high), (high, low)]
    return lax.ppermute(block, axis, route)


def from_behind(value, axis, steps):
    count = lax.axis_size(axis)
    first, last = (max(0, -steps), min(count, count - steps))
    return lax.ppermute(value, axis, [(source, source + steps) for source in range(first, last)])


def ordered(is_upper, mine, theirs, axis_dim):
    return jnp.where(
        is_upper,
        jnp.concatenate([theirs, mine], axis=axis_dim),
        jnp.concatenate([mine, theirs], axis=axis_dim),
    )


def sandwich(masked, blocks):
    inner = jnp.einsum("wij,jk->wik", blocks, masked, precision=HIGH)
    return jnp.einsum("ji,wjk->wik", masked, inner, precision=HIGH)


def local(env, site, sector_tiles, mpo_mask, mpo_coef, psi, center_coef):
    nsector = sector_tiles.shape[0]
    group = lax.axis_size("block") // nsector
    levels = group.bit_length() - 1
    device = lax.axis_index("block")
    sector = device // group
    member = device % group
    section = lax.axis_index("section")
    width_local = env.shape[1]
    extent = env.shape[2]
    labels = jnp.arange(nsector, dtype=jnp.int32)
    counts = sector_tiles * TROW
    size_here = jnp.sum(jnp.where(labels == sector, counts, 0))
    size_next = jnp.sum(jnp.where(labels == sector + 1, counts, 0))
    span = jnp.arange(extent, dtype=jnp.int32)
    rows_now = site[0]
    wave_now = psi[0]
    for segment in range(levels):
        other_rows, other_wave = swapped((rows_now, wave_now), "block", segment)
        is_upper = member // 2**segment % 2 == 1
        rows_now = ordered(is_upper, rows_now, other_rows, 0)
        wave_now = ordered(is_upper, wave_now, other_wave, 0)
    row_keep = (span < size_here).astype(jnp.float32)
    masks = []
    for spin in range(2):
        limit = size_here if spin == 0 else size_next
        col_keep = (span < limit).astype(jnp.float32)
        masks.append(rows_now[:, spin, :] * row_keep[:, None] * col_keep[None, :])
    blocks = env[0]
    mixing = mpo_coef[0] * mpo_mask[0].astype(jnp.float32)
    collected = jnp.stack([sandwich(masks[0], blocks), sandwich(masks[1], blocks)])
    for segment in range(levels):
        other_terms = swapped(collected, "block", segment)
        is_upper = member // 2**segment % 2 == 1
        collected = ordered(is_upper, collected, other_terms, 1)
    own_cols = lax.dynamic_slice_in_dim(mixing, member * width_local, width_local, 2)
    reduced = jnp.einsum("xwv,xwij->xvij", own_cols, collected, precision=HIGH)
    arrived = from_behind(reduced[1], "block", group)
    fresh = reduced[0] + arrived
    partner = swapped(fresh, "section", 0)
    left_env = jnp.where(section == 0, fresh, partner)
    right_env = jnp.where(section == 0, partner, fresh)
    first = jnp.einsum("wij,jk->wik", left_env, wave_now, precision=HIGH)
    second = jnp.einsum("wij,wjk->wik", first, right_env, precision=HIGH)
    weights = lax.dynamic_slice_in_dim(center_coef[0], member * width_local, width_local, 0)
    summed = jnp.einsum("w,wik->ik", weights, second, precision=HIGH)
    for segment in reversed(range(levels)):
        half_rows = summed.shape[0] // 2
        lower_part = summed[:half_rows]
        upper_part = summed[half_rows:]
        is_upper = member // 2**segment % 2 == 1
        keeping = jnp.where(is_upper, upper_part, lower_part)
        sending = jnp.where(is_upper, lower_part, upper_part)
        summed = keeping + swapped(sending, "block", segment)
    return (fresh[None], summed[None])


def solution(mesh):
    placed = (
        P("section", "block", None, None),
        P("section", "block", None, None),
        P(),
        P("section", None, None),
        P("section", None, None, None),
        P("section", "block", None),
        P("section", None),
    )
    one_each = mesh.shape["block"] == 16
    return jax.shard_map(
        routed if one_each else local,
        mesh=mesh,
        in_specs=placed,
        out_specs=(P("section", "block", None, None), P("section", "block", None)),
        check_vma=False,
    )
```
